32 devices in a mesh: owner: 16 (over z, y, x), pair: 2 (over core).
Axes of the slice: x: 2, y: 2, z: 4, core: 2. Of those that a mesh axis runs over, the one named last changes fastest.
Arguments:
- incident: float32 [32, 2, 32, 512], P('owner', None, None, 'pair'), may hold values from -6 to 6
- tmat: float32 [32, 2, 512, 512], P('owner', None, 'pair'), may hold values from -0.1875 to 0.1875
- blocks: float32 [336, 2, 512, 512], P('owner', None, None, 'pair'), may hold values from -0.09375 to 0.09375
- block_rows: int32 [336], P('owner'), may hold values from 0 to 1
- partners: int32 [336], replicated, may hold values from 0 to 31, as said below
- live: int32 [16], P('owner'), may hold values from 1 to 21, as said below
- owner_of: int32 [32], replicated, may hold values from 0 to 31, as said below
Outputs:
- scattered: float32 [32, 2, 32, 512], P('owner', None, None, 'pair')
- exciting: float32 [32, 2, 32, 512], P('owner', None, None, 'pair')
The draws below stay inside these ranges and needn't reach their ends.
Inputs may be any that keep to these rules, and one draw needn't show every extreme that they name: A permutation: particle p's coefficients and T-matrix stand in row owner_of[p]. `partners`: the 21 slots of one owner name distinct particles whose rows lie with owners either less than 7 positions away on either side around the cycle of owners or exactly 8 positions away, never the owner itself, at most 2 with any one other owner; for every owner some other owner holds exactly 2 of them. Slots n with n mod 21 below live[n // 21] are live; some owner has all 21 slots live.
All inputs are finite; a program needn't handle non-finite values.
Results may differ from the reference program's by a relative error of at most 0.0003.
Values sent between devices are 32-bit elements; how exact they have to be, the bound alone decides.
No kernel may reach another device: no remote copies, remote signals or barrier semaphores. Data moves between devices by JAX's collectives and lax.ppermute only.
A program may use at most 128 MiB of HBM per device.

```python
import jax
import jax.numpy as jnp
from jax import lax

L = 512
K = 32
PART_DEV = 2
BLK = 21
ITERS = 2
P_SIZE = 32
OWNERS = 16
NBLK = 336
WIN = 7
GROUPS = 13
CAP = 2


def particle_order(key):
    return jax.random.permutation(jax.random.fold_in(key, 11), P_SIZE).astype(jnp.int32)


def draw_owner_of(key, part):
    return particle_order(key)


def draw_partners(key, part):
    ordering = particle_order(key)
    inverse = jnp.zeros((P_SIZE,), jnp.int32).at[ordering].set(jnp.arange(P_SIZE, dtype=jnp.int32))
    choices_count = GROUPS * CAP
    scores = (jax.random.randint(jax.random.fold_in(key, 12), (OWNERS, choices_count), 0, 1 << 20) + 1) * choices_count
    positions = jnp.arange(choices_count, dtype=jnp.int32)[None, :]
    scores = jnp.where(positions < CAP, positions, scores + positions)
    chosen = jnp.argsort(scores, axis=1)[:, :BLK].astype(jnp.int32)
    group_index = chosen // CAP
    signed_gap = jnp.where(group_index == 0, OWNERS // 2, jnp.where(group_index < WIN, group_index, -(group_index - WIN + 1)))
    shifts = jax.random.randint(jax.random.fold_in(key, 13), (OWNERS, GROUPS), 0, PART_DEV)
    local_row = (chosen % CAP + jnp.take_along_axis(shifts, group_index, axis=1)) % PART_DEV
    holders = jnp.arange(OWNERS, dtype=jnp.int32)[:, None]
    row_ids = (holders + signed_gap) % OWNERS * PART_DEV + local_row
    return inverse[row_ids].reshape(OWNERS * BLK).astype(jnp.int32)


def draw_live(key, part):
    counts = jax.random.randint(jax.random.fold_in(key, 14), (OWNERS,), 1, BLK + 1)
    fullest = jax.random.randint(jax.random.fold_in(key, 15), (), 0, OWNERS)
    return counts.at[fullest].set(BLK).astype(jnp.int32)


def place_ends(entries, key, least, high):
    place = [jax.random.randint(jax.random.fold_in(key, axis), (), 0, length) for axis, length in enumerate(entries.shape)]
    main_axis = entries.shape.index(max(entries.shape))
    beside = place[:main_axis] + [(place[main_axis] + 1) % entries.shape[main_axis]] + place[main_axis + 1:]
    return entries.at[tuple(place)].set(least).at[tuple(beside)].set(high)


def block_levels(key, extent, shards, least, high):
    def one(position, blocks):
        steps = jax.random.uniform(jax.random.fold_in(jax.random.fold_in(key, 6), position), (blocks,), jnp.float32, least / len(shards), high / len(shards))
        return jnp.repeat(jnp.exp(steps), extent[position] // blocks).reshape((-1,) + (1,) * (len(extent) - position - 1))

    gain = one(*shards[0])
    for cut in shards[1:]:
        gain = gain * one(*cut)
    return gain


def gaussian(stream_key, extent, width, most, split=(), kind=jnp.bfloat16):
    drawn = jax.random.normal(stream_key, extent, jnp.float32) * width
    if len(split) > 0:
        drawn = block_levels(stream_key, extent, split, -0.22, 0.18) * drawn
    return jnp.clip(drawn, min=-most, max=most).astype(kind)


def setup_inputs(seed: int = 0) -> dict:
    arg_keys = jax.random.split(jax.random.key(seed), 8)
    incident = gaussian(arg_keys[0], (P_SIZE, 2, K, L), 1.0, 6.0, ((0, 16), (3, 2)), jnp.float32)
    tmat = gaussian(arg_keys[1], (P_SIZE, 2, L, L), (2 * L) ** -0.5, 0.1875, ((0, 16), (2, 2)), jnp.float32)
    blocks = gaussian(arg_keys[2], (NBLK, 2, L, L), ((2 * L * BLK) ** -0.5), 0.09375, ((0, 16), (3, 2)), jnp.float32)
    block_rows = place_ends(jax.random.randint(arg_keys[3], (NBLK,), 0, PART_DEV), jax.random.fold_in(arg_keys[3], 1), 0, PART_DEV - 1).astype(jnp.int32)
    partners = draw_partners(jax.random.fold_in(arg_keys[7], 71), 0)
    live = draw_live(jax.random.fold_in(arg_keys[7], 71), 0)
    owner_of = draw_owner_of(jax.random.fold_in(arg_keys[7], 71), 0)
    return dict(incident=incident, tmat=tmat, blocks=blocks, block_rows=block_rows, partners=partners, live=live, owner_of=owner_of)


HIGHEST = lax.Precision.HIGHEST


def complex_rows(matrix, vectors):
    directions = vectors.shape[1]
    stacked = vectors.reshape(2 * directions, vectors.shape[2])
    real_part = jnp.einsum("km,lm->kl", stacked, matrix[0], precision=HIGHEST, preferred_element_type=jnp.float32)
    imag_part = jnp.einsum("km,lm->kl", stacked, matrix[1], precision=HIGHEST, preferred_element_type=jnp.float32)
    return jnp.stack((real_part[:directions] - imag_part[directions:], imag_part[:directions] + real_part[directions:]))


def complex_cols(matrix, vectors):
    directions = vectors.shape[1]
    stacked = vectors.reshape(2 * directions, vectors.shape[2])
    real_part = jnp.einsum("kl,lm->km", stacked, matrix[0], precision=HIGHEST, preferred_element_type=jnp.float32)
    imag_part = jnp.einsum("kl,lm->km", stacked, matrix[1], precision=HIGHEST, preferred_element_type=jnp.float32)
    return jnp.stack((real_part[:directions] - imag_part[directions:], imag_part[:directions] + real_part[directions:]))


def reference(incident, tmat, blocks, block_rows, partners, live, owner_of):
    apply_tmat = jax.vmap(complex_rows)
    scattered = apply_tmat(tmat, incident)
    exciting = incident
    for iteration in range(ITERS):
        def accumulate(totals, block_index, current=scattered):
            holder = block_index // BLK
            holder_row = (holder * PART_DEV + block_rows[block_index]).astype(jnp.int32)
            partner_row = owner_of[partners[block_index]].astype(jnp.int32)
            active = (block_index % BLK) < live[holder]
            one_block = blocks[block_index]
            forward = complex_rows(one_block, current[partner_row])
            backward = complex_cols(one_block, current[holder_row])
            totals = totals.at[holder_row].add(jnp.where(active, forward, jnp.zeros_like(forward)))
            totals = totals.at[partner_row].add(jnp.where(active, backward, jnp.zeros_like(backward)))
            return totals, None
        totals, unused = lax.scan(accumulate, jnp.zeros_like(incident), jnp.arange(NBLK, dtype=jnp.int32))
        exciting = incident + totals
        scattered = apply_tmat(tmat, exciting)
    return scattered, exciting
```

```python
import functools

import jax
import jax.numpy as jnp
from jax import lax
from jax.experimental import pallas as pl
from jax.experimental.pallas import tpu as pltpu
from jax.sharding import PartitionSpec as P

ITERS = 2
F32 = jnp.float32
BF16 = jnp.bfloat16
MIB = 1 << 20


def split_value(value):
    high = value.astype(BF16)
    low = (value - high.astype(F32)).astype(BF16)
    return high, low


def stacked_parts(real, imag):
    real_high, real_low = split_value(real)
    imag_high, imag_low = split_value(imag)
    with_real = jnp.concatenate((real_high, imag_high, real_low, imag_low), axis=0)
    with_imag = jnp.concatenate((-imag_high, real_high, -imag_low, real_low), axis=0)
    return with_real, with_imag


def dot_nt(left, right):
    return lax.dot_general(left, right, (((1,), (1,)), ((), ())), preferred_element_type=F32)


def dot_nn(left, right):
    return jnp.dot(left, right, preferred_element_type=F32)


def tmat_kernel(mine_ref, theirs_ref, tmat_ref, side_ref, exciting_ref, scattered_ref):
    particles, _, directions, width = mine_ref.shape
    half = width // 2
    start = pl.multiple_of(side_ref[0] * half, half)
    for row in range(particles):
        real = mine_ref[row, 0] + theirs_ref[row, 0]
        imag = mine_ref[row, 1] + theirs_ref[row, 1]
        with_real, with_imag = stacked_parts(real, imag)
        real_high, real_low = split_value(tmat_ref[row, 0])
        imag_high, imag_low = split_value(tmat_ref[row, 1])
        total = dot_nt(real_high, with_real) + dot_nt(imag_high, with_imag)
        rest = dot_nt(real_low, with_real[: 2 * directions])
        rest += dot_nt(imag_low, with_imag[: 2 * directions])
        out = total[:, : 2 * directions] + total[:, 2 * directions :] + rest
        out = out.T
        scattered_ref[row, 0] = out[:directions]
        scattered_ref[row, 1] = out[directions:]
        for part in range(2):
            window = (row, part, slice(None), pl.ds(start, half))
            exciting_ref[row, part] = mine_ref[window] + theirs_ref[window]


def apply_tmat(mine, theirs, tmat, side):
    particles, _, directions, width = mine.shape
    half_shape = jax.ShapeDtypeStruct((particles, 2, directions, width // 2), F32)
    vmem = pl.BlockSpec(memory_space=pltpu.VMEM)
    return pl.pallas_call(
        tmat_kernel,
        out_shape=(half_shape, half_shape),
        in_specs=[vmem, vmem, vmem, pl.BlockSpec(memory_space=pltpu.SMEM)],
        out_specs=(vmem, vmem),
        compiler_params=pltpu.CompilerParams(vmem_limit_bytes=24 * MIB),
        name="tmat_apply",
    )(mine, theirs, tmat, side)


def backward_kernel(rows_ref, live_ref, partner_ref, field_ref, block_ref, out_ref, left_ref):
    slot = pl.program_id(0)
    directions = field_ref.shape[2]

    @pl.when(slot == 0)
    def _():
        for row in range(field_ref.shape[0]):
            with_real, with_imag = stacked_parts(field_ref[row, 0], field_ref[row, 1])
            left_ref[row, 0] = with_real
            left_ref[row, 1] = with_imag
        out_ref[...] = jnp.zeros_like(out_ref)

    @pl.when(slot < live_ref[0])
    def _():
        holder = rows_ref[slot]
        real_high, real_low = split_value(block_ref[0, 0])
        imag_high, imag_low = split_value(block_ref[0, 1])
        total = dot_nn(left_ref[holder, 0], real_high) + dot_nn(left_ref[holder, 1], imag_high)
        rest = dot_nn(left_ref[holder, 0, : 2 * directions], real_low)
        rest += dot_nn(left_ref[holder, 1, : 2 * directions], imag_low)
        out = total[: 2 * directions] + total[2 * directions :] + rest
        partner = partner_ref[slot]
        out_ref[partner, 0] = out[:directions]
        out_ref[partner, 1] = out[directions:]


def slot_block(slot, rows_ref, live_ref, partner_ref):
    return (jnp.minimum(slot, live_ref[0] - 1), 0, 0, 0)


def backward(rows, live, partner_row, field_full, blocks, total_rows):
    slots, _, width, half = blocks.shape
    particles, _, directions, _ = field_full.shape
    grid_spec = pltpu.PrefetchScalarGridSpec(
        num_scalar_prefetch=3,
        grid=(slots,),
        in_specs=[
            pl.BlockSpec(field_full.shape, lambda slot, *refs: (0, 0, 0, 0)),
            pl.BlockSpec((1, 2, width, half), slot_block),
        ],
        out_specs=pl.BlockSpec(
            (total_rows, 2, directions, half), lambda slot, *refs: (0, 0, 0, 0)
        ),
        scratch_shapes=[pltpu.VMEM((particles, 2, 4 * directions, width), BF16)],
    )
    return pl.pallas_call(
        backward_kernel,
        grid_spec=grid_spec,
        out_shape=jax.ShapeDtypeStruct((total_rows, 2, directions, half), F32),
        compiler_params=pltpu.CompilerParams(
            vmem_limit_bytes=44 * MIB, dimension_semantics=("arbitrary",)
        ),
        cost_estimate=pl.CostEstimate(
            flops=slots * 16 * directions * width * half,
            bytes_accessed=blocks.size * 4,
            transcendentals=0,
        ),
        name="blocks_backward",
    )(rows, live, partner_row, field_full, blocks)


def forward_kernel(rows_ref, live_ref, partner_ref, field_ref, block_ref, out_ref, acc_ref):
    slot = pl.program_id(0)
    directions = field_ref.shape[2]

    @pl.when(slot == 0)
    def _():
        acc_ref[...] = jnp.zeros_like(acc_ref)

    @pl.when(slot < live_ref[0])
    def _():
        holder = rows_ref[slot]
        with_real, with_imag = stacked_parts(field_ref[0, 0], field_ref[0, 1])
        real_high, real_low = split_value(block_ref[0, 0])
        imag_high, imag_low = split_value(block_ref[0, 1])
        total = dot_nt(real_high, with_real) + dot_nt(imag_high, with_imag)
        total += dot_nt(real_low, with_real) + dot_nt(imag_low, with_imag)
        acc_ref[holder] += total

    @pl.when(slot == pl.num_programs(0) - 1)
    def _():
        for row in range(acc_ref.shape[0]):
            total = acc_ref[row]
            out = (total[:, : 2 * directions] + total[:, 2 * directions :]).T
            out_ref[row, 0] = out[:directions]
            out_ref[row, 1] = out[directions:]


def slot_field(slot, rows_ref, live_ref, partner_ref):
    return (partner_ref[jnp.minimum(slot, live_ref[0] - 1)], 0, 0, 0)


def forward(rows, live, partner_row, every_field, blocks, particles):
    slots, _, width, half = blocks.shape
    directions = every_field.shape[2]
    grid_spec = pltpu.PrefetchScalarGridSpec(
        num_scalar_prefetch=3,
        grid=(slots,),
        in_specs=[
            pl.BlockSpec((1, 2, directions, half), slot_field),
            pl.BlockSpec((1, 2, width, half), slot_block),
        ],
        out_specs=pl.BlockSpec(
            (particles, 2, directions, width), lambda slot, *refs: (0, 0, 0, 0)
        ),
        scratch_shapes=[pltpu.VMEM((particles, width, 4 * directions), F32)],
    )
    return pl.pallas_call(
        forward_kernel,
        grid_spec=grid_spec,
        out_shape=jax.ShapeDtypeStruct((particles, 2, directions, width), F32),
        compiler_params=pltpu.CompilerParams(
            vmem_limit_bytes=24 * MIB, dimension_semantics=("arbitrary",)
        ),
        cost_estimate=pl.CostEstimate(
            flops=slots * 16 * directions * width * half,
            bytes_accessed=blocks.size * 4,
            transcendentals=0,
        ),
        name="blocks_forward",
    )(rows, live, partner_row, every_field, blocks)


def from_other(value):
    return lax.ppermute(value, "pair", [(0, 1), (1, 0)])


def local(incident, tmat, blocks, block_rows, partners, live, owner_of):
    particles, _, directions, half = incident.shape
    slots = blocks.shape[0]
    my_owner = lax.axis_index("owner")
    side = lax.axis_index("pair").astype(jnp.int32)
    my_partners = lax.dynamic_slice_in_dim(partners, my_owner * slots, slots)
    ids = jnp.arange(owner_of.shape[0], dtype=jnp.int32)
    partner_row = jnp.sum(
        jnp.where(my_partners[:, None] == ids[None, :], owner_of[None, :], 0), axis=1
    )
    total_rows = owner_of.shape[0]
    side_ref = side[None]

    def widened(value):
        zero = jnp.zeros_like(value)
        left = jnp.where(side == 0, value, zero)
        right = jnp.where(side == 1, value, zero)
        return jnp.concatenate((left, right), axis=3)

    mine = widened(incident)
    theirs = from_other(mine)
    exciting, scattered = apply_tmat(mine, theirs, tmat, side_ref)
    for _ in range(ITERS):
        every_field = lax.all_gather(scattered, "owner", axis=0, tiled=True)
        full = lax.all_gather(scattered, "pair", axis=3, tiled=True)
        given_back = backward(block_rows, live, partner_row, full, blocks, total_rows)
        returned = lax.psum_scatter(given_back, "owner", scatter_dimension=0, tiled=True)
        near = forward(block_rows, live, partner_row, every_field, blocks, particles)
        mine = near + widened(incident + returned)
        theirs = from_other(mine)
        exciting, scattered = apply_tmat(mine, theirs, tmat, side_ref)
    return (scattered, exciting)


def solution(mesh):
    in_specs = (
        P("owner", None, None, "pair"),
        P("owner", None, "pair", None),
        P("owner", None, None, "pair"),
        P("owner"),
        P(),
        P("owner"),
        P(),
    )
    out_specs = (P("owner", None, None, "pair"), P("owner", None, None, "pair"))
    return jax.shard_map(local, mesh=mesh, in_specs=in_specs, out_specs=out_specs, check_vma=False)
```

```python
import functools

import jax
import jax.numpy as jnp
from jax import lax
from jax.experimental import pallas as pl
from jax.experimental.pallas import tpu as pltpu
from jax.sharding import PartitionSpec as P

ITERS = 2
COLUMNS = 4
F32 = jnp.float32
BF16 = jnp.bfloat16
MIB = 1 << 20


def split_value(value):
    high = value.astype(BF16)
    low = (value - high.astype(F32)).astype(BF16)
    return high, low


def stacked_parts(real, imag):
    real_high, real_low = split_value(real)
    imag_high, imag_low = split_value(imag)
    with_real = jnp.concatenate((real_high, imag_high, real_low, imag_low), axis=0)
    with_imag = jnp.concatenate((-imag_high, real_high, -imag_low, real_low), axis=0)
    return with_real, with_imag


def dot_nt(left, right):
    return lax.dot_general(left, right, (((1,), (1,)), ((), ())), preferred_element_type=F32)


def dot_nn(left, right):
    return jnp.dot(left, right, preferred_element_type=F32)


def tmat_kernel(mine_ref, theirs_ref, tmat_ref, side_ref, exciting_ref, scattered_ref):
    particles, _, directions, width = mine_ref.shape
    half = width // 2
    start = pl.multiple_of(side_ref[0] * half, half)
    for row in range(particles):
        real = mine_ref[row, 0] + theirs_ref[row, 0]
        imag = mine_ref[row, 1] + theirs_ref[row, 1]
        with_real, with_imag = stacked_parts(real, imag)
        real_high, real_low = split_value(tmat_ref[row, 0])
        imag_high, imag_low = split_value(tmat_ref[row, 1])
        total = dot_nt(real_high, with_real) + dot_nt(imag_high, with_imag)
        rest = dot_nt(real_low, with_real[: 2 * directions])
        rest += dot_nt(imag_low, with_imag[: 2 * directions])
        out = total[:, : 2 * directions] + total[:, 2 * directions :] + rest
        out = out.T
        scattered_ref[row, 0] = out[:directions]
        scattered_ref[row, 1] = out[directions:]
        for part in range(2):
            window = (row, part, slice(None), pl.ds(start, half))
            exciting_ref[row, part] = mine_ref[window] + theirs_ref[window]


def apply_tmat(mine, theirs, tmat, side):
    particles, _, directions, width = mine.shape
    half_shape = jax.ShapeDtypeStruct((particles, 2, directions, width // 2), F32)
    vmem = pl.BlockSpec(memory_space=pltpu.VMEM)
    return pl.pallas_call(
        tmat_kernel,
        out_shape=(half_shape, half_shape),
        in_specs=[vmem, vmem, vmem, pl.BlockSpec(memory_space=pltpu.SMEM)],
        out_specs=(vmem, vmem),
        compiler_params=pltpu.CompilerParams(vmem_limit_bytes=24 * MIB),
        name="tmat_apply",
    )(mine, theirs, tmat, side)


def backward_kernel(rows_ref, live_ref, place_ref, side_ref, own_ref, other_ref, block_ref, *refs):
    out_refs, left_ref = refs[:-1], refs[-1]
    slot = pl.program_id(0)
    directions, half = own_ref.shape[2], own_ref.shape[3]
    layers = out_refs[0].shape[0]

    @pl.when(slot == 0)
    def _():
        for field_ref, side in ((own_ref, side_ref[0]), (other_ref, 1 - side_ref[0])):
            columns = pl.ds(pl.multiple_of(side * half, half), half)
            for row in range(field_ref.shape[0]):
                with_real, with_imag = stacked_parts(field_ref[row, 0], field_ref[row, 1])
                left_ref[row, 0, :, columns] = with_real
                left_ref[row, 1, :, columns] = with_imag
        for out_ref in out_refs:
            out_ref[...] = jnp.zeros_like(out_ref)

    @pl.when(slot < live_ref[0])
    def _():
        holder = rows_ref[slot]
        real_high, real_low = split_value(block_ref[0, 0])
        imag_high, imag_low = split_value(block_ref[0, 1])
        total = dot_nn(left_ref[holder, 0], real_high) + dot_nn(left_ref[holder, 1], imag_high)
        rest = dot_nn(left_ref[holder, 0, : 2 * directions], real_low)
        rest += dot_nn(left_ref[holder, 1, : 2 * directions], imag_low)
        out = total[: 2 * directions] + total[2 * directions :] + rest
        place = place_ref[slot]
        which, layer = place // layers, place % layers
        for number, out_ref in enumerate(out_refs):

            @pl.when(which == number)
            def _():
                out_ref[layer, 0] = out[:directions]
                out_ref[layer, 1] = out[directions:]


def slot_block(slot, rows_ref, live_ref, *refs):
    return (jnp.minimum(slot, live_ref[0] - 1), 0, 0, 0)


def backward(rows, live, place, side, own_half, other_half, blocks, layers):
    slots, _, width, half = blocks.shape
    particles, _, directions, _ = own_half.shape
    whole = pl.BlockSpec(own_half.shape, lambda slot, *refs: (0, 0, 0, 0))
    count = COLUMNS * particles
    shape = (layers, 2, directions, half)
    grid_spec = pltpu.PrefetchScalarGridSpec(
        num_scalar_prefetch=4,
        grid=(slots,),
        in_specs=[
            whole,
            whole,
            pl.BlockSpec((1, 2, width, half), slot_block),
        ],
        out_specs=[pl.BlockSpec(shape, lambda slot, *refs: (0, 0, 0, 0))] * count,
        scratch_shapes=[pltpu.VMEM((particles, 2, 4 * directions, width), BF16)],
    )
    return pl.pallas_call(
        backward_kernel,
        grid_spec=grid_spec,
        out_shape=[jax.ShapeDtypeStruct(shape, F32)] * count,
        compiler_params=pltpu.CompilerParams(
            vmem_limit_bytes=44 * MIB, dimension_semantics=("arbitrary",)
        ),
        cost_estimate=pl.CostEstimate(
            flops=slots * 16 * directions * width * half,
            bytes_accessed=blocks.size * 4,
            transcendentals=0,
        ),
        name="blocks_backward",
    )(rows, live, place, side, own_half, other_half, blocks)


def forward_kernel(pieces, rows_ref, live_ref, place_ref, *refs):
    field_refs = refs[: len(pieces)]
    block_ref, out_ref, every_ref, acc_ref = refs[len(pieces) :]
    slot = pl.program_id(0)
    directions = every_ref.shape[2]

    @pl.when(slot == 0)
    def _():
        acc_ref[...] = jnp.zeros_like(acc_ref)
        for first, field_ref in zip(pieces, field_refs):
            for row in range(field_ref.shape[0]):
                every_ref[first + row] = field_ref[row]

    @pl.when(slot < live_ref[0])
    def _():
        holder = rows_ref[slot]
        place = place_ref[slot]
        with_real, with_imag = stacked_parts(every_ref[place, 0], every_ref[place, 1])
        real_high, real_low = split_value(block_ref[0, 0])
        imag_high, imag_low = split_value(block_ref[0, 1])
        total = dot_nt(real_high, with_real) + dot_nt(imag_high, with_imag)
        total += dot_nt(real_low, with_real) + dot_nt(imag_low, with_imag)
        acc_ref[holder] += total

    @pl.when(slot == pl.num_programs(0) - 1)
    def _():
        for row in range(acc_ref.shape[0]):
            total = acc_ref[row]
            out = (total[:, : 2 * directions] + total[:, 2 * directions :]).T
            out_ref[row, 0] = out[:directions]
            out_ref[row, 1] = out[directions:]


def forward(rows, live, place, fields, blocks, particles):
    slots, _, width, half = blocks.shape
    directions = fields[0][1].shape[2]
    count = sum(value.shape[0] for _, value in fields)
    grid_spec = pltpu.PrefetchScalarGridSpec(
        num_scalar_prefetch=3,
        grid=(slots,),
        in_specs=[
            pl.BlockSpec(value.shape, lambda slot, *refs: (0, 0, 0, 0)) for _, value in fields
        ]
        + [pl.BlockSpec((1, 2, width, half), slot_block)],
        out_specs=pl.BlockSpec(
            (particles, 2, directions, width), lambda slot, *refs: (0, 0, 0, 0)
        ),
        scratch_shapes=[
            pltpu.VMEM((count, 2, directions, half), F32),
            pltpu.VMEM((particles, width, 4 * directions), F32),
        ],
    )
    return pl.pallas_call(
        functools.partial(forward_kernel, tuple(first for first, _ in fields)),
        grid_spec=grid_spec,
        out_shape=jax.ShapeDtypeStruct((particles, 2, directions, width), F32),
        compiler_params=pltpu.CompilerParams(
            vmem_limit_bytes=48 * MIB, dimension_semantics=("arbitrary",)
        ),
        cost_estimate=pl.CostEstimate(
            flops=slots * 16 * directions * width * half,
            bytes_accessed=blocks.size * 4,
            transcendentals=0,
        ),
        name="blocks_forward",
    )(rows, live, place, *[value for _, value in fields], blocks)


def across(value, bit):
    count = lax.axis_size("owner")
    return lax.ppermute(value, "owner", [(source, source ^ bit) for source in range(count)])


def along(value, shift):
    count = lax.axis_size("owner")
    step = shift * COLUMNS
    return lax.ppermute(
        value, "owner", [(source, (source + step) % count) for source in range(count)]
    )


def gather_rows(own, layers):
    particles = len(own)
    split = (particles + 1) // 2
    rest = range(1, layers)
    first_x = [across(value, 1) for value in own]
    first_y = [across(value, 2) for value in own]
    shifted = [[along(value, -shift) for value in own] for shift in rest]
    tails = [
        jnp.concatenate([shifted[shift - 1][particle] for shift in rest], axis=0)
        for particle in range(particles)
    ]
    first_d = [
        across(first_x[particle], 2) if particle < split else across(first_y[particle], 1)
        for particle in range(particles)
    ]
    tails_x = [across(value, 1) for value in tails]
    tails_y = [across(value, 2) for value in tails]
    tails_d = [
        across(tails_x[particle], 2) if particle < split else across(tails_y[particle], 1)
        for particle in range(particles)
    ]
    found = []
    for column, (heads, ends) in enumerate(
        ((own, tails), (first_x, tails_x), (first_y, tails_y), (first_d, tails_d))
    ):
        for particle in range(particles):
            base = (column * particles + particle) * layers
            found.append((base, heads[particle]))
            found.append((base + 1, ends[particle]))
    return found


def sum_back(products, particles, layers):
    split = (particles + 1) // 2
    own, to_x, to_y, to_d = (
        list(products[column * particles : (column + 1) * particles]) for column in range(COLUMNS)
    )
    for particle in range(particles):
        if particle < split:
            to_y[particle] = to_y[particle] + across(to_d[particle], 1)
        else:
            to_x[particle] = to_x[particle] + across(to_d[particle], 2)
    from_x = [across(value, 1) for value in to_x]
    from_y = [across(value, 2) for value in to_y]
    sums = [
        [own[particle][layer] + from_x[particle][layer] + from_y[particle][layer] for particle in range(particles)]
        for layer in range(layers)
    ]
    total = sums[0]
    for layer in range(1, layers):
        arrived = along(jnp.stack(sums[layer]), layer)
        total = [total[particle] + arrived[particle] for particle in range(particles)]
    return jnp.stack(total)


def from_other(value):
    return lax.ppermute(value, "pair", [(0, 1), (1, 0)])


def local(incident, tmat, blocks, block_rows, partners, live, owner_of):
    particles, _, directions, half = incident.shape
    slots = blocks.shape[0]
    layers = lax.axis_size("owner") // COLUMNS
    my_owner = lax.axis_index("owner").astype(jnp.int32)
    side = lax.axis_index("pair").astype(jnp.int32)
    my_partners = lax.dynamic_slice_in_dim(partners, my_owner * slots, slots)
    ids = jnp.arange(owner_of.shape[0], dtype=jnp.int32)
    partner_row = jnp.sum(
        jnp.where(my_partners[:, None] == ids[None, :], owner_of[None, :], 0), axis=1
    )
    partner_owner = partner_row // particles
    column = (partner_owner % COLUMNS) ^ (my_owner % COLUMNS)
    layer = (partner_owner // COLUMNS - my_owner // COLUMNS) % layers
    place = (column * particles + partner_row % particles) * layers + layer
    side_ref = side[None]

    def widened(value):
        zero = jnp.zeros_like(value)
        left = jnp.where(side == 0, value, zero)
        right = jnp.where(side == 1, value, zero)
        return jnp.concatenate((left, right), axis=3)

    mine = widened(incident)
    theirs = from_other(mine)
    exciting, scattered = apply_tmat(mine, theirs, tmat, side_ref)
    for _ in range(ITERS):
        own = [scattered[particle : particle + 1] for particle in range(particles)]
        other = from_other(scattered)
        fields = gather_rows(own, layers)
        products = backward(block_rows, live, place, side_ref, scattered, other, blocks, layers)
        near = forward(block_rows, live, place, fields, blocks, particles)
        returned = sum_back(products, particles, layers)
        mine = near + widened(incident + returned)
        theirs = from_other(mine)
        exciting, scattered = apply_tmat(mine, theirs, tmat, side_ref)
    return (scattered, exciting)


def solution(mesh):
    in_specs = (
        P("owner", None, None, "pair"),
        P("owner", None, "pair", None),
        P("owner", None, None, "pair"),
        P("owner"),
        P(),
        P("owner"),
        P(),
    )
    out_specs = (P("owner", None, None, "pair"), P("owner", None, None, "pair"))
    return jax.shard_map(local, mesh=mesh, in_specs=in_specs, out_specs=out_specs, check_vma=False)
```

```python
import functools

import jax
import jax.numpy as jnp
from jax import lax
from jax.experimental import pallas as pl
from jax.experimental.pallas import tpu as pltpu
from jax.sharding import PartitionSpec as P

ITERS = 2
COLUMNS = 4
BUFFERS = 4
F32 = jnp.float32
BF16 = jnp.bfloat16
MIB = 1 << 20
VMEM = pl.BlockSpec(memory_space=pltpu.VMEM)
SMEM = pl.BlockSpec(memory_space=pltpu.SMEM)
HBM = pl.BlockSpec(memory_space=pltpu.MemorySpace.HBM)


def split_value(value):
    high = value.astype(BF16)
    low = (value - high.astype(F32)).astype(BF16)
    return high, low


def stacked_parts(real, imag):
    real_high, real_low = split_value(real)
    imag_high, imag_low = split_value(imag)
    with_real = jnp.concatenate((real_high, imag_high, real_low, imag_low), axis=0)
    with_imag = jnp.concatenate((-imag_high, real_high, -imag_low, real_low), axis=0)
    return with_real, with_imag


def dot_nt(left, right):
    return lax.dot_general(left, right, (((1,), (1,)), ((), ())), preferred_element_type=F32)


def dot_nn(left, right):
    return jnp.dot(left, right, preferred_element_type=F32)


def params(*byte_counts):
    return pltpu.CompilerParams(vmem_limit_bytes=sum(byte_counts) + 6 * MIB)


def size_of(*arrays):
    return sum(value.size * value.dtype.itemsize for value in arrays)


def place_of(column, particle, layer, particles, layers):
    return (column * particles + particle) * layers + layer


def tmat_kernel(mine_ref, theirs_ref, tmat_ref, side_ref, exciting_ref, scattered_ref):
    particles, _, directions, width = mine_ref.shape
    half = width // 2
    start = pl.multiple_of(side_ref[0] * half, half)
    for row in range(particles):
        real = mine_ref[row, 0] + theirs_ref[row, 0]
        imag = mine_ref[row, 1] + theirs_ref[row, 1]
        with_real, with_imag = stacked_parts(real, imag)
        real_high, real_low = split_value(tmat_ref[row, 0])
        imag_high, imag_low = split_value(tmat_ref[row, 1])
        left = jnp.concatenate((real_high, imag_high, real_low, imag_low), axis=1)
        right = jnp.concatenate((with_real, with_imag, with_real, with_imag), axis=1)
        total = dot_nt(left, right)
        out = (total[:, : 2 * directions] + total[:, 2 * directions :]).T
        scattered_ref[row, 0] = out[:directions]
        scattered_ref[row, 1] = out[directions:]
        for part in range(2):
            window = (row, part, slice(None), pl.ds(start, half))
            exciting_ref[row, part] = mine_ref[window] + theirs_ref[window]


def apply_tmat(mine, theirs, tmat, side):
    particles, _, directions, width = mine.shape
    half_shape = jax.ShapeDtypeStruct((particles, 2, directions, width // 2), F32)
    return pl.pallas_call(
        tmat_kernel,
        out_shape=(half_shape, half_shape),
        in_specs=[VMEM, VMEM, VMEM, SMEM],
        out_specs=(VMEM, VMEM),
        compiler_params=params(2 * size_of(mine, theirs, tmat)),
        name="tmat_apply",
    )(mine, theirs, tmat, side)


def backward_kernel(first, rows_ref, live_ref, place_ref, side_ref, own_ref, other_ref, blocks_ref, *refs):
    if first:
        out_ref, parts_ref, left_ref, buf_ref, sems, made_ref, made_sems = refs
    else:
        out_ref, left_ref, buf_ref, sems = refs
    directions, half = own_ref.shape[2], own_ref.shape[3]
    width = 2 * half
    alive = live_ref[0]

    def fetch(slot, place):
        return pltpu.make_async_copy(blocks_ref.at[slot], buf_ref.at[place], sems.at[place])

    def keep(slot, place):
        return pltpu.make_async_copy(made_ref.at[place], parts_ref.at[slot], made_sems.at[place])

    for early in range(BUFFERS):

        @pl.when(early < alive)
        def _():
            fetch(early, early).start()

    for field_ref, side in ((own_ref, side_ref[0]), (other_ref, 1 - side_ref[0])):
        for row in range(field_ref.shape[0]):
            with_real, with_imag = stacked_parts(field_ref[row, 0], field_ref[row, 1])
            for part, value in enumerate((with_real, with_imag)):
                start = pl.multiple_of(part * width + side * half, half)
                left_ref[row, :, pl.ds(start, half)] = value
    out_ref[...] = jnp.zeros_like(out_ref)

    def body(slot, carry):
        here = lax.rem(slot, BUFFERS)
        fetch(slot, here).wait()
        holder = rows_ref[slot]
        if first:
            spot = lax.rem(slot, 2)

            @pl.when(slot >= 2)
            def _():
                keep(slot - 2, spot).wait()

            high, low = split_value(buf_ref[here].reshape(2 * width, half))
            made_ref[spot, 0] = high.reshape(2, width, half)
            made_ref[spot, 1] = low.reshape(2, width, half)
            keep(slot, spot).start()
        else:
            high = buf_ref[here, 0].reshape(2 * width, half)
            low = buf_ref[here, 1].reshape(2 * width, half)
        total = dot_nn(left_ref[holder], high)
        rest = dot_nn(left_ref[holder, : 2 * directions], low)
        out = total[: 2 * directions] + total[2 * directions :] + rest
        place = place_ref[slot]
        out_ref[place, 0] = out[:directions]
        out_ref[place, 1] = out[directions:]

        @pl.when(slot + BUFFERS < alive)
        def _():
            fetch(slot + BUFFERS, here).start()

        return carry

    lax.fori_loop(0, alive, body, 0)
    if first:

        @pl.when(alive >= 2)
        def _():
            keep(alive - 2, lax.rem(alive, 2)).wait()

        keep(alive - 1, lax.rem(alive - 1, 2)).wait()


def backward(first, rows, live, place, side, own_half, other_half, blocks, total_rows):
    particles, _, directions, half = own_half.shape
    width = 2 * half
    slots = blocks.shape[0]
    out_shape = [jax.ShapeDtypeStruct((total_rows, 2, directions, half), F32)]
    out_specs = [VMEM]
    scratch = [
        pltpu.VMEM((particles, 4 * directions, 2 * width), BF16),
        pltpu.VMEM((BUFFERS,) + blocks.shape[1:], blocks.dtype),
        pltpu.SemaphoreType.DMA((BUFFERS,)),
    ]
    if first:
        out_shape.append(jax.ShapeDtypeStruct((slots, 2, 2, width, half), BF16))
        out_specs.append(HBM)
        scratch.append(pltpu.VMEM((2, 2, 2, width, half), BF16))
        scratch.append(pltpu.SemaphoreType.DMA((2,)))
    return pl.pallas_call(
        functools.partial(backward_kernel, first),
        out_shape=out_shape,
        in_specs=[SMEM, SMEM, SMEM, SMEM, VMEM, VMEM, HBM],
        out_specs=out_specs,
        scratch_shapes=scratch,
        compiler_params=params(2 * size_of(own_half) + size_of(*out_shape[:1]), 9 * MIB),
        cost_estimate=pl.CostEstimate(
            flops=slots * 48 * directions * width * half,
            bytes_accessed=size_of(blocks) * (2 if first else 1),
            transcendentals=0,
        ),
        name="blocks_backward",
    )(rows, live, place, side, own_half, other_half, blocks)


def forward_kernel(copies, count, rows_ref, live_ref, place_ref, *refs):
    field_refs = refs[:count]
    parts_ref, out_ref, every_ref, acc_ref, buf_ref, sems = refs[count:]
    directions = out_ref.shape[2]
    alive = live_ref[0]

    def fetch(slot, place):
        return pltpu.make_async_copy(parts_ref.at[slot], buf_ref.at[place], sems.at[place])

    for early in range(BUFFERS):

        @pl.when(early < alive)
        def _():
            fetch(early, early).start()

    acc_ref[...] = jnp.zeros_like(acc_ref)
    for number, row, place in copies:
        every_ref[place] = field_refs[number][row]

    def body(slot, carry):
        here = lax.rem(slot, BUFFERS)
        holder = rows_ref[slot]
        place = place_ref[slot]
        with_real, with_imag = stacked_parts(every_ref[place, 0], every_ref[place, 1])
        right = jnp.concatenate((with_real, with_imag, with_real, with_imag), axis=1)
        fetch(slot, here).wait()
        left = jnp.concatenate(
            (buf_ref[here, 0, 0], buf_ref[here, 0, 1], buf_ref[here, 1, 0], buf_ref[here, 1, 1]),
            axis=1,
        )
        acc_ref[holder] += dot_nt(left, right)

        @pl.when(slot + BUFFERS < alive)
        def _():
            fetch(slot + BUFFERS, here).start()

        return carry

    lax.fori_loop(0, alive, body, 0)
    for row in range(acc_ref.shape[0]):
        total = acc_ref[row]
        out = (total[:, : 2 * directions] + total[:, 2 * directions :]).T
        out_ref[row, 0] = out[:directions]
        out_ref[row, 1] = out[directions:]


def forward(rows, live, place, fields, copies, parts, particles):
    slots, _, _, width, half = parts.shape
    directions = fields[0].shape[2]
    every = (len(copies), 2, directions, half)
    out_shape = jax.ShapeDtypeStruct((particles, 2, directions, width), F32)
    return pl.pallas_call(
        functools.partial(forward_kernel, copies, len(fields)),
        out_shape=out_shape,
        in_specs=[SMEM, SMEM, SMEM] + [VMEM] * len(fields) + [HBM],
        out_specs=VMEM,
        scratch_shapes=[
            pltpu.VMEM(every, F32),
            pltpu.VMEM((particles, width, 4 * directions), F32),
            pltpu.VMEM((BUFFERS,) + parts.shape[1:], BF16),
            pltpu.SemaphoreType.DMA((BUFFERS,)),
        ],
        compiler_params=params(3 * size_of(*fields), 8 * MIB),
        cost_estimate=pl.CostEstimate(
            flops=slots * 48 * directions * width * half,
            bytes_accessed=size_of(parts),
            transcendentals=0,
        ),
        name="blocks_forward",
    )(rows, live, place, *fields, parts)


def pack_kernel(plans, count, *refs):
    in_refs, out_refs = refs[:count], refs[count:]
    for out_ref, plan in zip(out_refs, plans):
        for row, terms in enumerate(plan):
            value = in_refs[terms[0][0]][terms[0][1]]
            for number, source in terms[1:]:
                value = value + in_refs[number][source]
            out_ref[row] = value


def pack(name, inputs, plans):
    shapes = [jax.ShapeDtypeStruct((len(plan),) + inputs[0].shape[1:], F32) for plan in plans]
    return pl.pallas_call(
        functools.partial(pack_kernel, plans, len(inputs)),
        out_shape=shapes,
        in_specs=[VMEM] * len(inputs),
        out_specs=[VMEM] * len(plans),
        compiler_params=params(size_of(*inputs), size_of(*shapes)),
        name=name,
    )(*inputs)


def total_kernel(count, near_ref, side_ref, products_ref, incident_ref, *refs):
    more, out_ref = refs[:count], refs[count]
    particles, half = incident_ref.shape[0], incident_ref.shape[3]
    layers = products_ref.shape[0] // (COLUMNS * particles)
    start = pl.multiple_of(side_ref[0] * half, half)
    out_ref[...] = near_ref[...]
    for particle in range(particles):
        value = incident_ref[particle] + products_ref[particle * layers]
        for ref in more:
            value = value + ref[particle]
        window = (particle, slice(None), slice(None), pl.ds(start, half))
        out_ref[window] = near_ref[window] + value


def whole_total(near, side, products, incident, more):
    return pl.pallas_call(
        functools.partial(total_kernel, len(more)),
        out_shape=jax.ShapeDtypeStruct(near.shape, F32),
        in_specs=[VMEM, SMEM] + [VMEM] * (2 + len(more)),
        out_specs=VMEM,
        compiler_params=params(size_of(near, near, products, incident, *more)),
        name="total",
    )(near, side, products, incident, *more)


def from_other(value):
    return lax.ppermute(value, "pair", [(0, 1), (1, 0)])


def across(value, bit):
    count = lax.axis_size("owner")
    return lax.ppermute(value, "owner", [(source, source ^ bit) for source in range(count)])


def along(value, shift):
    count = lax.axis_size("owner")
    step = shift * COLUMNS
    return lax.ppermute(
        value, "owner", [(source, (source + step) % count) for source in range(count)]
    )


def scatter_step(incident, scattered, blocks, parts, block_rows, live, place, side, layers):
    particles = incident.shape[0]
    every = range(particles)
    by_x = range((particles + 1) // 2)
    by_y = range((particles + 1) // 2, particles)
    rest = range(1, layers)
    at = functools.partial(place_of, particles=particles, layers=layers)
    total_rows = COLUMNS * particles * layers

    other = from_other(scattered)
    x1 = across(scattered, 1)
    y1 = across(scattered, 2)
    z1 = [along(scattered, -shift) for shift in rest]
    if parts is None:
        products, parts = backward(
            True, block_rows, live, place, side, scattered, other, blocks, total_rows
        )
    else:
        (products,) = backward(
            False, block_rows, live, place, side, scattered, other, parts, total_rows
        )

    inputs = [products] + z1
    z_rows = [[(shift, particle)] for shift in rest for particle in every]
    x_plan = z_rows + [[(0, at(3, particle, shift))] for particle in by_x for shift in rest]
    y_plan = z_rows + [[(0, at(3, particle, shift))] for particle in by_y for shift in rest]
    x2, y2 = pack("pack_second", inputs, [x_plan, y_plan])
    x2, y2 = across(x2, 1), across(y2, 2)

    def tail_row(particle, shift):
        return (shift - 1) * particles + particle

    def diagonal_row(particle, shift):
        return len(rest) * particles + (particle % len(by_x)) * len(rest) + shift - 1

    inputs = [products, x1, y1, x2, y2]
    x_plan, y_plan = [], []
    for particle in by_y:
        x_plan += [[(2, particle)]] + [[(4, tail_row(particle, shift))] for shift in rest]
    for particle in by_x:
        y_plan += [[(1, particle)]] + [[(3, tail_row(particle, shift))] for shift in rest]
    x_first, y_first = len(x_plan), len(y_plan)
    for particle in every:
        for shift in rest:
            x_terms = [(0, at(1, particle, shift))]
            y_terms = [(0, at(2, particle, shift))]
            if particle in by_x:
                y_terms.append((3, diagonal_row(particle, shift)))
            else:
                x_terms.append((4, diagonal_row(particle, shift)))
            x_plan.append(x_terms)
            y_plan.append(y_terms)
    x_last, y_last = len(x_plan), len(y_plan)
    x_plan += [[(0, at(3, particle, 0))] for particle in by_x]
    y_plan += [[(0, at(3, particle, 0))] for particle in by_y]
    x3, y3 = pack("pack_third", inputs, [x_plan, y_plan])
    x3, y3 = across(x3, 1), across(y3, 2)

    inputs = [products, x3, y3]
    x_plan, y_plan = [], []
    for particle in every:
        x_terms = [(0, at(1, particle, 0))]
        y_terms = [(0, at(2, particle, 0))]
        if particle in by_x:
            y_terms.append((1, x_last + particle))
        else:
            x_terms.append((2, y_last + particle - len(by_x)))
        x_plan.append(x_terms)
        y_plan.append(y_terms)
    z_plans = []
    for shift in rest:
        rows = []
        for particle in every:
            number = particle * len(rest) + shift - 1
            rows.append([(0, at(0, particle, shift)), (1, x_first + number), (2, y_first + number)])
        z_plans.append(rows)
    x4, y4, *z4 = pack("pack_fourth", inputs, [x_plan, y_plan] + z_plans)
    x4, y4 = across(x4, 1), across(y4, 2)
    z4 = [along(value, shift) for shift, value in zip(rest, z4)]

    fields = [scattered, x1, y1, x2, y2, x3, y3] + z1
    copies = []
    for particle in every:
        copies.append((0, particle, at(0, particle, 0)))
        copies.append((1, particle, at(1, particle, 0)))
        copies.append((2, particle, at(2, particle, 0)))
        for shift in rest:
            copies.append((6 + shift, particle, at(0, particle, shift)))
            copies.append((3, tail_row(particle, shift), at(1, particle, shift)))
            copies.append((4, tail_row(particle, shift), at(2, particle, shift)))
    for number, group in ((5, by_y), (6, by_x)):
        for order, particle in enumerate(group):
            for layer in range(layers):
                copies.append((number, order * layers + layer, at(3, particle, layer)))
    near = forward(block_rows, live, place, fields, tuple(copies), parts, particles)
    return whole_total(near, side, products, incident, [x4, y4] + z4), parts


def local(incident, tmat, blocks, block_rows, partners, live, owner_of):
    particles = incident.shape[0]
    slots = blocks.shape[0]
    layers = lax.axis_size("owner") // COLUMNS
    my_owner = lax.axis_index("owner").astype(jnp.int32)
    side = lax.axis_index("pair").astype(jnp.int32)
    my_partners = lax.dynamic_slice_in_dim(partners, my_owner * slots, slots)
    ids = jnp.arange(owner_of.shape[0], dtype=jnp.int32)
    partner_row = jnp.sum(
        jnp.where(my_partners[:, None] == ids[None, :], owner_of[None, :], 0), axis=1
    )
    partner_owner = partner_row // particles
    column = (partner_owner % COLUMNS) ^ (my_owner % COLUMNS)
    layer = (partner_owner // COLUMNS - my_owner // COLUMNS) % layers
    place = place_of(column, partner_row % particles, layer, particles, layers)
    side_ref = side[None]

    zero = jnp.zeros_like(incident)
    mine = jnp.concatenate(
        (jnp.where(side == 0, incident, zero), jnp.where(side == 1, incident, zero)), axis=3
    )
    theirs = from_other(mine)
    exciting, scattered = apply_tmat(mine, theirs, tmat, side_ref)
    parts = None
    for _ in range(ITERS):
        mine, parts = scatter_step(
            incident, scattered, blocks, parts, block_rows, live, place, side_ref, layers
        )
        theirs = from_other(mine)
        exciting, scattered = apply_tmat(mine, theirs, tmat, side_ref)
    return (scattered, exciting)


def solution(mesh):
    in_specs = (
        P("owner", None, None, "pair"),
        P("owner", None, "pair", None),
        P("owner", None, None, "pair"),
        P("owner"),
        P(),
        P("owner"),
        P(),
    )
    out_specs = (P("owner", None, None, "pair"), P("owner", None, None, "pair"))
    return jax.shard_map(local, mesh=mesh, in_specs=in_specs, out_specs=out_specs, check_vma=False)
```

```python
import functools

import jax
import jax.numpy as jnp
from jax import lax
from jax.experimental import pallas as pl
from jax.experimental.pallas import tpu as pltpu
from jax.sharding import PartitionSpec as P

ITERS = 2
COLUMNS = 4
BUFFERS = 4
F32 = jnp.float32
BF16 = jnp.bfloat16
MIB = 1 << 20
STREAM_LIMIT = 48 * MIB
VMEM = pl.BlockSpec(memory_space=pltpu.VMEM)
SMEM = pl.BlockSpec(memory_space=pltpu.SMEM)
ANY = pl.BlockSpec(memory_space=pl.ANY)
HBM = pl.BlockSpec(memory_space=pltpu.MemorySpace.HBM)


def split_value(value):
    high = value.astype(BF16)
    low = (value - high.astype(F32)).astype(BF16)
    return high, low


def stacked_parts(real, imag):
    real_high, real_low = split_value(real)
    imag_high, imag_low = split_value(imag)
    with_real = jnp.concatenate((real_high, imag_high, real_low, imag_low), axis=0)
    with_imag = jnp.concatenate((-imag_high, real_high, -imag_low, real_low), axis=0)
    return with_real, with_imag


def dot_nt(left, right):
    return lax.dot_general(left, right, (((1,), (1,)), ((), ())), preferred_element_type=F32)


def dot_nn(left, right):
    return jnp.dot(left, right, preferred_element_type=F32)


def params(*byte_counts):
    return pltpu.CompilerParams(vmem_limit_bytes=sum(byte_counts) + 6 * MIB)


def size_of(*arrays):
    return sum(value.size * value.dtype.itemsize for value in arrays)


def place_of(column, particle, layer, particles, layers):
    return (column * particles + particle) * layers + layer


def tmat_kernel(mine_ref, theirs_ref, tmat_ref, side_ref, exciting_ref, scattered_ref):
    particles, _, directions, width = mine_ref.shape
    half = width // 2
    start = pl.multiple_of(side_ref[0] * half, half)
    for row in range(particles):
        real = mine_ref[row, 0] + theirs_ref[row, 0]
        imag = mine_ref[row, 1] + theirs_ref[row, 1]
        with_real, with_imag = stacked_parts(real, imag)
        real_high, real_low = split_value(tmat_ref[row, 0])
        imag_high, imag_low = split_value(tmat_ref[row, 1])
        left = jnp.concatenate((real_high, imag_high, real_low, imag_low), axis=1)
        right = jnp.concatenate((with_real, with_imag, with_real, with_imag), axis=1)
        total = dot_nt(left, right)
        out = (total[:, : 2 * directions] + total[:, 2 * directions :]).T
        scattered_ref[row, 0] = out[:directions]
        scattered_ref[row, 1] = out[directions:]
        for part in range(2):
            window = (row, part, slice(None), pl.ds(start, half))
            exciting_ref[row, part] = mine_ref[window] + theirs_ref[window]


def apply_tmat(mine, theirs, tmat, side):
    particles, _, directions, width = mine.shape
    half_shape = jax.ShapeDtypeStruct((particles, 2, directions, width // 2), F32)
    return pl.pallas_call(
        tmat_kernel,
        out_shape=(half_shape, half_shape),
        in_specs=[VMEM, VMEM, VMEM, SMEM],
        out_specs=(VMEM, VMEM),
        compiler_params=params(2 * size_of(mine, theirs, tmat)),
        name="tmat_apply",
    )(mine, theirs, tmat, side)


def chosen_slots(group_ref, alive, groups, list_ref):
    def step(slot, found):
        list_ref[found] = slot
        group = group_ref[slot]
        wanted = jnp.logical_and(group >= groups[0], group <= groups[1])
        return found + jnp.where(wanted, 1, 0)

    return lax.fori_loop(0, alive, step, 0)


def backward_kernel(first, groups, base, rows_ref, live_ref, place_ref, group_ref, side_ref, *refs):
    own_ref, other_ref, blocks_ref = refs[:3]
    refs = refs[3:]
    if first:
        out_ref, parts_ref, list_ref, left_ref, buf_ref, sems, made_ref, made_sems = refs[-8:]
    else:
        out_ref, list_ref, left_ref, buf_ref, sems = refs
    directions, half = own_ref.shape[2], own_ref.shape[3]
    width = 2 * half
    wanted = chosen_slots(group_ref, live_ref[0], groups, list_ref)

    def fetch(turn, place):
        return pltpu.make_async_copy(
            blocks_ref.at[list_ref[turn]], buf_ref.at[place], sems.at[place]
        )

    def keep(turn, place):
        return pltpu.make_async_copy(
            made_ref.at[place], parts_ref.at[list_ref[turn]], made_sems.at[place]
        )

    for early in range(BUFFERS):

        @pl.when(early < wanted)
        def _():
            fetch(early, early).start()

    for field_ref, side in ((own_ref, side_ref[0]), (other_ref, 1 - side_ref[0])):
        for row in range(field_ref.shape[0]):
            with_real, with_imag = stacked_parts(field_ref[row, 0], field_ref[row, 1])
            for part, value in enumerate((with_real, with_imag)):
                start = pl.multiple_of(part * width + side * half, half)
                left_ref[row, :, pl.ds(start, half)] = value
    out_ref[...] = jnp.zeros_like(out_ref)

    def body(turn, carry):
        here = lax.rem(turn, BUFFERS)
        fetch(turn, here).wait()
        slot = list_ref[turn]
        holder = rows_ref[slot]
        if first:
            spot = lax.rem(turn, 2)

            @pl.when(turn >= 2)
            def _():
                keep(turn - 2, spot).wait()

            high, low = split_value(buf_ref[here].reshape(2 * width, half))
            made_ref[spot, 0] = high.reshape(2, width, half)
            made_ref[spot, 1] = low.reshape(2, width, half)
            keep(turn, spot).start()
        else:
            high = buf_ref[here, 0].reshape(2 * width, half)
            low = buf_ref[here, 1].reshape(2 * width, half)
        total = dot_nn(left_ref[holder], high)
        rest = dot_nn(left_ref[holder, : 2 * directions], low)
        out = total[: 2 * directions] + total[2 * directions :] + rest
        place = place_ref[slot] - base
        out_ref[place, 0] = out[:directions]
        out_ref[place, 1] = out[directions:]

        @pl.when(turn + BUFFERS < wanted)
        def _():
            fetch(turn + BUFFERS, here).start()

        return carry

    lax.fori_loop(0, wanted, body, 0)
    if first:

        @pl.when(wanted >= 2)
        def _():
            keep(wanted - 2, lax.rem(wanted, 2)).wait()

        @pl.when(wanted >= 1)
        def _():
            keep(wanted - 1, lax.rem(wanted - 1, 2)).wait()


def backward(first, groups, base, count, index, side, own_half, other_half, blocks, parts):
    particles, _, directions, half = own_half.shape
    width = 2 * half
    slots = blocks.shape[0]
    out_shape = [jax.ShapeDtypeStruct((count, 2, directions, half), F32)]
    out_specs = [VMEM]
    source = blocks if first else parts
    scratch = [
        pltpu.SMEM((slots + 1,), jnp.int32),
        pltpu.VMEM((particles, 4 * directions, 2 * width), BF16),
        pltpu.VMEM((BUFFERS,) + source.shape[1:], source.dtype),
        pltpu.SemaphoreType.DMA((BUFFERS,)),
    ]
    operands = [*index, side, own_half, other_half, source]
    in_specs = [SMEM] * 5 + [VMEM, VMEM, HBM]
    aliases = {}
    if first:
        out_shape.append(jax.ShapeDtypeStruct((slots, 2, 2, width, half), BF16))
        out_specs.append(HBM)
        scratch.append(pltpu.VMEM((2, 2, 2, width, half), BF16))
        scratch.append(pltpu.SemaphoreType.DMA((2,)))
        if parts is not None:
            aliases = {len(operands): 1}
            operands.append(parts)
            in_specs.append(HBM)
    return pl.pallas_call(
        functools.partial(backward_kernel, first, groups, base),
        out_shape=out_shape,
        in_specs=in_specs,
        out_specs=out_specs,
        scratch_shapes=scratch,
        input_output_aliases=aliases,
        compiler_params=pltpu.CompilerParams(vmem_limit_bytes=STREAM_LIMIT),
        cost_estimate=pl.CostEstimate(
            flops=slots * 24 * directions * width * half,
            bytes_accessed=size_of(blocks) // 2,
            transcendentals=0,
        ),
        name="backward_group" + str(groups[0]),
    )(*operands)


def forward_kernel(groups, copies, count, rows_ref, live_ref, place_ref, group_ref, *refs):
    field_refs = refs[:count]
    parts_ref = refs[count]
    out_ref, list_ref, every_ref, acc_ref, buf_ref, sems = refs[-6:]
    directions = out_ref.shape[2]
    wanted = chosen_slots(group_ref, live_ref[0], groups, list_ref)

    def fetch(turn, place):
        return pltpu.make_async_copy(
            parts_ref.at[list_ref[turn]], buf_ref.at[place], sems.at[place]
        )

    for early in range(BUFFERS):

        @pl.when(early < wanted)
        def _():
            fetch(early, early).start()

    acc_ref[...] = jnp.zeros_like(acc_ref)
    for number, row, place in copies:
        every_ref[place] = field_refs[number][row]

    def body(turn, carry):
        here = lax.rem(turn, BUFFERS)
        slot = list_ref[turn]
        holder = rows_ref[slot]
        place = place_ref[slot]
        with_real, with_imag = stacked_parts(every_ref[place, 0], every_ref[place, 1])
        fetch(turn, here).wait()
        total = dot_nt(with_real, buf_ref[here, 0, 0]) + dot_nt(with_imag, buf_ref[here, 0, 1])
        rest = dot_nt(with_real[: 2 * directions], buf_ref[here, 1, 0])
        rest += dot_nt(with_imag[: 2 * directions], buf_ref[here, 1, 1])
        acc_ref[holder] += total[: 2 * directions] + total[2 * directions :] + rest

        @pl.when(turn + BUFFERS < wanted)
        def _():
            fetch(turn + BUFFERS, here).start()

        return carry

    lax.fori_loop(0, wanted, body, 0)
    for row in range(acc_ref.shape[0]):
        out_ref[row, 0] = acc_ref[row, :directions]
        out_ref[row, 1] = acc_ref[row, directions:]


def forward(groups, index, fields, copies, parts, particles, total_rows, after):
    slots, _, _, width, half = parts.shape
    directions = fields[0].shape[2]
    out_shape = jax.ShapeDtypeStruct((particles, 2, directions, width), F32)
    return pl.pallas_call(
        functools.partial(forward_kernel, groups, copies, len(fields)),
        out_shape=out_shape,
        in_specs=[SMEM] * 4 + [VMEM] * len(fields) + [HBM] + [ANY] * len(after),
        out_specs=VMEM,
        scratch_shapes=[
            pltpu.SMEM((slots + 1,), jnp.int32),
            pltpu.VMEM((total_rows, 2, directions, half), F32),
            pltpu.VMEM((particles, 2 * directions, width), F32),
            pltpu.VMEM((BUFFERS,) + parts.shape[1:], BF16),
            pltpu.SemaphoreType.DMA((BUFFERS,)),
        ],
        compiler_params=pltpu.CompilerParams(vmem_limit_bytes=STREAM_LIMIT),
        cost_estimate=pl.CostEstimate(
            flops=slots * 16 * directions * width * half,
            bytes_accessed=size_of(parts) // 3,
            transcendentals=0,
        ),
        name="forward_group" + str(groups[0]),
    )(*index, *fields, parts, *after)


def pack_kernel(plans, count, *refs):
    in_refs, out_refs = refs[:count], refs[-len(plans) :]
    for out_ref, plan in zip(out_refs, plans):
        for row, terms in enumerate(plan):
            value = in_refs[terms[0][0]][terms[0][1]]
            for number, source in terms[1:]:
                value = value + in_refs[number][source]
            out_ref[row] = value


def pack(name, inputs, plans, after=()):
    shapes = [jax.ShapeDtypeStruct((len(plan),) + inputs[0].shape[1:], F32) for plan in plans]
    return pl.pallas_call(
        functools.partial(pack_kernel, plans, len(inputs)),
        out_shape=shapes,
        in_specs=[VMEM] * len(inputs) + [ANY] * len(after),
        out_specs=[VMEM] * len(plans),
        compiler_params=params(size_of(*inputs), size_of(*shapes)),
        name=name,
    )(*inputs, *after)


def total_kernel(counts, side_ref, incident_ref, *refs):
    nears, halves, out_ref = refs[: counts[0]], refs[counts[0] : -1], refs[-1]
    particles, half = incident_ref.shape[0], incident_ref.shape[3]
    start = pl.multiple_of(side_ref[0] * half, half)
    near = nears[0][...]
    for ref in nears[1:]:
        near = near + ref[...]
    out_ref[...] = near
    for particle in range(particles):
        value = incident_ref[particle]
        for ref, step in zip(halves, counts[1]):
            value = value + ref[particle * step]
        window = (particle, slice(None), slice(None), pl.ds(start, half))
        out_ref[window] = out_ref[window] + value


def whole_total(side, incident, nears, halves):
    arrays = [value for value, _ in halves]
    steps = tuple(step for _, step in halves)
    return pl.pallas_call(
        functools.partial(total_kernel, (len(nears), steps)),
        out_shape=jax.ShapeDtypeStruct(nears[0].shape, F32),
        in_specs=[SMEM] + [VMEM] * (1 + len(nears) + len(arrays)),
        out_specs=VMEM,
        compiler_params=params(size_of(*nears, nears[0], incident, *arrays)),
        name="total",
    )(side, incident, *nears, *arrays)


def from_other(value):
    return lax.ppermute(value, "pair", [(0, 1), (1, 0)])


def across(value, bit):
    count = lax.axis_size("owner")
    return lax.ppermute(value, "owner", [(source, source ^ bit) for source in range(count)])


def along(value, shift):
    count = lax.axis_size("owner")
    step = shift * COLUMNS
    return lax.ppermute(
        value, "owner", [(source, (source + step) % count) for source in range(count)]
    )


def scatter_step(incident, scattered, blocks, parts, index, side, layers):
    particles = incident.shape[0]
    every = range(particles)
    by_x = range((particles + 1) // 2)
    by_y = range((particles + 1) // 2, particles)
    rest = range(1, layers)
    at = functools.partial(place_of, particles=particles, layers=layers)
    total_rows = COLUMNS * particles * layers
    first_d = at(3, 0, 0)
    first = parts is None

    def diagonal(particle, layer):
        return at(0, particle, layer)

    other = from_other(scattered)
    x1 = across(scattered, 1)
    y1 = across(scattered, 2)
    fetched = (side, scattered, other, blocks)
    products_d, *made = backward(
        first, (2, 2), first_d, total_rows - first_d, index, *fetched, parts
    )
    if first:
        parts = made[0]

    inputs = [products_d, x1, y1, scattered]
    x_plan = [[(0, diagonal(particle, layer))] for particle in by_x for layer in range(layers)]
    y_plan = [[(0, diagonal(particle, layer))] for particle in by_y for layer in range(layers)]
    x_head, y_head = len(x_plan), len(y_plan)
    x_plan += [[(2, particle)] for particle in by_y]
    y_plan += [[(1, particle)] for particle in by_x]
    x2, y2, copied = pack(
        "pack_second", inputs, [x_plan, y_plan, [[(3, particle)] for particle in every]]
    )
    x2, y2 = across(x2, 1), across(y2, 2)
    z2 = [along(copied, -shift) for shift in rest]
    products, *made = backward(first, (0, 1), 0, first_d, index, *fetched, parts)
    if first:
        parts = made[0]

    inputs = [products, x2, y2]
    x_plan, y_plan = [], []
    for particle in every:
        for layer in range(layers):
            x_terms = [(0, at(1, particle, layer))]
            y_terms = [(0, at(2, particle, layer))]
            if particle in by_x:
                y_terms.append((1, diagonal(particle, layer)))
            else:
                x_terms.append((2, diagonal(particle - len(by_x), layer)))
            x_plan.append(x_terms)
            y_plan.append(y_terms)
    x3, y3, mark = pack("pack_third", inputs, [x_plan, y_plan, [[(1, 0)]]])
    x3, y3 = across(x3, 1), across(y3, 2)

    fields = [x1, y1] + z2
    copies = []
    for particle in every:
        copies.append((0, particle, at(1, particle, 0)))
        copies.append((1, particle, at(2, particle, 0)))
        for shift in rest:
            copies.append((1 + shift, particle, at(0, particle, shift)))
    near_first = forward(
        (0, 0), index, fields, tuple(copies), parts, particles, total_rows, [mark]
    )

    inputs = [products, x3, y3] + z2
    tails = [[(2 + shift, particle)] for particle in every for shift in rest]
    z_plans = [
        [
            [(0, at(0, particle, shift)), (1, diagonal(particle, shift)), (2, diagonal(particle, shift))]
            for particle in every
        ]
        for shift in rest
    ]
    x4, y4, *z4 = pack("pack_fourth", inputs, [tails, tails] + z_plans, [near_first])
    x4, y4 = across(x4, 1), across(y4, 2)
    z4 = [along(value, shift) for shift, value in zip(rest, z4)]

    def tail(particle, shift):
        return particle * len(rest) + shift - 1

    x5, y5, mark = pack(
        "pack_fifth",
        [x4, y4],
        [
            [[(1, tail(particle, shift))] for particle in by_y for shift in rest],
            [[(0, tail(particle, shift))] for particle in by_x for shift in rest],
            [[(0, 0)]],
        ],
    )
    x5, y5 = across(x5, 1), across(y5, 2)
    copies = []
    for particle in every:
        for shift in rest:
            copies.append((0, tail(particle, shift), at(1, particle, shift)))
            copies.append((1, tail(particle, shift), at(2, particle, shift)))
    near_second = forward(
        (1, 1), index, [x4, y4], tuple(copies), parts, particles, total_rows, [mark]
    )
    copies = []
    for heads, ends, head, group in ((0, 2, x_head, by_y), (1, 3, y_head, by_x)):
        for order, particle in enumerate(group):
            copies.append((heads, head + order, at(3, particle, 0)))
            for shift in rest:
                copies.append((ends, tail(order, shift), at(3, particle, shift)))
    near_last = forward(
        (2, 2), index, [x2, y2, x5, y5], tuple(copies), parts, particles, total_rows, [near_second]
    )
    halves = [(products, layers), (x3, layers), (y3, layers)] + [(value, 1) for value in z4]
    return whole_total(side, incident, [near_first, near_second, near_last], halves), parts


def local(incident, tmat, blocks, block_rows, partners, live, owner_of):
    particles = incident.shape[0]
    slots = blocks.shape[0]
    layers = lax.axis_size("owner") // COLUMNS
    my_owner = lax.axis_index("owner").astype(jnp.int32)
    side = lax.axis_index("pair").astype(jnp.int32)
    my_partners = lax.dynamic_slice_in_dim(partners, my_owner * slots, slots)
    ids = jnp.arange(owner_of.shape[0], dtype=jnp.int32)
    partner_row = jnp.sum(
        jnp.where(my_partners[:, None] == ids[None, :], owner_of[None, :], 0), axis=1
    )
    partner_owner = partner_row // particles
    column = (partner_owner % COLUMNS) ^ (my_owner % COLUMNS)
    layer = (partner_owner // COLUMNS - my_owner // COLUMNS) % layers
    place = place_of(column, partner_row % particles, layer, particles, layers)
    group = jnp.where(column == 3, 2, jnp.where((column == 0) | (layer == 0), 0, 1))
    index = (block_rows, live, place, group)
    side_ref = side[None]

    zero = jnp.zeros_like(incident)
    mine = jnp.concatenate(
        (jnp.where(side == 0, incident, zero), jnp.where(side == 1, incident, zero)), axis=3
    )
    theirs = from_other(mine)
    exciting, scattered = apply_tmat(mine, theirs, tmat, side_ref)
    parts = None
    for _ in range(ITERS):
        mine, parts = scatter_step(
            incident, scattered, blocks, parts, index, side_ref, layers
        )
        theirs = from_other(mine)
        exciting, scattered = apply_tmat(mine, theirs, tmat, side_ref)
    return (scattered, exciting)


def solution(mesh):
    in_specs = (
        P("owner", None, None, "pair"),
        P("owner", None, "pair", None),
        P("owner", None, None, "pair"),
        P("owner"),
        P(),
        P("owner"),
        P(),
    )
    out_specs = (P("owner", None, None, "pair"), P("owner", None, None, "pair"))
    return jax.shard_map(local, mesh=mesh, in_specs=in_specs, out_specs=out_specs, check_vma=False)
```

```python
import functools

import jax
import jax.numpy as jnp
from jax import lax
from jax.experimental import pallas as pl
from jax.experimental.pallas import tpu as pltpu
from jax.sharding import PartitionSpec as P

ITERS = 2
COLUMNS = 4
BUFFERS = 4
F32 = jnp.float32
BF16 = jnp.bfloat16
MIB = 1 << 20
STREAM_LIMIT = 48 * MIB
VMEM = pl.BlockSpec(memory_space=pltpu.VMEM)
SMEM = pl.BlockSpec(memory_space=pltpu.SMEM)
ANY = pl.BlockSpec(memory_space=pl.ANY)
HBM = pl.BlockSpec(memory_space=pltpu.MemorySpace.HBM)


def split_value(value):
    high = value.astype(BF16)
    low = (value - high.astype(F32)).astype(BF16)
    return high, low


def stacked_parts(real, imag):
    real_high, real_low = split_value(real)
    imag_high, imag_low = split_value(imag)
    with_real = jnp.concatenate((real_high, imag_high, real_low, imag_low), axis=0)
    with_imag = jnp.concatenate((-imag_high, real_high, -imag_low, real_low), axis=0)
    return with_real, with_imag


def dot_nt(left, right):
    return lax.dot_general(left, right, (((1,), (1,)), ((), ())), preferred_element_type=F32)


def dot_nn(left, right):
    return jnp.dot(left, right, preferred_element_type=F32)


def params(*byte_counts):
    return pltpu.CompilerParams(vmem_limit_bytes=sum(byte_counts) + 6 * MIB)


def size_of(*arrays):
    return sum(value.size * value.dtype.itemsize for value in arrays)


def place_of(column, particle, layer, particles, layers):
    return (column * particles + particle) * layers + layer


def prepare_kernel(layers, owner_ref, partners_ref, rows_of_ref, tmat_ref, *refs):
    parts_ref, place_ref, group_ref, buf_ref, sems = refs
    particles, _, half, width = tmat_ref.shape
    slots = place_ref.shape[0]

    def fetch(row):
        return pltpu.make_async_copy(tmat_ref.at[row], buf_ref.at[row], sems.at[row])

    for row in range(particles):
        fetch(row).start()
    me = owner_ref[0]
    my_column, my_layer = lax.rem(me, COLUMNS), lax.div(me, COLUMNS)

    def step(slot, carry):
        row = rows_of_ref[partners_ref[me * slots + slot]]
        owner, particle = lax.div(row, particles), lax.rem(row, particles)
        column = lax.bitwise_xor(lax.rem(owner, COLUMNS), my_column)
        layer = lax.rem(lax.div(owner, COLUMNS) - my_layer + layers, layers)
        place_ref[slot] = place_of(column, particle, layer, particles, layers)
        near = jnp.where(column == COLUMNS - 1, 2, 1)
        far = jnp.where(column == COLUMNS - 1, 4, 3)
        group_ref[slot] = jnp.where(column == 0, 0, jnp.where(layer == 0, near, far))
        return carry

    lax.fori_loop(0, slots, step, 0)
    for row in range(particles):
        fetch(row).wait()
        for part in range(2):
            high, low = split_value(buf_ref[row, part])
            parts_ref[row, :, part * width : (part + 1) * width] = high
            parts_ref[row, :, (2 + part) * width : (3 + part) * width] = low


def prepare(my_owner, partners, owner_of, tmat, slots, layers):
    particles, _, half, width = tmat.shape
    index_shape = jax.ShapeDtypeStruct((slots,), jnp.int32)
    return pl.pallas_call(
        functools.partial(prepare_kernel, layers),
        out_shape=(
            jax.ShapeDtypeStruct((particles, half, 4 * width), BF16),
            index_shape,
            index_shape,
        ),
        in_specs=[SMEM, SMEM, SMEM, HBM],
        out_specs=(VMEM, SMEM, SMEM),
        scratch_shapes=[pltpu.VMEM(tmat.shape, F32), pltpu.SemaphoreType.DMA((particles,))],
        compiler_params=params(3 * size_of(tmat)),
        name="prepare",
    )(my_owner, partners, owner_of, tmat)


def tmat_kernel(halves, side_ref, mine_ref, theirs_ref, parts_ref, *refs):
    exciting_ref = refs[0] if len(refs) == 3 else None
    scattered_ref, full_ref = refs[-2:]
    particles, _, directions, width = full_ref.shape
    half = width // 2
    start = pl.multiple_of(side_ref[0] * half, half)
    if halves:
        full_ref[:, :, :, pl.ds(start, half)] = mine_ref[...]
        full_ref[:, :, :, pl.ds(pl.multiple_of(half - start, half), half)] = theirs_ref[...]
    else:
        full_ref[...] = mine_ref[...] + theirs_ref[...]
    for row in range(particles):
        with_real, with_imag = stacked_parts(full_ref[row, 0], full_ref[row, 1])
        right = jnp.concatenate((with_real, with_imag, with_real, with_imag), axis=1)
        total = dot_nt(parts_ref[row], right)
        out = (total[:, : 2 * directions] + total[:, 2 * directions :]).T
        scattered_ref[row, 0] = out[:directions]
        scattered_ref[row, 1] = out[directions:]
    if exciting_ref is not None:
        exciting_ref[...] = full_ref[:, :, :, pl.ds(start, half)]


def apply_tmat(halves, last, side, mine, theirs, parts):
    particles, _, directions, _ = mine.shape
    half = parts.shape[1]
    half_shape = jax.ShapeDtypeStruct((particles, 2, directions, half), F32)
    count = 2 if last else 1
    return pl.pallas_call(
        functools.partial(tmat_kernel, halves),
        out_shape=[half_shape] * count,
        in_specs=[SMEM, VMEM, VMEM, VMEM],
        out_specs=[VMEM] * count,
        scratch_shapes=[pltpu.VMEM((particles, 2, directions, 2 * half), F32)],
        compiler_params=params(3 * size_of(mine, theirs), size_of(parts)),
        name="tmat_apply",
    )(side, mine, theirs, parts)


def chosen_slots(group_ref, alive, groups, list_ref):
    mask = sum(1 << group for group in groups)

    def step(slot, found):
        list_ref[found] = slot
        return found + (lax.shift_right_logical(mask, group_ref[slot]) & 1)

    return lax.fori_loop(0, alive, step, 0)


def backward_kernel(first, groups, base, rows_ref, live_ref, place_ref, group_ref, side_ref, *refs):
    own_ref, other_ref, blocks_ref = refs[:3]
    refs = refs[3:]
    if first:
        out_ref, parts_ref, list_ref, left_ref, buf_ref, sems, made_ref, made_sems = refs[-8:]
    else:
        out_ref, list_ref, left_ref, buf_ref, sems = refs
    directions, half = own_ref.shape[2], own_ref.shape[3]
    width = 2 * half
    wanted = chosen_slots(group_ref, live_ref[0], groups, list_ref)

    def fetch(turn, place):
        return pltpu.make_async_copy(
            blocks_ref.at[list_ref[turn]], buf_ref.at[place], sems.at[place]
        )

    def keep(turn, place):
        return pltpu.make_async_copy(
            made_ref.at[place], parts_ref.at[list_ref[turn]], made_sems.at[place]
        )

    for early in range(BUFFERS):

        @pl.when(early < wanted)
        def _():
            fetch(early, early).start()

    for field_ref, side in ((own_ref, side_ref[0]), (other_ref, 1 - side_ref[0])):
        for row in range(field_ref.shape[0]):
            with_real, with_imag = stacked_parts(field_ref[row, 0], field_ref[row, 1])
            for part, value in enumerate((with_real, with_imag)):
                start = pl.multiple_of(part * width + side * half, half)
                left_ref[row, :, pl.ds(start, half)] = value
    out_ref[...] = jnp.zeros_like(out_ref)

    def body(turn, carry):
        here = lax.rem(turn, BUFFERS)
        fetch(turn, here).wait()
        slot = list_ref[turn]
        holder = rows_ref[slot]
        if first:
            spot = lax.rem(turn, 2)

            @pl.when(turn >= 2)
            def _():
                keep(turn - 2, spot).wait()

            high, low = split_value(buf_ref[here].reshape(2 * width, half))
            made_ref[spot, 0] = high.reshape(2, width, half)
            made_ref[spot, 1] = low.reshape(2, width, half)
            keep(turn, spot).start()
        else:
            high = buf_ref[here, 0].reshape(2 * width, half)
            low = buf_ref[here, 1].reshape(2 * width, half)
        total = dot_nn(left_ref[holder], high)
        rest = dot_nn(left_ref[holder, : 2 * directions], low)
        out = total[: 2 * directions] + total[2 * directions :] + rest
        place = place_ref[slot] - base
        out_ref[place, 0] = out[:directions]
        out_ref[place, 1] = out[directions:]

        @pl.when(turn + BUFFERS < wanted)
        def _():
            fetch(turn + BUFFERS, here).start()

        return carry

    lax.fori_loop(0, wanted, body, 0)
    if first:

        @pl.when(wanted >= 2)
        def _():
            keep(wanted - 2, lax.rem(wanted, 2)).wait()

        @pl.when(wanted >= 1)
        def _():
            keep(wanted - 1, lax.rem(wanted - 1, 2)).wait()


def backward(first, groups, base, count, index, side, own_half, other_half, blocks, parts):
    particles, _, directions, half = own_half.shape
    width = 2 * half
    slots = blocks.shape[0]
    out_shape = [jax.ShapeDtypeStruct((count, 2, directions, half), F32)]
    out_specs = [VMEM]
    source = blocks if first else parts
    scratch = [
        pltpu.SMEM((slots + 1,), jnp.int32),
        pltpu.VMEM((particles, 4 * directions, 2 * width), BF16),
        pltpu.VMEM((BUFFERS,) + source.shape[1:], source.dtype),
        pltpu.SemaphoreType.DMA((BUFFERS,)),
    ]
    operands = [*index, side, own_half, other_half, source]
    in_specs = [SMEM] * 5 + [VMEM, VMEM, HBM]
    aliases = {}
    if first:
        out_shape.append(jax.ShapeDtypeStruct((slots, 2, 2, width, half), BF16))
        out_specs.append(HBM)
        scratch.append(pltpu.VMEM((2, 2, 2, width, half), BF16))
        scratch.append(pltpu.SemaphoreType.DMA((2,)))
        if parts is not None:
            aliases = {len(operands): 1}
            operands.append(parts)
            in_specs.append(HBM)
    return pl.pallas_call(
        functools.partial(backward_kernel, first, groups, base),
        out_shape=out_shape,
        in_specs=in_specs,
        out_specs=out_specs,
        scratch_shapes=scratch,
        input_output_aliases=aliases,
        compiler_params=pltpu.CompilerParams(vmem_limit_bytes=STREAM_LIMIT),
        cost_estimate=pl.CostEstimate(
            flops=directions * width * half,
            bytes_accessed=size_of(own_half),
            transcendentals=0,
        ),
        name="backward_group" + str(groups[0]),
    )(*operands)


def forward_kernel(groups, copies, count, rows_ref, live_ref, place_ref, group_ref, *refs):
    field_refs = refs[:count]
    parts_ref = refs[count]
    out_ref, list_ref, every_ref, acc_ref, buf_ref, sems = refs[-6:]
    directions = out_ref.shape[2]
    wanted = chosen_slots(group_ref, live_ref[0], groups, list_ref)

    def fetch(turn, place):
        return pltpu.make_async_copy(
            parts_ref.at[list_ref[turn]], buf_ref.at[place], sems.at[place]
        )

    for early in range(BUFFERS):

        @pl.when(early < wanted)
        def _():
            fetch(early, early).start()

    acc_ref[...] = jnp.zeros_like(acc_ref)
    for number, row, place in copies:
        every_ref[place] = field_refs[number][row]

    def body(turn, carry):
        here = lax.rem(turn, BUFFERS)
        slot = list_ref[turn]
        holder = rows_ref[slot]
        place = place_ref[slot]
        with_real, with_imag = stacked_parts(every_ref[place, 0], every_ref[place, 1])
        fetch(turn, here).wait()
        total = dot_nt(with_real, buf_ref[here, 0, 0]) + dot_nt(with_imag, buf_ref[here, 0, 1])
        rest = dot_nt(with_real[: 2 * directions], buf_ref[here, 1, 0])
        rest += dot_nt(with_imag[: 2 * directions], buf_ref[here, 1, 1])
        acc_ref[holder] += total[: 2 * directions] + total[2 * directions :] + rest

        @pl.when(turn + BUFFERS < wanted)
        def _():
            fetch(turn + BUFFERS, here).start()

        return carry

    lax.fori_loop(0, wanted, body, 0)
    for row in range(acc_ref.shape[0]):
        out_ref[row, 0] = acc_ref[row, :directions]
        out_ref[row, 1] = acc_ref[row, directions:]


def forward(groups, index, fields, copies, parts, particles, total_rows, after):
    slots, _, _, width, half = parts.shape
    directions = fields[0].shape[2]
    out_shape = jax.ShapeDtypeStruct((particles, 2, directions, width), F32)
    return pl.pallas_call(
        functools.partial(forward_kernel, groups, copies, len(fields)),
        out_shape=out_shape,
        in_specs=[SMEM] * 4 + [VMEM] * len(fields) + [HBM] + [ANY] * len(after),
        out_specs=VMEM,
        scratch_shapes=[
            pltpu.SMEM((slots + 1,), jnp.int32),
            pltpu.VMEM((total_rows, 2, directions, half), F32),
            pltpu.VMEM((particles, 2 * directions, width), F32),
            pltpu.VMEM((BUFFERS,) + parts.shape[1:], BF16),
            pltpu.SemaphoreType.DMA((BUFFERS,)),
        ],
        compiler_params=pltpu.CompilerParams(vmem_limit_bytes=STREAM_LIMIT),
        cost_estimate=pl.CostEstimate(
            flops=directions * width * half,
            bytes_accessed=size_of(out_shape),
            transcendentals=0,
        ),
        name="forward_group" + str(groups[0]),
    )(*index, *fields, parts, *after)


def pack_kernel(plans, count, *refs):
    in_refs, out_refs = refs[:count], refs[-len(plans) :]
    for out_ref, plan in zip(out_refs, plans):
        for row, terms in enumerate(plan):
            value = in_refs[terms[0][0]][terms[0][1]]
            for number, source in terms[1:]:
                value = value + in_refs[number][source]
            out_ref[row] = value


def pack(name, inputs, plans, after=()):
    shapes = [jax.ShapeDtypeStruct((len(plan),) + inputs[0].shape[1:], F32) for plan in plans]
    return pl.pallas_call(
        functools.partial(pack_kernel, plans, len(inputs)),
        out_shape=shapes,
        in_specs=[VMEM] * len(inputs) + [ANY] * len(after),
        out_specs=[VMEM] * len(plans),
        compiler_params=params(size_of(*inputs), size_of(*shapes)),
        name=name,
    )(*inputs, *after)


def total_kernel(counts, side_ref, incident_ref, *refs):
    nears, halves, out_ref = refs[: counts[0]], refs[counts[0] : -1], refs[-1]
    particles, half = incident_ref.shape[0], incident_ref.shape[3]
    start = pl.multiple_of(side_ref[0] * half, half)
    near = nears[0][...]
    for ref in nears[1:]:
        near = near + ref[...]
    out_ref[...] = near
    for particle in range(particles):
        value = incident_ref[particle]
        for ref, step in zip(halves, counts[1]):
            value = value + ref[particle * step]
        window = (particle, slice(None), slice(None), pl.ds(start, half))
        out_ref[window] = out_ref[window] + value


def whole_total(side, incident, nears, halves):
    arrays = [value for value, _ in halves]
    steps = tuple(step for _, step in halves)
    return pl.pallas_call(
        functools.partial(total_kernel, (len(nears), steps)),
        out_shape=jax.ShapeDtypeStruct(nears[0].shape, F32),
        in_specs=[SMEM] + [VMEM] * (1 + len(nears) + len(arrays)),
        out_specs=VMEM,
        compiler_params=params(size_of(*nears, nears[0], incident, *arrays)),
        name="total",
    )(side, incident, *nears, *arrays)


def from_other(value):
    return lax.ppermute(value, "pair", [(0, 1), (1, 0)])


def across(value, bit):
    count = lax.axis_size("owner")
    return lax.ppermute(value, "owner", [(source, source ^ bit) for source in range(count)])


def along(value, shift):
    count = lax.axis_size("owner")
    step = shift * COLUMNS
    return lax.ppermute(
        value, "owner", [(source, (source + step) % count) for source in range(count)]
    )


def scatter_step(incident, scattered, blocks, parts, index, side, layers):
    particles = incident.shape[0]
    every = range(particles)
    by_x = range((particles + 1) // 2)
    by_y = range((particles + 1) // 2, particles)
    rest = range(1, layers)
    at = functools.partial(place_of, particles=particles, layers=layers)
    total_rows = COLUMNS * particles * layers
    first_n, first_d = at(1, 0, 0), at(3, 0, 0)
    first = parts is None

    def row_of(particle, layer):
        return particle * layers + layer

    other = from_other(scattered)
    x1 = across(scattered, 1)
    y1 = across(scattered, 2)
    fetched = (side, scattered, other, blocks)
    products_d, *made = backward(
        first, (2, 4), first_d, total_rows - first_d, index, *fetched, parts
    )
    if first:
        parts = made[0]

    inputs = [products_d, x1, y1]
    x_plan = [[(0, row_of(particle, layer))] for particle in by_x for layer in range(layers)]
    y_plan = [[(0, row_of(particle, layer))] for particle in by_y for layer in range(layers)]
    x_head, y_head = len(x_plan), len(y_plan)
    x_plan += [[(2, particle)] for particle in by_y]
    y_plan += [[(1, particle)] for particle in by_x]
    x2, y2 = pack("pack_second", inputs, [x_plan, y_plan])
    x2, y2 = across(x2, 1), across(y2, 2)
    products_n, *made = backward(first, (1, 3), first_n, first_d - first_n, index, *fetched, parts)
    if first:
        parts = made[0]

    inputs = [products_n, x2, y2, scattered]
    x_plan, y_plan = [], []
    for particle in every:
        for layer in range(layers):
            x_terms = [(0, at(1, particle, layer) - first_n)]
            y_terms = [(0, at(2, particle, layer) - first_n)]
            if particle in by_x:
                y_terms.append((1, row_of(particle, layer)))
            else:
                x_terms.append((2, row_of(particle - len(by_x), layer)))
            x_plan.append(x_terms)
            y_plan.append(y_terms)
    x3, y3, copied = pack(
        "pack_third", inputs, [x_plan, y_plan, [[(3, particle)] for particle in every]]
    )
    x3, y3 = across(x3, 1), across(y3, 2)
    z3 = [along(copied, -shift) for shift in rest]
    products_o, *made = backward(
        first, (0,), 0, first_n, index, side, copied, other, blocks, parts
    )
    if first:
        parts = made[0]

    inputs = [products_o, x3, y3] + z3
    tails = [[(2 + shift, particle)] for particle in every for shift in rest]
    z_plans = [
        [
            [(number, row_of(particle, shift)) for number in range(3)]
            for particle in every
        ]
        for shift in rest
    ]
    x4, y4, mark, *z4 = pack("pack_fourth", inputs, [tails, tails, [[(1, 0)]]] + z_plans)
    x4, y4 = across(x4, 1), across(y4, 2)
    z4 = [along(value, shift) for shift, value in zip(rest, z4)]
    copies = []
    for particle in every:
        copies.append((0, particle, at(1, particle, 0)))
        copies.append((1, particle, at(2, particle, 0)))
        if particle in by_x:
            copies.append((3, y_head + particle, at(3, particle, 0)))
        else:
            copies.append((2, x_head + particle - len(by_x), at(3, particle, 0)))
        for shift in rest:
            copies.append((3 + shift, particle, at(0, particle, shift)))
    near_first = forward(
        (0, 1, 2), index, [x1, y1, x2, y2] + z3, tuple(copies), parts, particles, total_rows, [mark]
    )

    def tail(particle, shift):
        return particle * len(rest) + shift - 1

    x5, y5, mark = pack(
        "pack_fifth",
        [x4, y4],
        [
            [[(1, tail(particle, shift))] for particle in by_y for shift in rest],
            [[(0, tail(particle, shift))] for particle in by_x for shift in rest],
            [[(0, 0)]],
        ],
        [near_first],
    )
    x5, y5 = across(x5, 1), across(y5, 2)
    copies = []
    for particle in every:
        for shift in rest:
            copies.append((0, tail(particle, shift), at(1, particle, shift)))
            copies.append((1, tail(particle, shift), at(2, particle, shift)))
    near_second = forward(
        (3,), index, [x4, y4], tuple(copies), parts, particles, total_rows, [mark]
    )
    copies = []
    for number, group in ((0, by_y), (1, by_x)):
        for order, particle in enumerate(group):
            for shift in rest:
                copies.append((number, tail(order, shift), at(3, particle, shift)))
    near_last = forward(
        (4,), index, [x5, y5], tuple(copies), parts, particles, total_rows, [near_second]
    )
    halves = [(products_o, layers), (x3, layers), (y3, layers)] + [(value, 1) for value in z4]
    return whole_total(side, incident, [near_first, near_second, near_last], halves), parts


def local(incident, tmat, blocks, block_rows, partners, live, owner_of):
    slots = blocks.shape[0]
    layers = lax.axis_size("owner") // COLUMNS
    my_owner = lax.axis_index("owner").astype(jnp.int32)[None]
    side = lax.axis_index("pair").astype(jnp.int32)[None]
    theirs = from_other(incident)
    tmat_parts, place, group = prepare(my_owner, partners, owner_of, tmat, slots, layers)
    index = (block_rows, live, place, group)
    (scattered,) = apply_tmat(True, False, side, incident, theirs, tmat_parts)
    parts = None
    for turn in range(ITERS):
        mine, parts = scatter_step(incident, scattered, blocks, parts, index, side, layers)
        theirs = from_other(mine)
        last = turn == ITERS - 1
        *exciting, scattered = apply_tmat(False, last, side, mine, theirs, tmat_parts)
    return (scattered, exciting[0])


def solution(mesh):
    in_specs = (
        P("owner", None, None, "pair"),
        P("owner", None, "pair", None),
        P("owner", None, None, "pair"),
        P("owner"),
        P(),
        P("owner"),
        P(),
    )
    out_specs = (P("owner", None, None, "pair"), P("owner", None, None, "pair"))
    return jax.shard_map(local, mesh=mesh, in_specs=in_specs, out_specs=out_specs, check_vma=False)
```

```python
import functools

import jax
import jax.numpy as jnp
from jax import lax
from jax.experimental import pallas as pl
from jax.experimental.pallas import tpu as pltpu
from jax.sharding import PartitionSpec as P

ITERS = 2
COLUMNS = 4
BUFFERS = 4
F32 = jnp.float32
BF16 = jnp.bfloat16
MIB = 1 << 20
STREAM_LIMIT = 48 * MIB
ALONE_LIMIT = 63 * MIB
GROUPS = 5
VMEM = pl.BlockSpec(memory_space=pltpu.VMEM)
SMEM = pl.BlockSpec(memory_space=pltpu.SMEM)
ANY = pl.BlockSpec(memory_space=pl.ANY)
HBM = pl.BlockSpec(memory_space=pltpu.MemorySpace.HBM)


def split_value(value):
    high = value.astype(BF16)
    low = (value - high.astype(F32)).astype(BF16)
    return high, low


def stacked_parts(real, imag):
    real_high, real_low = split_value(real)
    imag_high, imag_low = split_value(imag)
    with_real = jnp.concatenate((real_high, imag_high, real_low, imag_low), axis=0)
    with_imag = jnp.concatenate((-imag_high, real_high, -imag_low, real_low), axis=0)
    return with_real, with_imag


def dot_nt(left, right):
    return lax.dot_general(left, right, (((1,), (1,)), ((), ())), preferred_element_type=F32)


def dot_nn(left, right):
    return jnp.dot(left, right, preferred_element_type=F32)


def params(*byte_counts):
    return pltpu.CompilerParams(vmem_limit_bytes=sum(byte_counts) + 6 * MIB)


def size_of(*arrays):
    return sum(value.size * value.dtype.itemsize for value in arrays)


def place_of(column, particle, layer, particles, layers):
    return (column * particles + particle) * layers + layer


def prepare_kernel(
    layers, slots, owner_ref, side_ref, partners_ref, rows_of_ref, holders_ref, live_ref, tmat_ref, *refs
):
    parts_ref, index_ref, buf_ref, sems = refs
    particles, _, half, width = tmat_ref.shape
    stride, counts = GROUPS * slots, 3 * GROUPS * slots

    def fetch(row):
        return pltpu.make_async_copy(tmat_ref.at[row], buf_ref.at[row], sems.at[row])

    for row in range(particles):
        fetch(row).start()
    me = owner_ref[0]
    my_column, my_layer = lax.rem(me, COLUMNS), lax.div(me, COLUMNS)
    for group in range(GROUPS):
        index_ref[counts + group] = 0
    index_ref[counts + GROUPS] = side_ref[0]

    def step(slot, carry):
        row = rows_of_ref[partners_ref[me * slots + slot]]
        owner, particle = lax.div(row, particles), lax.rem(row, particles)
        column = lax.bitwise_xor(lax.rem(owner, COLUMNS), my_column)
        layer = lax.rem(lax.div(owner, COLUMNS) - my_layer + layers, layers)
        near = jnp.where(column == COLUMNS - 1, 2, 1)
        far = jnp.where(column == COLUMNS - 1, 4, 3)
        group = jnp.where(column == 0, 0, jnp.where(layer == 0, near, far))
        found = index_ref[counts + group]
        index_ref[counts + group] = found + 1
        position = group * slots + found
        index_ref[position] = slot
        index_ref[stride + position] = place_of(column, particle, layer, particles, layers)
        index_ref[2 * stride + position] = holders_ref[slot]
        return carry

    lax.fori_loop(0, live_ref[0], step, 0)
    for row in range(particles):
        fetch(row).wait()
        for part in range(2):
            high, low = split_value(buf_ref[row, part])
            parts_ref[row, :, part * width : (part + 1) * width] = high
            parts_ref[row, :, (2 + part) * width : (3 + part) * width] = low


def prepare(my_owner, side, partners, owner_of, block_rows, live, tmat, layers):
    particles, _, half, width = tmat.shape
    slots = block_rows.shape[0]
    return pl.pallas_call(
        functools.partial(prepare_kernel, layers, slots),
        out_shape=(
            jax.ShapeDtypeStruct((particles, half, 4 * width), BF16),
            jax.ShapeDtypeStruct((3 * GROUPS * slots + GROUPS + 1,), jnp.int32),
        ),
        in_specs=[SMEM] * 6 + [HBM],
        out_specs=(VMEM, SMEM),
        scratch_shapes=[pltpu.VMEM(tmat.shape, F32), pltpu.SemaphoreType.DMA((particles,))],
        compiler_params=pltpu.CompilerParams(vmem_limit_bytes=ALONE_LIMIT),
        name="prepare",
    )(my_owner, side, partners, owner_of, block_rows, live, tmat)


def tmat_kernel(halves, side_ref, mine_ref, theirs_ref, parts_ref, *refs):
    exciting_ref = refs[0] if len(refs) == 3 else None
    scattered_ref, full_ref = refs[-2:]
    particles, _, directions, width = full_ref.shape
    half = width // 2
    start = pl.multiple_of(side_ref[0] * half, half)
    if halves:
        full_ref[:, :, :, pl.ds(start, half)] = mine_ref[...]
        full_ref[:, :, :, pl.ds(pl.multiple_of(half - start, half), half)] = theirs_ref[...]
    else:
        full_ref[...] = mine_ref[...] + theirs_ref[...]
    for row in range(particles):
        with_real, with_imag = stacked_parts(full_ref[row, 0], full_ref[row, 1])
        right = jnp.concatenate((with_real, with_imag, with_real, with_imag), axis=1)
        total = dot_nt(parts_ref[row], right)
        out = (total[:, : 2 * directions] + total[:, 2 * directions :]).T
        scattered_ref[row, 0] = out[:directions]
        scattered_ref[row, 1] = out[directions:]
    if exciting_ref is not None:
        exciting_ref[...] = full_ref[:, :, :, pl.ds(start, half)]


def apply_tmat(halves, last, side, mine, theirs, parts):
    particles, _, directions, _ = mine.shape
    half = parts.shape[1]
    half_shape = jax.ShapeDtypeStruct((particles, 2, directions, half), F32)
    count = 2 if last else 1
    return pl.pallas_call(
        functools.partial(tmat_kernel, halves),
        out_shape=[half_shape] * count,
        in_specs=[SMEM, VMEM, VMEM, VMEM],
        out_specs=[VMEM] * count,
        scratch_shapes=[pltpu.VMEM((particles, 2, directions, 2 * half), F32)],
        compiler_params=(
            pltpu.CompilerParams(vmem_limit_bytes=ALONE_LIMIT - size_of(parts, theirs))
            if halves
            else params(3 * size_of(mine, theirs), size_of(parts))
        ),
        name="tmat_apply",
    )(side, mine, theirs, parts)


def chosen_slots(index_ref, groups, slots):
    stride, counts = GROUPS * slots, 3 * GROUPS * slots
    starts, total = [], 0
    for group in groups:
        starts.append(total)
        total = total + index_ref[counts + group]

    def at_turn(turn):
        position = groups[0] * slots + turn
        for group, start in zip(groups[1:], starts[1:]):
            position = jnp.where(turn >= start, group * slots + turn - start, position)
        return [index_ref[number * stride + position] for number in range(3)]

    return total, at_turn


def backward_kernel(first, groups, base, index_ref, own_ref, other_ref, blocks_ref, *refs):
    if first:
        out_ref, parts_ref, left_ref, buf_ref, sems, made_ref, made_sems = refs[-7:]
    else:
        out_ref, left_ref, buf_ref, sems = refs
    directions, half = own_ref.shape[2], own_ref.shape[3]
    width = 2 * half
    slots = blocks_ref.shape[0]
    wanted, at_turn = chosen_slots(index_ref, groups, slots)
    own_side = index_ref[3 * GROUPS * slots + GROUPS]

    def fetch(turn, place):
        return pltpu.make_async_copy(
            blocks_ref.at[at_turn(turn)[0]], buf_ref.at[place], sems.at[place]
        )

    def keep(turn, place):
        return pltpu.make_async_copy(
            made_ref.at[place], parts_ref.at[at_turn(turn)[0]], made_sems.at[place]
        )

    for early in range(BUFFERS):

        @pl.when(early < wanted)
        def _():
            fetch(early, early).start()

    for field_ref, side in ((own_ref, own_side), (other_ref, 1 - own_side)):
        for row in range(field_ref.shape[0]):
            with_real, with_imag = stacked_parts(field_ref[row, 0], field_ref[row, 1])
            for part, value in enumerate((with_real, with_imag)):
                start = pl.multiple_of(part * width + side * half, half)
                left_ref[row, :, pl.ds(start, half)] = value
    out_ref[...] = jnp.zeros_like(out_ref)

    def body(turn, carry):
        here = lax.rem(turn, BUFFERS)
        fetch(turn, here).wait()
        _, place, holder = at_turn(turn)
        place = place - base
        if first:
            spot = lax.rem(turn, 2)

            @pl.when(turn >= 2)
            def _():
                keep(turn - 2, spot).wait()

            high, low = split_value(buf_ref[here].reshape(2 * width, half))
            made_ref[spot, 0] = high.reshape(2, width, half)
            made_ref[spot, 1] = low.reshape(2, width, half)
            keep(turn, spot).start()
        else:
            high = buf_ref[here, 0].reshape(2 * width, half)
            low = buf_ref[here, 1].reshape(2 * width, half)
        total = dot_nn(left_ref[holder], high)
        rest = dot_nn(left_ref[holder, : 2 * directions], low)
        out = total[: 2 * directions] + total[2 * directions :] + rest
        out_ref[place, 0] = out[:directions]
        out_ref[place, 1] = out[directions:]

        @pl.when(turn + BUFFERS < wanted)
        def _():
            fetch(turn + BUFFERS, here).start()

        return carry

    lax.fori_loop(0, wanted, body, 0)
    if first:

        @pl.when(wanted >= 2)
        def _():
            keep(wanted - 2, lax.rem(wanted, 2)).wait()

        @pl.when(wanted >= 1)
        def _():
            keep(wanted - 1, lax.rem(wanted - 1, 2)).wait()


def backward(first, groups, base, count, index, own_half, other_half, blocks, parts):
    particles, _, directions, half = own_half.shape
    width = 2 * half
    slots = blocks.shape[0]
    out_shape = [jax.ShapeDtypeStruct((count, 2, directions, half), F32)]
    out_specs = [VMEM]
    source = blocks if first else parts
    scratch = [
        pltpu.VMEM((particles, 4 * directions, 2 * width), BF16),
        pltpu.VMEM((BUFFERS,) + source.shape[1:], source.dtype),
        pltpu.SemaphoreType.DMA((BUFFERS,)),
    ]
    operands = [index, own_half, other_half, source]
    in_specs = [SMEM, VMEM, VMEM, HBM]
    aliases = {}
    if first:
        out_shape.append(jax.ShapeDtypeStruct((slots, 2, 2, width, half), BF16))
        out_specs.append(HBM)
        scratch.append(pltpu.VMEM((2, 2, 2, width, half), BF16))
        scratch.append(pltpu.SemaphoreType.DMA((2,)))
        if parts is not None:
            aliases = {len(operands): 1}
            operands.append(parts)
            in_specs.append(HBM)
    return pl.pallas_call(
        functools.partial(backward_kernel, first, groups, base),
        out_shape=out_shape,
        in_specs=in_specs,
        out_specs=out_specs,
        scratch_shapes=scratch,
        input_output_aliases=aliases,
        compiler_params=pltpu.CompilerParams(vmem_limit_bytes=STREAM_LIMIT),
        cost_estimate=pl.CostEstimate(
            flops=directions * width * half,
            bytes_accessed=size_of(own_half),
            transcendentals=0,
        ),
        name="backward_group" + str(groups[0]),
    )(*operands)


def forward_kernel(groups, copies, count, index_ref, *refs):
    field_refs = refs[:count]
    parts_ref = refs[count]
    out_ref, every_ref, acc_ref, buf_ref, sems = refs[-5:]
    directions = out_ref.shape[2]
    wanted, at_turn = chosen_slots(index_ref, groups, parts_ref.shape[0])

    def fetch(turn, place):
        return pltpu.make_async_copy(
            parts_ref.at[at_turn(turn)[0]], buf_ref.at[place], sems.at[place]
        )

    for early in range(BUFFERS):

        @pl.when(early < wanted)
        def _():
            fetch(early, early).start()

    acc_ref[...] = jnp.zeros_like(acc_ref)
    for number, row, place in copies:
        every_ref[place] = field_refs[number][row]

    def body(turn, carry):
        here = lax.rem(turn, BUFFERS)
        _, place, holder = at_turn(turn)
        with_real, with_imag = stacked_parts(every_ref[place, 0], every_ref[place, 1])
        fetch(turn, here).wait()
        total = dot_nt(with_real, buf_ref[here, 0, 0]) + dot_nt(with_imag, buf_ref[here, 0, 1])
        rest = dot_nt(with_real[: 2 * directions], buf_ref[here, 1, 0])
        rest += dot_nt(with_imag[: 2 * directions], buf_ref[here, 1, 1])
        acc_ref[holder] += total[: 2 * directions] + total[2 * directions :] + rest

        @pl.when(turn + BUFFERS < wanted)
        def _():
            fetch(turn + BUFFERS, here).start()

        return carry

    lax.fori_loop(0, wanted, body, 0)
    for row in range(acc_ref.shape[0]):
        out_ref[row, 0] = acc_ref[row, :directions]
        out_ref[row, 1] = acc_ref[row, directions:]


def forward(groups, index, fields, copies, parts, particles, total_rows, after):
    slots, _, _, width, half = parts.shape
    directions = fields[0].shape[2]
    out_shape = jax.ShapeDtypeStruct((particles, 2, directions, width), F32)
    return pl.pallas_call(
        functools.partial(forward_kernel, groups, copies, len(fields)),
        out_shape=out_shape,
        in_specs=[SMEM] + [VMEM] * len(fields) + [HBM] + [ANY] * len(after),
        out_specs=VMEM,
        scratch_shapes=[
                pltpu.VMEM((total_rows, 2, directions, half), F32),
            pltpu.VMEM((particles, 2 * directions, width), F32),
            pltpu.VMEM((BUFFERS,) + parts.shape[1:], BF16),
            pltpu.SemaphoreType.DMA((BUFFERS,)),
        ],
        compiler_params=pltpu.CompilerParams(vmem_limit_bytes=STREAM_LIMIT),
        cost_estimate=pl.CostEstimate(
            flops=directions * width * half,
            bytes_accessed=size_of(out_shape),
            transcendentals=0,
        ),
        name="forward_group" + str(groups[0]),
    )(index, *fields, parts, *after)


def pack_kernel(plans, count, *refs):
    in_refs, out_refs = refs[:count], refs[-len(plans) :]
    for out_ref, plan in zip(out_refs, plans):
        for row, terms in enumerate(plan):
            value = in_refs[terms[0][0]][terms[0][1]]
            for number, source in terms[1:]:
                value = value + in_refs[number][source]
            out_ref[row] = value


def pack(name, inputs, plans, after=()):
    shapes = [jax.ShapeDtypeStruct((len(plan),) + inputs[0].shape[1:], F32) for plan in plans]
    return pl.pallas_call(
        functools.partial(pack_kernel, plans, len(inputs)),
        out_shape=shapes,
        in_specs=[VMEM] * len(inputs) + [ANY] * len(after),
        out_specs=[VMEM] * len(plans),
        compiler_params=params(size_of(*inputs), size_of(*shapes)),
        name=name,
    )(*inputs, *after)


def total_kernel(counts, side_ref, incident_ref, *refs):
    nears, halves, out_ref = refs[: counts[0]], refs[counts[0] : -1], refs[-1]
    particles, half = incident_ref.shape[0], incident_ref.shape[3]
    start = pl.multiple_of(side_ref[0] * half, half)
    near = nears[0][...]
    for ref in nears[1:]:
        near = near + ref[...]
    out_ref[...] = near
    for particle in range(particles):
        value = incident_ref[particle]
        for ref, step in zip(halves, counts[1]):
            value = value + ref[particle * step]
        window = (particle, slice(None), slice(None), pl.ds(start, half))
        out_ref[window] = out_ref[window] + value


def whole_total(side, incident, nears, halves):
    arrays = [value for value, _ in halves]
    steps = tuple(step for _, step in halves)
    return pl.pallas_call(
        functools.partial(total_kernel, (len(nears), steps)),
        out_shape=jax.ShapeDtypeStruct(nears[0].shape, F32),
        in_specs=[SMEM] + [VMEM] * (1 + len(nears) + len(arrays)),
        out_specs=VMEM,
        compiler_params=params(size_of(*nears, nears[0], incident, *arrays)),
        name="total",
    )(side, incident, *nears, *arrays)


def from_other(value):
    return lax.ppermute(value, "pair", [(0, 1), (1, 0)])


def across(value, bit):
    count = lax.axis_size("owner")
    return lax.ppermute(value, "owner", [(source, source ^ bit) for source in range(count)])


def along(value, shift):
    count = lax.axis_size("owner")
    step = shift * COLUMNS
    return lax.ppermute(
        value, "owner", [(source, (source + step) % count) for source in range(count)]
    )


def scatter_step(incident, scattered, blocks, parts, index, side, layers):
    particles = incident.shape[0]
    every = range(particles)
    by_x = range((particles + 1) // 2)
    by_y = range((particles + 1) // 2, particles)
    rest = range(1, layers)
    at = functools.partial(place_of, particles=particles, layers=layers)
    total_rows = COLUMNS * particles * layers
    first_n, first_d = at(1, 0, 0), at(3, 0, 0)
    first = parts is None

    def row_of(particle, layer):
        return particle * layers + layer

    other = from_other(scattered)
    x1 = across(scattered, 1)
    y1 = across(scattered, 2)
    fetched = (scattered, other, blocks)
    products_d, *made = backward(
        first, (2, 4), first_d, total_rows - first_d, index, *fetched, parts
    )
    if first:
        parts = made[0]

    inputs = [products_d, x1, y1]
    x_plan = [[(0, row_of(particle, layer))] for particle in by_x for layer in range(layers)]
    y_plan = [[(0, row_of(particle, layer))] for particle in by_y for layer in range(layers)]
    x_head, y_head = len(x_plan), len(y_plan)
    x_plan += [[(2, particle)] for particle in by_y]
    y_plan += [[(1, particle)] for particle in by_x]
    x2, y2 = pack("pack_second", inputs, [x_plan, y_plan])
    x2, y2 = across(x2, 1), across(y2, 2)
    products_n, *made = backward(first, (1, 3), first_n, first_d - first_n, index, *fetched, parts)
    if first:
        parts = made[0]

    inputs = [products_n, x2, y2, scattered]
    x_plan, y_plan = [], []
    for particle in every:
        for layer in range(layers):
            x_terms = [(0, at(1, particle, layer) - first_n)]
            y_terms = [(0, at(2, particle, layer) - first_n)]
            if particle in by_x:
                y_terms.append((1, row_of(particle, layer)))
            else:
                x_terms.append((2, row_of(particle - len(by_x), layer)))
            x_plan.append(x_terms)
            y_plan.append(y_terms)
    x3, y3, copied = pack(
        "pack_third", inputs, [x_plan, y_plan, [[(3, particle)] for particle in every]]
    )
    x3, y3 = across(x3, 1), across(y3, 2)
    z3 = [along(copied, -shift) for shift in rest]
    products_o, *made = backward(
        first, (0,), 0, first_n, index, copied, other, blocks, parts
    )
    if first:
        parts = made[0]

    inputs = [products_o, x3, y3] + z3
    tails = [[(2 + shift, particle)] for particle in every for shift in rest]
    z_plans = [
        [
            [(number, row_of(particle, shift)) for number in range(3)]
            for particle in every
        ]
        for shift in rest
    ]
    x4, y4, mark, *z4 = pack("pack_fourth", inputs, [tails, tails, [[(1, 0)]]] + z_plans)
    x4, y4 = across(x4, 1), across(y4, 2)
    z4 = [along(value, shift) for shift, value in zip(rest, z4)]
    copies = []
    for particle in every:
        copies.append((0, particle, at(1, particle, 0)))
        copies.append((1, particle, at(2, particle, 0)))
        if particle in by_x:
            copies.append((3, y_head + particle, at(3, particle, 0)))
        else:
            copies.append((2, x_head + particle - len(by_x), at(3, particle, 0)))
        for shift in rest:
            copies.append((3 + shift, particle, at(0, particle, shift)))
    near_first = forward(
        (0, 1, 2), index, [x1, y1, x2, y2] + z3, tuple(copies), parts, particles, total_rows, [mark]
    )

    def tail(particle, shift):
        return particle * len(rest) + shift - 1

    x5, y5, mark = pack(
        "pack_fifth",
        [x4, y4],
        [
            [[(1, tail(particle, shift))] for particle in by_y for shift in rest],
            [[(0, tail(particle, shift))] for particle in by_x for shift in rest],
            [[(0, 0)]],
        ],
        [near_first, z4[len(z4) // 2]],
    )
    x5, y5 = across(x5, 1), across(y5, 2)
    copies = []
    for particle in every:
        for shift in rest:
            copies.append((0, tail(particle, shift), at(1, particle, shift)))
            copies.append((1, tail(particle, shift), at(2, particle, shift)))
    near_second = forward(
        (3,), index, [x4, y4], tuple(copies), parts, particles, total_rows, [mark]
    )
    copies = []
    for number, group in ((0, by_y), (1, by_x)):
        for order, particle in enumerate(group):
            for shift in rest:
                copies.append((number, tail(order, shift), at(3, particle, shift)))
    near_last = forward(
        (4,), index, [x5, y5], tuple(copies), parts, particles, total_rows, [near_second]
    )
    halves = [(products_o, layers), (x3, layers), (y3, layers)] + [(value, 1) for value in z4]
    return whole_total(side, incident, [near_first, near_second, near_last], halves), parts


def local(incident, tmat, blocks, block_rows, partners, live, owner_of):
    layers = lax.axis_size("owner") // COLUMNS
    my_owner = lax.axis_index("owner").astype(jnp.int32)[None]
    side = lax.axis_index("pair").astype(jnp.int32)[None]
    theirs = from_other(incident)
    tmat_parts, index = prepare(
        my_owner, side, partners, owner_of, block_rows, live, tmat, layers
    )
    (scattered,) = apply_tmat(True, False, side, incident, theirs, tmat_parts)
    parts = None
    for turn in range(ITERS):
        mine, parts = scatter_step(incident, scattered, blocks, parts, index, side, layers)
        theirs = from_other(mine)
        last = turn == ITERS - 1
        *exciting, scattered = apply_tmat(False, last, side, mine, theirs, tmat_parts)
    return (scattered, exciting[0])


def solution(mesh):
    in_specs = (
        P("owner", None, None, "pair"),
        P("owner", None, "pair", None),
        P("owner", None, None, "pair"),
        P("owner"),
        P(),
        P("owner"),
        P(),
    )
    out_specs = (P("owner", None, None, "pair"), P("owner", None, None, "pair"))
    return jax.shard_map(local, mesh=mesh, in_specs=in_specs, out_specs=out_specs, check_vma=False)
```

```python
import functools

import jax
import jax.numpy as jnp
from jax import lax
from jax.experimental import pallas as pl
from jax.experimental.pallas import tpu as pltpu
from jax.sharding import PartitionSpec as P

ITERS = 2
COLUMNS = 4
BUFFERS = 4
F32 = jnp.float32
BF16 = jnp.bfloat16
MIB = 1 << 20
STREAM_LIMIT = 48 * MIB
ALONE_LIMIT = 61 * MIB
GROUPS = 5
VMEM = pl.BlockSpec(memory_space=pltpu.VMEM)
SMEM = pl.BlockSpec(memory_space=pltpu.SMEM)
ANY = pl.BlockSpec(memory_space=pl.ANY)
HBM = pl.BlockSpec(memory_space=pltpu.MemorySpace.HBM)


def split_value(value):
    high = value.astype(BF16)
    low = (value - high.astype(F32)).astype(BF16)
    return high, low


def stacked_parts(real, imag):
    real_high, real_low = split_value(real)
    imag_high, imag_low = split_value(imag)
    with_real = jnp.concatenate((real_high, imag_high, real_low, imag_low), axis=0)
    with_imag = jnp.concatenate((-imag_high, real_high, -imag_low, real_low), axis=0)
    return with_real, with_imag


def dot_nt(left, right):
    return lax.dot_general(left, right, (((1,), (1,)), ((), ())), preferred_element_type=F32)


def dot_nn(left, right):
    return jnp.dot(left, right, preferred_element_type=F32)


def params(*byte_counts):
    return pltpu.CompilerParams(vmem_limit_bytes=sum(byte_counts) + 6 * MIB)


def size_of(*arrays):
    return sum(value.size * value.dtype.itemsize for value in arrays)


def place_of(column, particle, layer, particles, layers):
    return (column * particles + particle) * layers + layer


def prepare_kernel(
    layers, slots, owner_ref, side_ref, partners_ref, rows_of_ref, holders_ref, live_ref, tmat_ref, *refs
):
    parts_ref, index_ref, buf_ref, sems = refs
    particles, _, half, width = tmat_ref.shape
    stride, counts = GROUPS * slots, 3 * GROUPS * slots

    def fetch(row):
        return pltpu.make_async_copy(tmat_ref.at[row], buf_ref.at[row], sems.at[row])

    for row in range(particles):
        fetch(row).start()
    me = owner_ref[0]
    my_column, my_layer = lax.rem(me, COLUMNS), lax.div(me, COLUMNS)
    for group in range(GROUPS):
        index_ref[counts + group] = 0
    index_ref[counts + GROUPS] = side_ref[0]

    def step(slot, carry):
        row = rows_of_ref[partners_ref[me * slots + slot]]
        owner, particle = lax.div(row, particles), lax.rem(row, particles)
        column = lax.bitwise_xor(lax.rem(owner, COLUMNS), my_column)
        layer = lax.bitwise_xor(lax.div(owner, COLUMNS), my_layer)
        near = jnp.where(column == COLUMNS - 1, 2, 1)
        far = jnp.where(column == COLUMNS - 1, 4, 3)
        group = jnp.where(column == 0, 0, jnp.where(layer == 0, near, far))
        found = index_ref[counts + group]
        index_ref[counts + group] = found + 1
        position = group * slots + found
        index_ref[position] = slot
        index_ref[stride + position] = place_of(column, particle, layer, particles, layers)
        index_ref[2 * stride + position] = holders_ref[slot]
        return carry

    lax.fori_loop(0, live_ref[0], step, 0)
    for row in range(particles):
        fetch(row).wait()
        for part in range(2):
            high, low = split_value(buf_ref[row, part])
            parts_ref[row, :, part * width : (part + 1) * width] = high
            parts_ref[row, :, (2 + part) * width : (3 + part) * width] = low


def prepare(my_owner, side, partners, owner_of, block_rows, live, tmat, layers):
    particles, _, half, width = tmat.shape
    slots = block_rows.shape[0]
    return pl.pallas_call(
        functools.partial(prepare_kernel, layers, slots),
        out_shape=(
            jax.ShapeDtypeStruct((particles, half, 4 * width), BF16),
            jax.ShapeDtypeStruct((3 * GROUPS * slots + GROUPS + 1,), jnp.int32),
        ),
        in_specs=[SMEM] * 6 + [HBM],
        out_specs=(VMEM, SMEM),
        scratch_shapes=[pltpu.VMEM(tmat.shape, F32), pltpu.SemaphoreType.DMA((particles,))],
        compiler_params=pltpu.CompilerParams(vmem_limit_bytes=ALONE_LIMIT),
        name="prepare",
    )(my_owner, side, partners, owner_of, block_rows, live, tmat)


def tmat_kernel(halves, side_ref, mine_ref, theirs_ref, parts_ref, *refs):
    exciting_ref = refs[0] if len(refs) == 3 else None
    scattered_ref, full_ref = refs[-2:]
    particles, _, directions, width = full_ref.shape
    half = width // 2
    start = pl.multiple_of(side_ref[0] * half, half)
    if halves:
        full_ref[:, :, :, pl.ds(start, half)] = mine_ref[...]
        full_ref[:, :, :, pl.ds(pl.multiple_of(half - start, half), half)] = theirs_ref[...]
    else:
        full_ref[...] = mine_ref[...] + theirs_ref[...]
    for row in range(particles):
        with_real, with_imag = stacked_parts(full_ref[row, 0], full_ref[row, 1])
        right = jnp.concatenate((with_real, with_imag, with_real, with_imag), axis=1)
        total = dot_nt(parts_ref[row], right)
        out = (total[:, : 2 * directions] + total[:, 2 * directions :]).T
        scattered_ref[row, 0] = out[:directions]
        scattered_ref[row, 1] = out[directions:]
    if exciting_ref is not None:
        exciting_ref[...] = full_ref[:, :, :, pl.ds(start, half)]


def apply_tmat(halves, last, side, mine, theirs, parts):
    particles, _, directions, _ = mine.shape
    half = parts.shape[1]
    half_shape = jax.ShapeDtypeStruct((particles, 2, directions, half), F32)
    count = 2 if last else 1
    return pl.pallas_call(
        functools.partial(tmat_kernel, halves),
        out_shape=[half_shape] * count,
        in_specs=[SMEM, VMEM, VMEM, VMEM],
        out_specs=[VMEM] * count,
        scratch_shapes=[pltpu.VMEM((particles, 2, directions, 2 * half), F32)],
        compiler_params=params(3 * size_of(mine, theirs), size_of(parts)),
        name="tmat_apply",
    )(side, mine, theirs, parts)


def chosen_slots(index_ref, groups, slots):
    stride, counts = GROUPS * slots, 3 * GROUPS * slots
    starts, total = [], 0
    for group in groups:
        starts.append(total)
        total = total + index_ref[counts + group]

    def at_turn(turn):
        position = groups[0] * slots + turn
        for group, start in zip(groups[1:], starts[1:]):
            position = jnp.where(turn >= start, group * slots + turn - start, position)
        return [index_ref[number * stride + position] for number in range(3)]

    return total, at_turn


def backward_kernel(first, groups, base, index_ref, own_ref, other_ref, blocks_ref, *refs):
    if first:
        out_ref, parts_ref, left_ref, buf_ref, sems, made_ref, made_sems = refs[-7:]
    else:
        out_ref, left_ref, buf_ref, sems = refs
    directions, half = own_ref.shape[2], own_ref.shape[3]
    width = 2 * half
    slots = blocks_ref.shape[0]
    wanted, at_turn = chosen_slots(index_ref, groups, slots)
    own_side = index_ref[3 * GROUPS * slots + GROUPS]

    def fetch(turn, place):
        return pltpu.make_async_copy(
            blocks_ref.at[at_turn(turn)[0]], buf_ref.at[place], sems.at[place]
        )

    def keep(turn, place):
        return pltpu.make_async_copy(
            made_ref.at[place], parts_ref.at[at_turn(turn)[0]], made_sems.at[place]
        )

    for early in range(BUFFERS):

        @pl.when(early < wanted)
        def _():
            fetch(early, early).start()

    for field_ref, side in ((own_ref, own_side), (other_ref, 1 - own_side)):
        for row in range(other_ref.shape[0]):
            with_real, with_imag = stacked_parts(field_ref[row, 0], field_ref[row, 1])
            for part, value in enumerate((with_real, with_imag)):
                start = pl.multiple_of(part * width + side * half, half)
                left_ref[row, :, pl.ds(start, half)] = value
    out_ref[...] = jnp.zeros_like(out_ref)

    def body(turn, carry):
        here = lax.rem(turn, BUFFERS)
        fetch(turn, here).wait()
        _, place, holder = at_turn(turn)
        place = place - base
        if first:
            spot = lax.rem(turn, 2)

            @pl.when(turn >= 2)
            def _():
                keep(turn - 2, spot).wait()

            high, low = split_value(buf_ref[here].reshape(2 * width, half))
            made_ref[spot, 0] = high.reshape(2, width, half)
            made_ref[spot, 1] = low.reshape(2, width, half)
            keep(turn, spot).start()
        else:
            high = buf_ref[here, 0].reshape(2 * width, half)
            low = buf_ref[here, 1].reshape(2 * width, half)
        total = dot_nn(left_ref[holder], high)
        rest = dot_nn(left_ref[holder, : 2 * directions], low)
        out = total[: 2 * directions] + total[2 * directions :] + rest
        out_ref[place, 0] = out[:directions]
        out_ref[place, 1] = out[directions:]

        @pl.when(turn + BUFFERS < wanted)
        def _():
            fetch(turn + BUFFERS, here).start()

        return carry

    lax.fori_loop(0, wanted, body, 0)
    if first:

        @pl.when(wanted >= 2)
        def _():
            keep(wanted - 2, lax.rem(wanted, 2)).wait()

        @pl.when(wanted >= 1)
        def _():
            keep(wanted - 1, lax.rem(wanted - 1, 2)).wait()


def backward(first, groups, base, count, index, own_half, other_half, blocks, parts):
    particles, _, directions, half = other_half.shape
    width = 2 * half
    slots = blocks.shape[0]
    out_shape = [jax.ShapeDtypeStruct((count, 2, directions, half), F32)]
    out_specs = [VMEM]
    source = blocks if first else parts
    scratch = [
        pltpu.VMEM((particles, 4 * directions, 2 * width), BF16),
        pltpu.VMEM((BUFFERS,) + source.shape[1:], source.dtype),
        pltpu.SemaphoreType.DMA((BUFFERS,)),
    ]
    operands = [index, own_half, other_half, source]
    in_specs = [SMEM, VMEM, VMEM, HBM]
    aliases = {}
    if first:
        out_shape.append(jax.ShapeDtypeStruct((slots, 2, 2, width, half), BF16))
        out_specs.append(HBM)
        scratch.append(pltpu.VMEM((2, 2, 2, width, half), BF16))
        scratch.append(pltpu.SemaphoreType.DMA((2,)))
        if parts is not None:
            aliases = {len(operands): 1}
            operands.append(parts)
            in_specs.append(HBM)
    return pl.pallas_call(
        functools.partial(backward_kernel, first, groups, base),
        out_shape=out_shape,
        in_specs=in_specs,
        out_specs=out_specs,
        scratch_shapes=scratch,
        input_output_aliases=aliases,
        compiler_params=pltpu.CompilerParams(vmem_limit_bytes=STREAM_LIMIT),
        cost_estimate=pl.CostEstimate(
            flops=directions * width * half,
            bytes_accessed=size_of(own_half),
            transcendentals=0,
        ),
        name="backward_group" + str(groups[0]),
    )(*operands)


def forward_kernel(groups, copies, count, index_ref, *refs):
    field_refs = refs[:count]
    parts_ref = refs[count]
    out_ref, every_ref, acc_ref, buf_ref, sems = refs[-5:]
    directions = out_ref.shape[2]
    wanted, at_turn = chosen_slots(index_ref, groups, parts_ref.shape[0])

    def fetch(turn, place):
        return pltpu.make_async_copy(
            parts_ref.at[at_turn(turn)[0]], buf_ref.at[place], sems.at[place]
        )

    for early in range(BUFFERS):

        @pl.when(early < wanted)
        def _():
            fetch(early, early).start()

    acc_ref[...] = jnp.zeros_like(acc_ref)
    for number, row, place in copies:
        every_ref[place] = field_refs[number][row]

    def body(turn, carry):
        here = lax.rem(turn, BUFFERS)
        _, place, holder = at_turn(turn)
        with_real, with_imag = stacked_parts(every_ref[place, 0], every_ref[place, 1])
        fetch(turn, here).wait()
        total = dot_nt(with_real, buf_ref[here, 0, 0]) + dot_nt(with_imag, buf_ref[here, 0, 1])
        rest = dot_nt(with_real[: 2 * directions], buf_ref[here, 1, 0])
        rest += dot_nt(with_imag[: 2 * directions], buf_ref[here, 1, 1])
        acc_ref[holder] += total[: 2 * directions] + total[2 * directions :] + rest

        @pl.when(turn + BUFFERS < wanted)
        def _():
            fetch(turn + BUFFERS, here).start()

        return carry

    lax.fori_loop(0, wanted, body, 0)
    for row in range(acc_ref.shape[0]):
        out_ref[row, 0] = acc_ref[row, :directions]
        out_ref[row, 1] = acc_ref[row, directions:]


def forward(groups, index, fields, copies, parts, particles, total_rows, after):
    slots, _, _, width, half = parts.shape
    directions = fields[0].shape[2]
    out_shape = jax.ShapeDtypeStruct((particles, 2, directions, width), F32)
    return pl.pallas_call(
        functools.partial(forward_kernel, groups, copies, len(fields)),
        out_shape=out_shape,
        in_specs=[SMEM] + [VMEM] * len(fields) + [HBM] + [ANY] * len(after),
        out_specs=VMEM,
        scratch_shapes=[
                pltpu.VMEM((total_rows, 2, directions, half), F32),
            pltpu.VMEM((particles, 2 * directions, width), F32),
            pltpu.VMEM((BUFFERS,) + parts.shape[1:], BF16),
            pltpu.SemaphoreType.DMA((BUFFERS,)),
        ],
        compiler_params=pltpu.CompilerParams(vmem_limit_bytes=STREAM_LIMIT),
        cost_estimate=pl.CostEstimate(
            flops=directions * width * half,
            bytes_accessed=size_of(out_shape),
            transcendentals=0,
        ),
        name="forward_group" + str(groups[0]),
    )(index, *fields, parts, *after)


def pack_kernel(plans, count, *refs):
    in_refs, out_refs = refs[:count], refs[-len(plans) :]
    for out_ref, plan in zip(out_refs, plans):
        for row, terms in enumerate(plan):
            value = in_refs[terms[0][0]][terms[0][1]]
            for number, source in terms[1:]:
                value = value + in_refs[number][source]
            out_ref[row] = value


def pack(name, inputs, plans, after=()):
    shapes = [jax.ShapeDtypeStruct((len(plan),) + inputs[0].shape[1:], F32) for plan in plans]
    return pl.pallas_call(
        functools.partial(pack_kernel, plans, len(inputs)),
        out_shape=shapes,
        in_specs=[VMEM] * len(inputs) + [ANY] * len(after),
        out_specs=[VMEM] * len(plans),
        compiler_params=params(size_of(*inputs), size_of(*shapes)),
        name=name,
    )(*inputs, *after)


def total_kernel(counts, side_ref, incident_ref, *refs):
    nears, halves, out_ref = refs[: counts[0]], refs[counts[0] : -1], refs[-1]
    particles, half = incident_ref.shape[0], incident_ref.shape[3]
    start = pl.multiple_of(side_ref[0] * half, half)
    near = nears[0][...]
    for ref in nears[1:]:
        near = near + ref[...]
    out_ref[...] = near
    for particle in range(particles):
        value = incident_ref[particle]
        for ref, step in zip(halves, counts[1]):
            value = value + ref[particle * step]
        window = (particle, slice(None), slice(None), pl.ds(start, half))
        out_ref[window] = out_ref[window] + value


def whole_total(side, incident, nears, halves):
    arrays = [value for value, _ in halves]
    steps = tuple(step for _, step in halves)
    return pl.pallas_call(
        functools.partial(total_kernel, (len(nears), steps)),
        out_shape=jax.ShapeDtypeStruct(nears[0].shape, F32),
        in_specs=[SMEM] + [VMEM] * (1 + len(nears) + len(arrays)),
        out_specs=VMEM,
        compiler_params=params(size_of(*nears, nears[0], incident, *arrays)),
        name="total",
    )(side, incident, *nears, *arrays)


def from_other(value):
    return lax.ppermute(value, "pair", [(0, 1), (1, 0)])


def across(value, bit):
    count = lax.axis_size("owner")
    return lax.ppermute(value, "owner", [(source, source ^ bit) for source in range(count)])


def scatter_step(incident, scattered, blocks, parts, index, side, layers):
    particles = incident.shape[0]
    every = range(particles)
    by_x = range((particles + 1) // 2)
    by_y = range((particles + 1) // 2, particles)
    rest = range(1, layers)
    powers = [1 << step for step in range(layers.bit_length() - 1)]
    at = functools.partial(place_of, particles=particles, layers=layers)
    total_rows = COLUMNS * particles * layers
    first_n, first_d = at(1, 0, 0), at(3, 0, 0)
    first = parts is None

    def row_of(particle, layer):
        return particle * layers + layer

    other = from_other(scattered)
    x1 = across(scattered, 1)
    y1 = across(scattered, 2)
    fetched = (scattered, other, blocks)
    products_d, *made = backward(
        first, (2, 4), first_d, total_rows - first_d, index, *fetched, parts
    )
    if first:
        parts = made[0]

    inputs = [products_d, x1, y1, scattered]
    x_plan = [[(0, row_of(particle, layer))] for particle in by_x for layer in range(layers)]
    y_plan = [[(0, row_of(particle, layer))] for particle in by_y for layer in range(layers)]
    x_head, y_head = len(x_plan), len(y_plan)
    x_plan += [[(2, particle)] for particle in by_y]
    y_plan += [[(1, particle)] for particle in by_x]
    x2, y2, copied = pack(
        "pack_second", inputs, [x_plan, y_plan, [[(3, particle)] for particle in every]]
    )
    x2, y2 = across(x2, 1), across(y2, 2)
    reached = [across(copied, COLUMNS)]
    products_n, *made = backward(first, (1, 3), first_n, first_d - first_n, index, *fetched, parts)
    if first:
        parts = made[0]

    def z_row(particle, layer):
        step = layer.bit_length() - 1
        return step, (layer - (1 << step)) * particles + particle

    def z_rows(offset, own, count):
        rows = []
        for layer in range(count):
            for particle in every:
                if layer == 0:
                    rows.append([(own, particle)])
                else:
                    step, row = z_row(particle, layer)
                    rows.append([(offset + step, row)])
        return rows

    inputs = [products_n, x2, y2, scattered] + reached
    x_plan, y_plan = [], []
    for particle in every:
        for layer in range(layers):
            x_terms = [(0, at(1, particle, layer) - first_n)]
            y_terms = [(0, at(2, particle, layer) - first_n)]
            if particle in by_x:
                y_terms.append((1, row_of(particle, layer)))
            else:
                x_terms.append((2, row_of(particle - len(by_x), layer)))
            x_plan.append(x_terms)
            y_plan.append(y_terms)
    x3, y3, known = pack("pack_third", inputs, [x_plan, y_plan, z_rows(4, 3, 2)])
    x3, y3 = across(x3, 1), across(y3, 2)
    for bit in powers[1:]:
        if bit > 2:
            (known,) = pack("pack_layers", [scattered] + reached, [z_rows(1, 0, bit)])
        reached.append(across(known, bit * COLUMNS))
    products_o, *made = backward(first, (0,), 0, first_n, index, known, other, blocks, parts)
    if first:
        parts = made[0]
    copies = []
    for particle in every:
        copies.append((0, particle, at(1, particle, 0)))
        copies.append((1, particle, at(2, particle, 0)))
        if particle in by_x:
            copies.append((3, y_head + particle, at(3, particle, 0)))
        else:
            copies.append((2, x_head + particle - len(by_x), at(3, particle, 0)))
    near_level = forward(
        (1, 2), index, [x1, y1, x2, y2], tuple(copies), parts, particles, total_rows, [known]
    )

    def summed(layer, particle, arrived):
        terms = [(number, row_of(particle, layer)) for number in range(3)]
        return terms + [(number, layer * particles + particle) for number in arrived]

    def half_sums(bit, arrived):
        return [summed(layer, particle, arrived) for layer in range(bit, 2 * bit) for particle in every]

    inputs = [products_o, x3, y3] + reached
    tails = []
    for particle in every:
        for layer in rest:
            step, row = z_row(particle, layer)
            tails.append([(3 + step, row)])
    x4, y4, sums, mark = pack(
        "pack_fourth",
        inputs,
        [tails, tails, half_sums(powers[-1], ()), [[(1, 0)]]],
        [near_level],
    )
    x4, y4 = across(x4, 1), across(y4, 2)
    arrived = [across(sums, powers[-1] * COLUMNS)]
    copies = []
    for particle in every:
        for layer in rest:
            step, row = z_row(particle, layer)
            copies.append((step, row, at(0, particle, layer)))
    near_column = forward(
        (0,), index, reached, tuple(copies), parts, particles, total_rows, [mark]
    )

    def tail(particle, layer):
        return particle * len(rest) + layer - 1

    x5, y5, mark = pack(
        "pack_fifth",
        [x4, y4],
        [
            [[(1, tail(particle, layer))] for particle in by_y for layer in rest],
            [[(0, tail(particle, layer))] for particle in by_x for layer in rest],
            [[(0, 0)]],
        ],
        [near_column],
    )
    x5, y5 = across(x5, 1), across(y5, 2)
    for bit in powers[-2::-1]:
        numbers = range(3, 3 + len(arrived))
        (sums,) = pack(
            "pack_sums", [products_o, x3, y3] + arrived, [half_sums(bit, numbers)], [mark]
        )
        arrived.append(across(sums, bit * COLUMNS))
    copies = []
    for particle in every:
        for layer in rest:
            copies.append((0, tail(particle, layer), at(1, particle, layer)))
            copies.append((1, tail(particle, layer), at(2, particle, layer)))
    near_second = forward(
        (3,), index, [x4, y4], tuple(copies), parts, particles, total_rows, [mark, sums]
    )
    copies = []
    for number, group in ((0, by_y), (1, by_x)):
        for order, particle in enumerate(group):
            for layer in rest:
                copies.append((number, tail(order, layer), at(3, particle, layer)))
    near_last = forward(
        (4,), index, [x5, y5], tuple(copies), parts, particles, total_rows, [near_second]
    )
    nears = [near_level, near_column, near_second, near_last]
    halves = [(products_o, layers), (x3, layers), (y3, layers)] + [(value, 1) for value in arrived]
    return whole_total(side, incident, nears, halves), parts


def local(incident, tmat, blocks, block_rows, partners, live, owner_of):
    layers = lax.axis_size("owner") // COLUMNS
    my_owner = lax.axis_index("owner").astype(jnp.int32)[None]
    side = lax.axis_index("pair").astype(jnp.int32)[None]
    theirs = from_other(incident)
    tmat_parts, index = prepare(
        my_owner, side, partners, owner_of, block_rows, live, tmat, layers
    )
    (scattered,) = apply_tmat(True, False, side, incident, theirs, tmat_parts)
    parts = None
    for turn in range(ITERS):
        mine, parts = scatter_step(incident, scattered, blocks, parts, index, side, layers)
        theirs = from_other(mine)
        last = turn == ITERS - 1
        *exciting, scattered = apply_tmat(False, last, side, mine, theirs, tmat_parts)
    return (scattered, exciting[0])


def solution(mesh):
    in_specs = (
        P("owner", None, None, "pair"),
        P("owner", None, "pair", None),
        P("owner", None, None, "pair"),
        P("owner"),
        P(),
        P("owner"),
        P(),
    )
    out_specs = (P("owner", None, None, "pair"), P("owner", None, None, "pair"))
    return jax.shard_map(local, mesh=mesh, in_specs=in_specs, out_specs=out_specs, check_vma=False)
```

```python
import functools

import jax
import jax.numpy as jnp
from jax import lax
from jax.experimental import pallas as pl
from jax.experimental.pallas import tpu as pltpu
from jax.sharding import PartitionSpec as P

ITERS = 2
COLUMNS = 4
BUFFERS = 4
F32 = jnp.float32
BF16 = jnp.bfloat16
MIB = 1 << 20
STREAM_LIMIT = 48 * MIB
ALONE_LIMIT = 119 * MIB // 2
GROUPS = 5
VMEM = pl.BlockSpec(memory_space=pltpu.VMEM)
SMEM = pl.BlockSpec(memory_space=pltpu.SMEM)
ANY = pl.BlockSpec(memory_space=pl.ANY)
HBM = pl.BlockSpec(memory_space=pltpu.MemorySpace.HBM)


def split_value(value):
    high = value.astype(BF16)
    low = (value - high.astype(F32)).astype(BF16)
    return high, low


def stacked_parts(real, imag):
    real_high, real_low = split_value(real)
    imag_high, imag_low = split_value(imag)
    with_real = jnp.concatenate((real_high, imag_high, real_low, imag_low), axis=0)
    with_imag = jnp.concatenate((-imag_high, real_high, -imag_low, real_low), axis=0)
    return with_real, with_imag


def dot_nt(left, right):
    return lax.dot_general(left, right, (((1,), (1,)), ((), ())), preferred_element_type=F32)


def dot_nn(left, right):
    return jnp.dot(left, right, preferred_element_type=F32)


def params(*byte_counts):
    return pltpu.CompilerParams(vmem_limit_bytes=sum(byte_counts) + 6 * MIB)


def size_of(*arrays):
    return sum(value.size * value.dtype.itemsize for value in arrays)


def place_of(column, particle, layer, particles, layers):
    return (column * particles + particle) * layers + layer


def index_kernel(
    layers, particles, owner_ref, side_ref, partners_ref, rows_of_ref, holders_ref, live_ref, *refs
):
    index_ref = refs[-1]
    slots = holders_ref.shape[0]
    stride, counts = GROUPS * slots, 3 * GROUPS * slots
    me = owner_ref[0]
    my_column, my_layer = lax.rem(me, COLUMNS), lax.div(me, COLUMNS)
    for group in range(GROUPS):
        index_ref[counts + group] = 0
    index_ref[counts + GROUPS] = side_ref[0]

    def step(slot, carry):
        row = rows_of_ref[partners_ref[me * slots + slot]]
        owner, particle = lax.div(row, particles), lax.rem(row, particles)
        column = lax.bitwise_xor(lax.rem(owner, COLUMNS), my_column)
        layer = lax.bitwise_xor(lax.div(owner, COLUMNS), my_layer)
        near = jnp.where(column == COLUMNS - 1, 2, 1)
        far = jnp.where(column == COLUMNS - 1, 4, 3)
        group = jnp.where(column == 0, 0, jnp.where(layer == 0, near, far))
        found = index_ref[counts + group]
        index_ref[counts + group] = found + 1
        position = group * slots + found
        index_ref[position] = slot
        index_ref[stride + position] = place_of(column, particle, layer, particles, layers)
        index_ref[2 * stride + position] = holders_ref[slot]
        return carry

    lax.fori_loop(0, live_ref[0], step, 0)


def slot_index(my_owner, side, partners, owner_of, block_rows, live, layers, particles, after):
    slots = block_rows.shape[0]
    return pl.pallas_call(
        functools.partial(index_kernel, layers, particles),
        out_shape=jax.ShapeDtypeStruct((3 * GROUPS * slots + GROUPS + 1,), jnp.int32),
        in_specs=[SMEM] * 6 + [ANY],
        out_specs=SMEM,
        name="slot_index",
    )(my_owner, side, partners, owner_of, block_rows, live, after)


def prepare_kernel(tmat_ref, incident_ref, parts_ref, copy_ref, buf_ref, sems):
    particles, _, half, width = tmat_ref.shape

    def fetch(row):
        return pltpu.make_async_copy(tmat_ref.at[row], buf_ref.at[row], sems.at[row])

    for row in range(particles):
        fetch(row).start()
    own = pltpu.make_async_copy(incident_ref, copy_ref, sems.at[particles])
    own.start()
    for row in range(particles):
        fetch(row).wait()
        for part in range(2):
            high, low = split_value(buf_ref[row, part])
            parts_ref[row, :, part * width : (part + 1) * width] = high
            parts_ref[row, :, (2 + part) * width : (3 + part) * width] = low
    own.wait()


def prepare(tmat, incident):
    particles, _, half, width = tmat.shape
    return pl.pallas_call(
        prepare_kernel,
        out_shape=(
            jax.ShapeDtypeStruct((particles, half, 4 * width), BF16),
            jax.ShapeDtypeStruct(incident.shape, F32),
        ),
        in_specs=[HBM, HBM],
        out_specs=(VMEM, VMEM),
        scratch_shapes=[pltpu.VMEM(tmat.shape, F32), pltpu.SemaphoreType.DMA((particles + 1,))],
        compiler_params=pltpu.CompilerParams(vmem_limit_bytes=ALONE_LIMIT),
        name="prepare",
    )(tmat, incident)


def tmat_kernel(halves, side_ref, mine_ref, theirs_ref, parts_ref, *refs):
    last = len(refs) == 4
    exciting_ref = refs[0] if last else None
    scattered_ref, full_ref = refs[1:3] if last else refs
    particles, _, directions, width = full_ref.shape
    half = width // 2
    start = pl.multiple_of(side_ref[0] * half, half)
    if halves:
        full_ref[:, :, :, pl.ds(start, half)] = mine_ref[...]
        full_ref[:, :, :, pl.ds(pl.multiple_of(half - start, half), half)] = theirs_ref[...]
    else:
        full_ref[...] = mine_ref[...] + theirs_ref[...]
    if last:
        window = full_ref.at[:, :, :, pl.ds(start, half)]
        leave = pltpu.make_async_copy(window, exciting_ref, refs[3])
        leave.start()
    for row in range(particles):
        with_real, with_imag = stacked_parts(full_ref[row, 0], full_ref[row, 1])
        right = jnp.concatenate((with_real, with_imag, with_real, with_imag), axis=1)
        total = dot_nt(parts_ref[row], right)
        out = (total[:, : 2 * directions] + total[:, 2 * directions :]).T
        scattered_ref[row, 0] = out[:directions]
        scattered_ref[row, 1] = out[directions:]
    if last:
        leave.wait()


def apply_tmat(halves, last, side, mine, theirs, parts):
    particles, _, directions, _ = mine.shape
    half = parts.shape[1]
    half_shape = jax.ShapeDtypeStruct((particles, 2, directions, half), F32)
    scratch = [pltpu.VMEM((particles, 2, directions, 2 * half), F32)]
    if last:
        scratch.append(pltpu.SemaphoreType.DMA)
    return pl.pallas_call(
        functools.partial(tmat_kernel, halves),
        out_shape=[half_shape] * (2 if last else 1),
        in_specs=[SMEM, VMEM, VMEM, VMEM],
        out_specs=[HBM, VMEM] if last else [VMEM],
        scratch_shapes=scratch,
        compiler_params=params(3 * size_of(mine, theirs), size_of(parts)),
        name="tmat_apply",
    )(side, mine, theirs, parts)


def chosen_slots(index_ref, groups, slots):
    stride, counts = GROUPS * slots, 3 * GROUPS * slots
    starts, total = [], 0
    for group in groups:
        starts.append(total)
        total = total + index_ref[counts + group]

    def at_turn(turn):
        position = groups[0] * slots + turn
        for group, start in zip(groups[1:], starts[1:]):
            position = jnp.where(turn >= start, group * slots + turn - start, position)
        return [index_ref[number * stride + position] for number in range(3)]

    return total, at_turn


def backward_kernel(first, groups, base, index_ref, own_ref, other_ref, blocks_ref, *refs):
    if first:
        out_ref, parts_ref, left_ref, buf_ref, sems, made_ref, made_sems = refs[-7:]
    else:
        out_ref, left_ref, buf_ref, sems = refs
    directions, half = own_ref.shape[2], own_ref.shape[3]
    width = 2 * half
    slots = blocks_ref.shape[0]
    wanted, at_turn = chosen_slots(index_ref, groups, slots)
    own_side = index_ref[3 * GROUPS * slots + GROUPS]

    def fetch(turn, place):
        return pltpu.make_async_copy(
            blocks_ref.at[at_turn(turn)[0]], buf_ref.at[place], sems.at[place]
        )

    def keep(turn, place):
        return pltpu.make_async_copy(
            made_ref.at[place], parts_ref.at[at_turn(turn)[0]], made_sems.at[place]
        )

    for early in range(BUFFERS):

        @pl.when(early < wanted)
        def _():
            fetch(early, early).start()

    for field_ref, side in ((own_ref, own_side), (other_ref, 1 - own_side)):
        for row in range(other_ref.shape[0]):
            with_real, with_imag = stacked_parts(field_ref[row, 0], field_ref[row, 1])
            for part, value in enumerate((with_real, with_imag)):
                start = pl.multiple_of(part * width + side * half, half)
                left_ref[row, :, pl.ds(start, half)] = value
    out_ref[...] = jnp.zeros_like(out_ref)

    def body(turn, carry):
        here = lax.rem(turn, BUFFERS)
        fetch(turn, here).wait()
        _, place, holder = at_turn(turn)
        place = place - base
        if first:
            spot = lax.rem(turn, 2)

            @pl.when(turn >= 2)
            def _():
                keep(turn - 2, spot).wait()

            high, low = split_value(buf_ref[here].reshape(2 * width, half))
            made_ref[spot, 0] = high.reshape(2, width, half)
            made_ref[spot, 1] = low.reshape(2, width, half)
            keep(turn, spot).start()
        else:
            high = buf_ref[here, 0].reshape(2 * width, half)
            low = buf_ref[here, 1].reshape(2 * width, half)
        total = dot_nn(left_ref[holder], high)
        rest = dot_nn(left_ref[holder, : 2 * directions], low)
        out = total[: 2 * directions] + total[2 * directions :] + rest
        out_ref[place, 0] = out[:directions]
        out_ref[place, 1] = out[directions:]

        @pl.when(turn + BUFFERS < wanted)
        def _():
            fetch(turn + BUFFERS, here).start()

        return carry

    lax.fori_loop(0, wanted, body, 0)
    if first:

        @pl.when(wanted >= 2)
        def _():
            keep(wanted - 2, lax.rem(wanted, 2)).wait()

        @pl.when(wanted >= 1)
        def _():
            keep(wanted - 1, lax.rem(wanted - 1, 2)).wait()


def backward(first, groups, base, count, index, own_half, other_half, blocks, parts):
    particles, _, directions, half = other_half.shape
    width = 2 * half
    slots = blocks.shape[0]
    out_shape = [jax.ShapeDtypeStruct((count, 2, directions, half), F32)]
    out_specs = [VMEM]
    source = blocks if first else parts
    scratch = [
        pltpu.VMEM((particles, 4 * directions, 2 * width), BF16),
        pltpu.VMEM((BUFFERS,) + source.shape[1:], source.dtype),
        pltpu.SemaphoreType.DMA((BUFFERS,)),
    ]
    operands = [index, own_half, other_half, source]
    in_specs = [SMEM, VMEM, VMEM, HBM]
    aliases = {}
    if first:
        out_shape.append(jax.ShapeDtypeStruct((slots, 2, 2, width, half), BF16))
        out_specs.append(HBM)
        scratch.append(pltpu.VMEM((2, 2, 2, width, half), BF16))
        scratch.append(pltpu.SemaphoreType.DMA((2,)))
        if parts is not None:
            aliases = {len(operands): 1}
            operands.append(parts)
            in_specs.append(HBM)
    return pl.pallas_call(
        functools.partial(backward_kernel, first, groups, base),
        out_shape=out_shape,
        in_specs=in_specs,
        out_specs=out_specs,
        scratch_shapes=scratch,
        input_output_aliases=aliases,
        compiler_params=pltpu.CompilerParams(vmem_limit_bytes=STREAM_LIMIT),
        cost_estimate=pl.CostEstimate(
            flops=directions * width * half,
            bytes_accessed=size_of(own_half),
            transcendentals=0,
        ),
        name="backward_group" + str(groups[0]),
    )(*operands)


def forward_kernel(groups, copies, count, index_ref, *refs):
    field_refs = refs[:count]
    parts_ref = refs[count]
    out_ref, every_ref, acc_ref, buf_ref, sems = refs[-5:]
    directions = out_ref.shape[2]
    wanted, at_turn = chosen_slots(index_ref, groups, parts_ref.shape[0])

    def fetch(turn, place):
        return pltpu.make_async_copy(
            parts_ref.at[at_turn(turn)[0]], buf_ref.at[place], sems.at[place]
        )

    for early in range(BUFFERS):

        @pl.when(early < wanted)
        def _():
            fetch(early, early).start()

    acc_ref[...] = jnp.zeros_like(acc_ref)
    for number, row, place in copies:
        every_ref[place] = field_refs[number][row]

    def body(turn, carry):
        here = lax.rem(turn, BUFFERS)
        _, place, holder = at_turn(turn)
        with_real, with_imag = stacked_parts(every_ref[place, 0], every_ref[place, 1])
        fetch(turn, here).wait()
        left = jnp.concatenate((with_real, with_imag), axis=1)
        high = jnp.concatenate((buf_ref[here, 0, 0], buf_ref[here, 0, 1]), axis=1)
        low = jnp.concatenate((buf_ref[here, 1, 0], buf_ref[here, 1, 1]), axis=1)
        total = dot_nt(left, high)
        rest = dot_nt(left[: 2 * directions], low)
        acc_ref[holder] += total[: 2 * directions] + total[2 * directions :] + rest

        @pl.when(turn + BUFFERS < wanted)
        def _():
            fetch(turn + BUFFERS, here).start()

        return carry

    lax.fori_loop(0, wanted, body, 0)
    for row in range(acc_ref.shape[0]):
        out_ref[row, 0] = acc_ref[row, :directions]
        out_ref[row, 1] = acc_ref[row, directions:]


def forward(groups, index, fields, copies, parts, particles, total_rows, after):
    slots, _, _, width, half = parts.shape
    directions = fields[0].shape[2]
    out_shape = jax.ShapeDtypeStruct((particles, 2, directions, width), F32)
    return pl.pallas_call(
        functools.partial(forward_kernel, groups, copies, len(fields)),
        out_shape=out_shape,
        in_specs=[SMEM] + [VMEM] * len(fields) + [HBM] + [ANY] * len(after),
        out_specs=VMEM,
        scratch_shapes=[
                pltpu.VMEM((total_rows, 2, directions, half), F32),
            pltpu.VMEM((particles, 2 * directions, width), F32),
            pltpu.VMEM((BUFFERS,) + parts.shape[1:], BF16),
            pltpu.SemaphoreType.DMA((BUFFERS,)),
        ],
        compiler_params=pltpu.CompilerParams(vmem_limit_bytes=STREAM_LIMIT),
        cost_estimate=pl.CostEstimate(
            flops=directions * width * half,
            bytes_accessed=size_of(out_shape),
            transcendentals=0,
        ),
        name="forward_group" + str(groups[0]),
    )(index, *fields, parts, *after)


def pack_kernel(plans, count, *refs):
    in_refs, out_refs = refs[:count], refs[-len(plans) :]
    for out_ref, plan in zip(out_refs, plans):
        for row, terms in enumerate(plan):
            value = in_refs[terms[0][0]][terms[0][1]]
            for number, source in terms[1:]:
                value = value + in_refs[number][source]
            out_ref[row] = value


def pack(name, inputs, plans, after=()):
    shapes = [jax.ShapeDtypeStruct((len(plan),) + inputs[0].shape[1:], F32) for plan in plans]
    return pl.pallas_call(
        functools.partial(pack_kernel, plans, len(inputs)),
        out_shape=shapes,
        in_specs=[VMEM] * len(inputs) + [ANY] * len(after),
        out_specs=[VMEM] * len(plans),
        compiler_params=params(size_of(*inputs), size_of(*shapes)),
        name=name,
    )(*inputs, *after)


def total_kernel(counts, side_ref, incident_ref, *refs):
    nears, halves, out_ref = refs[: counts[0]], refs[counts[0] : -1], refs[-1]
    particles, half = incident_ref.shape[0], incident_ref.shape[3]
    start = pl.multiple_of(side_ref[0] * half, half)
    near = nears[0][...]
    for ref in nears[1:]:
        near = near + ref[...]
    out_ref[...] = near
    for particle in range(particles):
        value = incident_ref[particle]
        for ref, step in zip(halves, counts[1]):
            value = value + ref[particle * step]
        window = (particle, slice(None), slice(None), pl.ds(start, half))
        out_ref[window] = out_ref[window] + value


def whole_total(side, incident, nears, halves):
    arrays = [value for value, _ in halves]
    steps = tuple(step for _, step in halves)
    return pl.pallas_call(
        functools.partial(total_kernel, (len(nears), steps)),
        out_shape=jax.ShapeDtypeStruct(nears[0].shape, F32),
        in_specs=[SMEM] + [VMEM] * (1 + len(nears) + len(arrays)),
        out_specs=VMEM,
        compiler_params=params(size_of(*nears, nears[0], incident, *arrays)),
        name="total",
    )(side, incident, *nears, *arrays)


def from_other(value):
    return lax.ppermute(value, "pair", [(0, 1), (1, 0)])


def across(value, bit):
    count = lax.axis_size("owner")
    return lax.ppermute(value, "owner", [(source, source ^ bit) for source in range(count)])


def scatter_step(incident, scattered, blocks, parts, index, side, layers):
    particles = incident.shape[0]
    every = range(particles)
    by_x = range((particles + 1) // 2)
    by_y = range((particles + 1) // 2, particles)
    rest = range(1, layers)
    powers = [1 << step for step in range(layers.bit_length() - 1)]
    at = functools.partial(place_of, particles=particles, layers=layers)
    total_rows = COLUMNS * particles * layers
    first_n, first_d = at(1, 0, 0), at(3, 0, 0)
    first = parts is None

    def row_of(particle, layer):
        return particle * layers + layer

    other = from_other(scattered)
    x1 = across(scattered, 1)
    y1 = across(scattered, 2)
    reached = [across(scattered, COLUMNS)]
    where = {1: (0, 0), 2: (1, 0), 3: (2, 0)}
    fetched = (scattered, other, blocks)
    products_d, *made = backward(
        first, (2, 4), first_d, total_rows - first_d, index, *fetched, parts
    )
    if first:
        parts = made[0]

    inputs = [products_d, x1, y1, scattered]
    x_plan = [[(0, row_of(particle, layer))] for particle in by_x for layer in range(layers)]
    y_plan = [[(0, row_of(particle, layer))] for particle in by_y for layer in range(layers)]
    x_head, y_head = len(x_plan), len(y_plan)
    x_plan += [[(2, particle)] for particle in by_y]
    y_plan += [[(1, particle)] for particle in by_x]
    x2, y2, copied = pack(
        "pack_second",
        inputs,
        [x_plan, y_plan, [[(3, particle)] for particle in every]],
        reached,
    )
    x2, y2 = across(x2, 1), across(y2, 2)
    reached.append(across(copied, 2 * COLUMNS))
    products_n, *made = backward(first, (1, 3), first_n, first_d - first_n, index, *fetched, parts)
    if first:
        parts = made[0]

    def z_row(particle, layer):
        number, start = where[layer]
        return number, start + particle

    inputs = [products_n, x2, y2, scattered, reached[0]]
    x_plan, y_plan = [], []
    for particle in every:
        for layer in range(layers):
            x_terms = [(0, at(1, particle, layer) - first_n)]
            y_terms = [(0, at(2, particle, layer) - first_n)]
            if particle in by_x:
                y_terms.append((1, row_of(particle, layer)))
            else:
                x_terms.append((2, row_of(particle - len(by_x), layer)))
            x_plan.append(x_terms)
            y_plan.append(y_terms)
    z_plans = [[[(number, particle)] for particle in every] for number in (3, 4)]
    x3, y3, copied, known = pack("pack_third", inputs, [x_plan, y_plan] + z_plans, reached[1:])
    x3, y3 = across(x3, 1), across(y3, 2)
    reached.append(across(known, 2 * COLUMNS))
    for bit in powers[2:]:
        plan = [[(0, particle)] for particle in every]
        for layer in range(1, bit):
            plan += [[(1 + where[layer][0], where[layer][1] + particle)] for particle in every]
        (known,) = pack("pack_layers", [scattered] + reached, [plan])
        for layer in range(bit):
            where[bit + layer] = (len(reached), layer * particles)
        reached.append(across(known, bit * COLUMNS))
    products_o, *made = backward(first, (0,), 0, first_n, index, copied, other, blocks, parts)
    if first:
        parts = made[0]
    copies = []
    for particle in every:
        copies.append((0, particle, at(1, particle, 0)))
        copies.append((1, particle, at(2, particle, 0)))
        if particle in by_x:
            copies.append((3, y_head + particle, at(3, particle, 0)))
        else:
            copies.append((2, x_head + particle - len(by_x), at(3, particle, 0)))
    near_level = forward(
        (1, 2),
        index,
        [x1, y1, x2, y2],
        tuple(copies),
        parts,
        particles,
        total_rows,
        [products_o],
    )

    def summed(layer, particle, arrived):
        terms = [(number, row_of(particle, layer)) for number in range(3)]
        return terms + [(number, layer * particles + particle) for number in arrived]

    def half_sums(bit, arrived):
        return [summed(layer, particle, arrived) for layer in range(bit, 2 * bit) for particle in every]

    inputs = [products_o, x3, y3] + reached
    tails = []
    for particle in every:
        for layer in rest:
            step, row = z_row(particle, layer)
            tails.append([(3 + step, row)])
    x4, y4, sums, mark = pack(
        "pack_fourth",
        inputs,
        [tails, tails, half_sums(powers[-1], ()), [[(1, 0)]]],
        [near_level],
    )
    x4, y4 = across(x4, 1), across(y4, 2)
    arrived = [across(sums, powers[-1] * COLUMNS)]
    copies = []
    for particle in every:
        for layer in rest:
            step, row = z_row(particle, layer)
            copies.append((step, row, at(0, particle, layer)))
    near_column = forward(
        (0,), index, reached, tuple(copies), parts, particles, total_rows, [mark]
    )

    def tail(particle, layer):
        return particle * len(rest) + layer - 1

    x5, y5, mark = pack(
        "pack_fifth",
        [x4, y4],
        [
            [[(1, tail(particle, layer))] for particle in by_y for layer in rest],
            [[(0, tail(particle, layer))] for particle in by_x for layer in rest],
            [[(0, 0)]],
        ],
        [near_column],
    )
    x5, y5 = across(x5, 1), across(y5, 2)
    for bit in powers[-2::-1]:
        numbers = range(3, 3 + len(arrived))
        (sums,) = pack(
            "pack_sums", [products_o, x3, y3] + arrived, [half_sums(bit, numbers)], [mark]
        )
        arrived.append(across(sums, bit * COLUMNS))
    copies = []
    for particle in every:
        for layer in rest:
            copies.append((0, tail(particle, layer), at(1, particle, layer)))
            copies.append((1, tail(particle, layer), at(2, particle, layer)))
    near_second = forward(
        (3,), index, [x4, y4], tuple(copies), parts, particles, total_rows, [mark, sums]
    )
    copies = []
    for number, group in ((0, by_y), (1, by_x)):
        for order, particle in enumerate(group):
            for layer in rest:
                copies.append((number, tail(order, layer), at(3, particle, layer)))
    near_last = forward(
        (4,), index, [x5, y5], tuple(copies), parts, particles, total_rows, [near_second]
    )
    nears = [near_level, near_column, near_second, near_last]
    halves = [(products_o, layers), (x3, layers), (y3, layers)] + [(value, 1) for value in arrived]
    return whole_total(side, incident, nears, halves), parts


def local(incident, tmat, blocks, block_rows, partners, live, owner_of):
    layers = lax.axis_size("owner") // COLUMNS
    my_owner = lax.axis_index("owner").astype(jnp.int32)[None]
    side = lax.axis_index("pair").astype(jnp.int32)[None]
    theirs = from_other(incident)
    tmat_parts, incident = prepare(tmat, incident)
    (scattered,) = apply_tmat(True, False, side, incident, theirs, tmat_parts)
    index = slot_index(
        my_owner, side, partners, owner_of, block_rows, live, layers, incident.shape[0], scattered
    )
    parts = None
    for turn in range(ITERS):
        mine, parts = scatter_step(incident, scattered, blocks, parts, index, side, layers)
        theirs = from_other(mine)
        last = turn == ITERS - 1
        *exciting, scattered = apply_tmat(False, last, side, mine, theirs, tmat_parts)
    return (scattered, exciting[0])


def solution(mesh):
    in_specs = (
        P("owner", None, None, "pair"),
        P("owner", None, "pair", None),
        P("owner", None, None, "pair"),
        P("owner"),
        P(),
        P("owner"),
        P(),
    )
    out_specs = (P("owner", None, None, "pair"), P("owner", None, None, "pair"))
    return jax.shard_map(local, mesh=mesh, in_specs=in_specs, out_specs=out_specs, check_vma=False)
```

```python
import functools

import jax
import jax.numpy as jnp
from jax import lax
from jax.experimental import pallas as pl
from jax.experimental.pallas import tpu as pltpu
from jax.sharding import PartitionSpec as P

ITERS = 2
COLUMNS = 4
BUFFERS = 4
F32 = jnp.float32
BF16 = jnp.bfloat16
MIB = 1 << 20
STREAM_LIMIT = 48 * MIB
GROUPS = 5
VMEM = pl.BlockSpec(memory_space=pltpu.VMEM)
SMEM = pl.BlockSpec(memory_space=pltpu.SMEM)
ANY = pl.BlockSpec(memory_space=pl.ANY)
HBM = pl.BlockSpec(memory_space=pltpu.MemorySpace.HBM)


def split_value(value):
    high = value.astype(BF16)
    low = (value - high.astype(F32)).astype(BF16)
    return high, low


def stacked_parts(real, imag):
    real_high, real_low = split_value(real)
    imag_high, imag_low = split_value(imag)
    with_real = jnp.concatenate((real_high, imag_high, real_low, imag_low), axis=0)
    with_imag = jnp.concatenate((-imag_high, real_high, -imag_low, real_low), axis=0)
    return with_real, with_imag


def dot_nt(left, right):
    return lax.dot_general(left, right, (((1,), (1,)), ((), ())), preferred_element_type=F32)


def dot_nn(left, right):
    return jnp.dot(left, right, preferred_element_type=F32)


def params(*byte_counts):
    return pltpu.CompilerParams(vmem_limit_bytes=sum(byte_counts) + 6 * MIB)


def size_of(*arrays):
    return sum(value.size * value.dtype.itemsize for value in arrays)


def place_of(column, particle, layer, particles, layers):
    return (column * particles + particle) * layers + layer


def index_kernel(
    layers, particles, owner_ref, side_ref, partners_ref, rows_of_ref, holders_ref, live_ref, *refs
):
    index_ref = refs[-1]
    slots = holders_ref.shape[0]
    stride, counts = GROUPS * slots, 3 * GROUPS * slots
    me = owner_ref[0]
    my_column, my_layer = lax.rem(me, COLUMNS), lax.div(me, COLUMNS)
    for group in range(GROUPS):
        index_ref[counts + group] = 0
    index_ref[counts + GROUPS] = side_ref[0]

    def step(slot, carry):
        row = rows_of_ref[partners_ref[me * slots + slot]]
        owner, particle = lax.div(row, particles), lax.rem(row, particles)
        column = lax.bitwise_xor(lax.rem(owner, COLUMNS), my_column)
        layer = lax.bitwise_xor(lax.div(owner, COLUMNS), my_layer)
        near = jnp.where(column == COLUMNS - 1, 2, 1)
        far = jnp.where(column == COLUMNS - 1, 4, 3)
        group = jnp.where(column == 0, 0, jnp.where(layer == 0, near, far))
        found = index_ref[counts + group]
        index_ref[counts + group] = found + 1
        position = group * slots + found
        index_ref[position] = slot
        index_ref[stride + position] = place_of(column, particle, layer, particles, layers)
        index_ref[2 * stride + position] = holders_ref[slot]
        return carry

    lax.fori_loop(0, live_ref[0], step, 0)


def slot_index(my_owner, side, partners, owner_of, block_rows, live, layers, particles, after):
    slots = block_rows.shape[0]
    return pl.pallas_call(
        functools.partial(index_kernel, layers, particles),
        out_shape=jax.ShapeDtypeStruct((3 * GROUPS * slots + GROUPS + 1,), jnp.int32),
        in_specs=[SMEM] * 6 + [ANY],
        out_specs=SMEM,
        compiler_params=params(),
        name="slot_index",
    )(my_owner, side, partners, owner_of, block_rows, live, after)


def prepare_kernel(tmat_ref, incident_ref, parts_ref, copy_ref, buf_ref, sems):
    particles, _, half, width = tmat_ref.shape

    def fetch(row):
        return pltpu.make_async_copy(tmat_ref.at[row], buf_ref.at[row], sems.at[row])

    for row in range(particles):
        fetch(row).start()
    own = pltpu.make_async_copy(incident_ref, copy_ref, sems.at[particles])
    own.start()
    for row in range(particles):
        fetch(row).wait()
        for part in range(2):
            high, low = split_value(buf_ref[row, part])
            parts_ref[row, :, part * width : (part + 1) * width] = high
            parts_ref[row, :, (2 + part) * width : (3 + part) * width] = low
    own.wait()


def prepare(tmat, incident):
    particles, _, half, width = tmat.shape
    return pl.pallas_call(
        prepare_kernel,
        out_shape=(
            jax.ShapeDtypeStruct((particles, half, 4 * width), BF16),
            jax.ShapeDtypeStruct(incident.shape, F32),
        ),
        in_specs=[HBM, HBM],
        out_specs=(VMEM, VMEM),
        scratch_shapes=[pltpu.VMEM(tmat.shape, F32), pltpu.SemaphoreType.DMA((particles + 1,))],
        compiler_params=params(2 * size_of(tmat), size_of(incident)),
        name="prepare",
    )(tmat, incident)


def tmat_kernel(halves, side_ref, mine_ref, theirs_ref, parts_ref, *refs):
    last = len(refs) == 4
    exciting_ref = refs[0] if last else None
    scattered_ref, full_ref = refs[1:3] if last else refs
    particles, _, directions, width = full_ref.shape
    half = width // 2
    start = pl.multiple_of(side_ref[0] * half, half)
    if halves:
        full_ref[:, :, :, pl.ds(start, half)] = mine_ref[...]
        full_ref[:, :, :, pl.ds(pl.multiple_of(half - start, half), half)] = theirs_ref[...]
    else:
        full_ref[...] = mine_ref[...] + theirs_ref[...]
    if last:
        window = full_ref.at[:, :, :, pl.ds(start, half)]
        leave = pltpu.make_async_copy(window, exciting_ref, refs[3])
        leave.start()
    for row in range(particles):
        with_real, with_imag = stacked_parts(full_ref[row, 0], full_ref[row, 1])
        right = jnp.concatenate((with_real, with_imag, with_real, with_imag), axis=1)
        total = dot_nt(parts_ref[row], right)
        out = (total[:, : 2 * directions] + total[:, 2 * directions :]).T
        scattered_ref[row, 0] = out[:directions]
        scattered_ref[row, 1] = out[directions:]
    if last:
        leave.wait()


def apply_tmat(halves, last, side, mine, theirs, parts):
    particles, _, directions, _ = mine.shape
    half = parts.shape[1]
    half_shape = jax.ShapeDtypeStruct((particles, 2, directions, half), F32)
    scratch = [pltpu.VMEM((particles, 2, directions, 2 * half), F32)]
    if last:
        scratch.append(pltpu.SemaphoreType.DMA)
    return pl.pallas_call(
        functools.partial(tmat_kernel, halves),
        out_shape=[half_shape] * (2 if last else 1),
        in_specs=[SMEM, VMEM, VMEM, VMEM],
        out_specs=[HBM, VMEM] if last else [VMEM],
        scratch_shapes=scratch,
        compiler_params=params(3 * size_of(mine, theirs), size_of(parts)),
        name="tmat_apply",
    )(side, mine, theirs, parts)


def chosen_slots(index_ref, groups, slots):
    stride, counts = GROUPS * slots, 3 * GROUPS * slots
    starts, total = [], 0
    for group in groups:
        starts.append(total)
        total = total + index_ref[counts + group]

    def at_turn(turn):
        position = groups[0] * slots + turn
        for group, start in zip(groups[1:], starts[1:]):
            position = jnp.where(turn >= start, group * slots + turn - start, position)
        return [index_ref[number * stride + position] for number in range(3)]

    return total, at_turn


def backward_kernel(first, groups, base, index_ref, own_ref, other_ref, blocks_ref, *refs):
    if first:
        out_ref, parts_ref, left_ref, buf_ref, sems, made_ref, made_sems = refs[-7:]
    else:
        out_ref, left_ref, buf_ref, sems = refs
    directions, half = own_ref.shape[2], own_ref.shape[3]
    width = 2 * half
    slots = blocks_ref.shape[0]
    wanted, at_turn = chosen_slots(index_ref, groups, slots)
    own_side = index_ref[3 * GROUPS * slots + GROUPS]

    def fetch(turn, place):
        return pltpu.make_async_copy(
            blocks_ref.at[at_turn(turn)[0]], buf_ref.at[place], sems.at[place]
        )

    def keep(turn, place):
        return pltpu.make_async_copy(
            made_ref.at[place], parts_ref.at[at_turn(turn)[0]], made_sems.at[place]
        )

    for early in range(BUFFERS):

        @pl.when(early < wanted)
        def _():
            fetch(early, early).start()

    for field_ref, side in ((own_ref, own_side), (other_ref, 1 - own_side)):
        for row in range(other_ref.shape[0]):
            with_real, with_imag = stacked_parts(field_ref[row, 0], field_ref[row, 1])
            for part, value in enumerate((with_real, with_imag)):
                start = pl.multiple_of(part * width + side * half, half)
                left_ref[row, :, pl.ds(start, half)] = value
    out_ref[...] = jnp.zeros_like(out_ref)

    def body(turn, carry):
        here = lax.rem(turn, BUFFERS)
        fetch(turn, here).wait()
        _, place, holder = at_turn(turn)
        place = place - base
        if first:
            spot = lax.rem(turn, 2)

            @pl.when(turn >= 2)
            def _():
                keep(turn - 2, spot).wait()

            high, low = split_value(buf_ref[here].reshape(2 * width, half))
            made_ref[spot, 0] = high.reshape(2, width, half)
            made_ref[spot, 1] = low.reshape(2, width, half)
            keep(turn, spot).start()
        else:
            high = buf_ref[here, 0].reshape(2 * width, half)
            low = buf_ref[here, 1].reshape(2 * width, half)
        total = dot_nn(left_ref[holder], high)
        rest = dot_nn(left_ref[holder, : 2 * directions], low)
        out = total[: 2 * directions] + total[2 * directions :] + rest
        out_ref[place, 0] = out[:directions]
        out_ref[place, 1] = out[directions:]

        @pl.when(turn + BUFFERS < wanted)
        def _():
            fetch(turn + BUFFERS, here).start()

        return carry

    lax.fori_loop(0, wanted, body, 0)
    if first:

        @pl.when(wanted >= 2)
        def _():
            keep(wanted - 2, lax.rem(wanted, 2)).wait()

        @pl.when(wanted >= 1)
        def _():
            keep(wanted - 1, lax.rem(wanted - 1, 2)).wait()


def backward(first, groups, base, count, index, own_half, other_half, blocks, parts):
    particles, _, directions, half = other_half.shape
    width = 2 * half
    slots = blocks.shape[0]
    out_shape = [jax.ShapeDtypeStruct((count, 2, directions, half), F32)]
    out_specs = [VMEM]
    source = blocks if first else parts
    scratch = [
        pltpu.VMEM((particles, 4 * directions, 2 * width), BF16),
        pltpu.VMEM((BUFFERS,) + source.shape[1:], source.dtype),
        pltpu.SemaphoreType.DMA((BUFFERS,)),
    ]
    operands = [index, own_half, other_half, source]
    in_specs = [SMEM, VMEM, VMEM, HBM]
    aliases = {}
    if first:
        out_shape.append(jax.ShapeDtypeStruct((slots, 2, 2, width, half), BF16))
        out_specs.append(HBM)
        scratch.append(pltpu.VMEM((2, 2, 2, width, half), BF16))
        scratch.append(pltpu.SemaphoreType.DMA((2,)))
        if parts is not None:
            aliases = {len(operands): 1}
            operands.append(parts)
            in_specs.append(HBM)
    return pl.pallas_call(
        functools.partial(backward_kernel, first, groups, base),
        out_shape=out_shape,
        in_specs=in_specs,
        out_specs=out_specs,
        scratch_shapes=scratch,
        input_output_aliases=aliases,
        compiler_params=pltpu.CompilerParams(vmem_limit_bytes=STREAM_LIMIT),
        cost_estimate=pl.CostEstimate(
            flops=directions * width * half,
            bytes_accessed=size_of(own_half),
            transcendentals=0,
        ),
        name="backward_group" + str(groups[0]),
    )(*operands)


def forward_kernel(groups, copies, count, index_ref, *refs):
    field_refs = refs[:count]
    parts_ref = refs[count]
    out_ref, every_ref, acc_ref, buf_ref, sems = refs[-5:]
    directions = out_ref.shape[2]
    wanted, at_turn = chosen_slots(index_ref, groups, parts_ref.shape[0])

    def fetch(turn, place):
        return pltpu.make_async_copy(
            parts_ref.at[at_turn(turn)[0]], buf_ref.at[place], sems.at[place]
        )

    for early in range(BUFFERS):

        @pl.when(early < wanted)
        def _():
            fetch(early, early).start()

    acc_ref[...] = jnp.zeros_like(acc_ref)
    for number, row, place in copies:
        every_ref[place] = field_refs[number][row]

    def body(turn, carry):
        here = lax.rem(turn, BUFFERS)
        _, place, holder = at_turn(turn)
        with_real, with_imag = stacked_parts(every_ref[place, 0], every_ref[place, 1])
        fetch(turn, here).wait()
        total = dot_nt(buf_ref[here, 0, 0], with_real) + dot_nt(buf_ref[here, 0, 1], with_imag)
        total += dot_nt(buf_ref[here, 1, 0], with_real) + dot_nt(buf_ref[here, 1, 1], with_imag)
        acc_ref[holder] += total

        @pl.when(turn + BUFFERS < wanted)
        def _():
            fetch(turn + BUFFERS, here).start()

        return carry

    lax.fori_loop(0, wanted, body, 0)
    for row in range(acc_ref.shape[0]):
        total = acc_ref[row]
        out = (total[:, : 2 * directions] + total[:, 2 * directions :]).T
        out_ref[row, 0] = out[:directions]
        out_ref[row, 1] = out[directions:]


def forward(groups, index, fields, copies, parts, particles, total_rows, after):
    slots, _, _, width, half = parts.shape
    directions = fields[0].shape[2]
    out_shape = jax.ShapeDtypeStruct((particles, 2, directions, width), F32)
    return pl.pallas_call(
        functools.partial(forward_kernel, groups, copies, len(fields)),
        out_shape=out_shape,
        in_specs=[SMEM] + [VMEM] * len(fields) + [HBM] + [ANY] * len(after),
        out_specs=VMEM,
        scratch_shapes=[
                pltpu.VMEM((total_rows, 2, directions, half), F32),
            pltpu.VMEM((particles, width, 4 * directions), F32),
            pltpu.VMEM((BUFFERS,) + parts.shape[1:], BF16),
            pltpu.SemaphoreType.DMA((BUFFERS,)),
        ],
        compiler_params=pltpu.CompilerParams(vmem_limit_bytes=STREAM_LIMIT),
        cost_estimate=pl.CostEstimate(
            flops=directions * width * half,
            bytes_accessed=size_of(out_shape),
            transcendentals=0,
        ),
        name="forward_group" + str(groups[0]),
    )(index, *fields, parts, *after)


def pack_kernel(plans, count, *refs):
    in_refs, out_refs = refs[:count], refs[-len(plans) :]
    for out_ref, plan in zip(out_refs, plans):
        for row, terms in enumerate(plan):
            value = in_refs[terms[0][0]][terms[0][1]]
            for number, source in terms[1:]:
                value = value + in_refs[number][source]
            out_ref[row] = value


def pack(name, inputs, plans, after=()):
    shapes = [jax.ShapeDtypeStruct((len(plan),) + inputs[0].shape[1:], F32) for plan in plans]
    return pl.pallas_call(
        functools.partial(pack_kernel, plans, len(inputs)),
        out_shape=shapes,
        in_specs=[VMEM] * len(inputs) + [ANY] * len(after),
        out_specs=[VMEM] * len(plans),
        compiler_params=params(size_of(*inputs), size_of(*shapes)),
        name=name,
    )(*inputs, *after)


def total_kernel(counts, side_ref, incident_ref, *refs):
    nears, halves, out_ref = refs[: counts[0]], refs[counts[0] : -1], refs[-1]
    particles, half = incident_ref.shape[0], incident_ref.shape[3]
    start = pl.multiple_of(side_ref[0] * half, half)
    near = nears[0][...]
    for ref in nears[1:]:
        near = near + ref[...]
    out_ref[...] = near
    for particle in range(particles):
        value = incident_ref[particle]
        for ref, step in zip(halves, counts[1]):
            value = value + ref[particle * step]
        window = (particle, slice(None), slice(None), pl.ds(start, half))
        out_ref[window] = out_ref[window] + value


def whole_total(side, incident, nears, halves):
    arrays = [value for value, _ in halves]
    steps = tuple(step for _, step in halves)
    return pl.pallas_call(
        functools.partial(total_kernel, (len(nears), steps)),
        out_shape=jax.ShapeDtypeStruct(nears[0].shape, F32),
        in_specs=[SMEM] + [VMEM] * (1 + len(nears) + len(arrays)),
        out_specs=VMEM,
        compiler_params=params(size_of(*nears, nears[0], incident, *arrays)),
        name="total",
    )(side, incident, *nears, *arrays)


def from_other(value):
    return lax.ppermute(value, "pair", [(0, 1), (1, 0)])


def across(value, bit):
    count = lax.axis_size("owner")
    return lax.ppermute(value, "owner", [(source, source ^ bit) for source in range(count)])


def scatter_step(incident, scattered, blocks, parts, index, side, layers):
    particles = incident.shape[0]
    every = range(particles)
    by_x = range((particles + 1) // 2)
    by_y = range((particles + 1) // 2, particles)
    rest = range(1, layers)
    powers = [1 << step for step in range(layers.bit_length() - 1)]
    at = functools.partial(place_of, particles=particles, layers=layers)
    total_rows = COLUMNS * particles * layers
    first_n, first_d = at(1, 0, 0), at(3, 0, 0)
    first = parts is None

    def row_of(particle, layer):
        return particle * layers + layer

    other = from_other(scattered)
    x1 = across(scattered, 1)
    y1 = across(scattered, 2)
    reached = [across(scattered, COLUMNS)]
    where = {1: (0, 0), 2: (1, 0), 3: (2, 0)}
    fetched = (scattered, other, blocks)
    products_d, *made = backward(
        first, (2, 4), first_d, total_rows - first_d, index, *fetched, parts
    )
    if first:
        parts = made[0]

    inputs = [products_d, x1, y1, scattered]
    x_plan = [[(0, row_of(particle, layer))] for particle in by_x for layer in range(layers)]
    y_plan = [[(0, row_of(particle, layer))] for particle in by_y for layer in range(layers)]
    x_head, y_head = len(x_plan), len(y_plan)
    x_plan += [[(2, particle)] for particle in by_y]
    y_plan += [[(1, particle)] for particle in by_x]
    x2, y2, copied = pack(
        "pack_second",
        inputs,
        [x_plan, y_plan, [[(3, particle)] for particle in every]],
        reached,
    )
    x2, y2 = across(x2, 1), across(y2, 2)
    reached.append(across(copied, 2 * COLUMNS))
    products_n, *made = backward(first, (1, 3), first_n, first_d - first_n, index, *fetched, parts)
    if first:
        parts = made[0]

    def z_row(particle, layer):
        number, start = where[layer]
        return number, start + particle

    inputs = [products_n, x2, y2, scattered, reached[0]]
    x_plan, y_plan = [], []
    for particle in every:
        for layer in range(layers):
            x_terms = [(0, at(1, particle, layer) - first_n)]
            y_terms = [(0, at(2, particle, layer) - first_n)]
            if particle in by_x:
                y_terms.append((1, row_of(particle, layer)))
            else:
                x_terms.append((2, row_of(particle - len(by_x), layer)))
            x_plan.append(x_terms)
            y_plan.append(y_terms)
    z_plans = [[[(number, particle)] for particle in every] for number in (3, 4)]
    x3, y3, copied, known = pack("pack_third", inputs, [x_plan, y_plan] + z_plans, reached[1:])
    x3, y3 = across(x3, 1), across(y3, 2)
    reached.append(across(known, 2 * COLUMNS))
    for bit in powers[2:]:
        plan = [[(0, particle)] for particle in every]
        for layer in range(1, bit):
            plan += [[(1 + where[layer][0], where[layer][1] + particle)] for particle in every]
        (known,) = pack("pack_layers", [scattered] + reached, [plan])
        for layer in range(bit):
            where[bit + layer] = (len(reached), layer * particles)
        reached.append(across(known, bit * COLUMNS))
    products_o, *made = backward(first, (0,), 0, first_n, index, copied, other, blocks, parts)
    if first:
        parts = made[0]
    copies = []
    for particle in every:
        copies.append((0, particle, at(1, particle, 0)))
        copies.append((1, particle, at(2, particle, 0)))
        if particle in by_x:
            copies.append((3, y_head + particle, at(3, particle, 0)))
        else:
            copies.append((2, x_head + particle - len(by_x), at(3, particle, 0)))
    near_level = forward(
        (1, 2),
        index,
        [x1, y1, x2, y2],
        tuple(copies),
        parts,
        particles,
        total_rows,
        [products_o],
    )

    def summed(layer, particle, arrived):
        terms = [(number, row_of(particle, layer)) for number in range(3)]
        return terms + [(number, layer * particles + particle) for number in arrived]

    def half_sums(bit, arrived):
        return [summed(layer, particle, arrived) for layer in range(bit, 2 * bit) for particle in every]

    inputs = [products_o, x3, y3] + reached
    tails = []
    for particle in every:
        for layer in rest:
            step, row = z_row(particle, layer)
            tails.append([(3 + step, row)])
    x4, y4, sums, mark = pack(
        "pack_fourth",
        inputs,
        [tails, tails, half_sums(powers[-1], ()), [[(1, 0)]]],
        [near_level],
    )
    x4, y4 = across(x4, 1), across(y4, 2)
    arrived = [across(sums, powers[-1] * COLUMNS)]
    copies = []
    for particle in every:
        for layer in rest:
            step, row = z_row(particle, layer)
            copies.append((step, row, at(0, particle, layer)))
    near_column = forward(
        (0,), index, reached, tuple(copies), parts, particles, total_rows, [mark]
    )

    def tail(particle, layer):
        return particle * len(rest) + layer - 1

    x5, y5, mark = pack(
        "pack_fifth",
        [x4, y4],
        [
            [[(1, tail(particle, layer))] for particle in by_y for layer in rest],
            [[(0, tail(particle, layer))] for particle in by_x for layer in rest],
            [[(0, 0)]],
        ],
        [near_column],
    )
    x5, y5 = across(x5, 1), across(y5, 2)
    for bit in powers[-2::-1]:
        numbers = range(3, 3 + len(arrived))
        (sums,) = pack(
            "pack_sums", [products_o, x3, y3] + arrived, [half_sums(bit, numbers)], [mark]
        )
        arrived.append(across(sums, bit * COLUMNS))
    copies = []
    for particle in every:
        for layer in rest:
            copies.append((0, tail(particle, layer), at(1, particle, layer)))
            copies.append((1, tail(particle, layer), at(2, particle, layer)))
    near_second = forward(
        (3,), index, [x4, y4], tuple(copies), parts, particles, total_rows, [mark, sums]
    )
    copies = []
    for number, group in ((0, by_y), (1, by_x)):
        for order, particle in enumerate(group):
            for layer in rest:
                copies.append((number, tail(order, layer), at(3, particle, layer)))
    near_last = forward(
        (4,), index, [x5, y5], tuple(copies), parts, particles, total_rows, [near_second]
    )
    nears = [near_level, near_column, near_second, near_last]
    halves = [(products_o, layers), (x3, layers), (y3, layers)] + [(value, 1) for value in arrived]
    return whole_total(side, incident, nears, halves), parts


def local(incident, tmat, blocks, block_rows, partners, live, owner_of):
    layers = lax.axis_size("owner") // COLUMNS
    my_owner = lax.axis_index("owner").astype(jnp.int32)[None]
    side = lax.axis_index("pair").astype(jnp.int32)[None]
    theirs = from_other(incident)
    tmat_parts, incident = prepare(tmat, incident)
    (scattered,) = apply_tmat(True, False, side, incident, theirs, tmat_parts)
    index = slot_index(
        my_owner, side, partners, owner_of, block_rows, live, layers, incident.shape[0], scattered
    )
    parts = None
    for turn in range(ITERS):
        mine, parts = scatter_step(incident, scattered, blocks, parts, index, side, layers)
        theirs = from_other(mine)
        last = turn == ITERS - 1
        *exciting, scattered = apply_tmat(False, last, side, mine, theirs, tmat_parts)
    return (scattered, exciting[0])


def solution(mesh):
    in_specs = (
        P("owner", None, None, "pair"),
        P("owner", None, "pair", None),
        P("owner", None, None, "pair"),
        P("owner"),
        P(),
        P("owner"),
        P(),
    )
    out_specs = (P("owner", None, None, "pair"), P("owner", None, None, "pair"))
    return jax.shard_map(local, mesh=mesh, in_specs=in_specs, out_specs=out_specs, check_vma=False)
```

```python
import functools

import jax
import jax.numpy as jnp
from jax import lax
from jax.experimental import pallas as pl
from jax.experimental.pallas import tpu as pltpu
from jax.sharding import PartitionSpec as P

ITERS = 2
COLUMNS = 4
BUFFERS = 4
F32 = jnp.float32
BF16 = jnp.bfloat16
MIB = 1 << 20
STREAM_LIMIT = 48 * MIB
ALONE_LIMIT = 63 * MIB
GROUPS = 5
VMEM = pl.BlockSpec(memory_space=pltpu.VMEM)
SMEM = pl.BlockSpec(memory_space=pltpu.SMEM)
ANY = pl.BlockSpec(memory_space=pl.ANY)
HBM = pl.BlockSpec(memory_space=pltpu.MemorySpace.HBM)


def split_value(value):
    high = value.astype(BF16)
    low = (value - high.astype(F32)).astype(BF16)
    return high, low


def stacked_parts(real, imag):
    real_high, real_low = split_value(real)
    imag_high, imag_low = split_value(imag)
    with_real = jnp.concatenate((real_high, imag_high, real_low, imag_low), axis=0)
    with_imag = jnp.concatenate((-imag_high, real_high, -imag_low, real_low), axis=0)
    return with_real, with_imag


def dot_nt(left, right):
    return lax.dot_general(left, right, (((1,), (1,)), ((), ())), preferred_element_type=F32)


def dot_nn(left, right):
    return jnp.dot(left, right, preferred_element_type=F32)


def params(*byte_counts):
    return pltpu.CompilerParams(vmem_limit_bytes=sum(byte_counts) + 6 * MIB)


def size_of(*arrays):
    return sum(value.size * value.dtype.itemsize for value in arrays)


def place_of(column, particle, layer, particles, layers):
    return (column * particles + particle) * layers + layer


def index_kernel(
    layers, particles, owner_ref, side_ref, partners_ref, rows_of_ref, holders_ref, live_ref, *refs
):
    index_ref = refs[-1]
    slots = holders_ref.shape[0]
    stride, counts = GROUPS * slots, 3 * GROUPS * slots
    me = owner_ref[0]
    my_column, my_layer = lax.rem(me, COLUMNS), lax.div(me, COLUMNS)
    for group in range(GROUPS):
        index_ref[counts + group] = 0
    index_ref[counts + GROUPS] = side_ref[0]

    def step(slot, carry):
        row = rows_of_ref[partners_ref[me * slots + slot]]
        owner, particle = lax.div(row, particles), lax.rem(row, particles)
        column = lax.bitwise_xor(lax.rem(owner, COLUMNS), my_column)
        layer = lax.bitwise_xor(lax.div(owner, COLUMNS), my_layer)
        near = jnp.where(column == COLUMNS - 1, 2, 1)
        far = jnp.where(column == COLUMNS - 1, 4, 3)
        group = jnp.where(column == 0, 0, jnp.where(layer == 0, near, far))
        found = index_ref[counts + group]
        index_ref[counts + group] = found + 1
        position = group * slots + found
        index_ref[position] = slot
        index_ref[stride + position] = place_of(column, particle, layer, particles, layers)
        index_ref[2 * stride + position] = holders_ref[slot]
        return carry

    lax.fori_loop(0, live_ref[0], step, 0)


def slot_index(my_owner, side, partners, owner_of, block_rows, live, layers, particles):
    slots = block_rows.shape[0]
    return pl.pallas_call(
        functools.partial(index_kernel, layers, particles),
        out_shape=jax.ShapeDtypeStruct((3 * GROUPS * slots + GROUPS + 1,), jnp.int32),
        in_specs=[SMEM] * 6,
        out_specs=SMEM,
        compiler_params=pltpu.CompilerParams(vmem_limit_bytes=ALONE_LIMIT),
        name="slot_index",
    )(my_owner, side, partners, owner_of, block_rows, live)


def prepare_kernel(tmat_ref, incident_ref, after_ref, parts_ref, copy_ref, buf_ref, sems):
    particles, _, half, width = tmat_ref.shape

    def fetch(row):
        return pltpu.make_async_copy(tmat_ref.at[row], buf_ref.at[row], sems.at[row])

    for row in range(particles):
        fetch(row).start()
    own = pltpu.make_async_copy(incident_ref, copy_ref, sems.at[particles])
    own.start()
    for row in range(particles):
        fetch(row).wait()
        for part in range(2):
            high, low = split_value(buf_ref[row, part])
            parts_ref[row, :, part * width : (part + 1) * width] = high
            parts_ref[row, :, (2 + part) * width : (3 + part) * width] = low
    own.wait()


def prepare(tmat, incident, after):
    particles, _, half, width = tmat.shape
    return pl.pallas_call(
        prepare_kernel,
        out_shape=(
            jax.ShapeDtypeStruct((particles, half, 4 * width), BF16),
            jax.ShapeDtypeStruct(incident.shape, F32),
        ),
        in_specs=[HBM, HBM, ANY],
        out_specs=(VMEM, VMEM),
        scratch_shapes=[pltpu.VMEM(tmat.shape, F32), pltpu.SemaphoreType.DMA((particles + 1,))],
        compiler_params=params(2 * size_of(tmat), size_of(incident)),
        name="prepare",
    )(tmat, incident, after)


def tmat_kernel(halves, side_ref, mine_ref, theirs_ref, parts_ref, *refs):
    last = len(refs) == 4
    exciting_ref = refs[0] if last else None
    scattered_ref, full_ref = refs[1:3] if last else refs
    particles, _, directions, width = full_ref.shape
    half = width // 2
    start = pl.multiple_of(side_ref[0] * half, half)
    if halves:
        full_ref[:, :, :, pl.ds(start, half)] = mine_ref[...]
        full_ref[:, :, :, pl.ds(pl.multiple_of(half - start, half), half)] = theirs_ref[...]
    else:
        full_ref[...] = mine_ref[...] + theirs_ref[...]
    if last:
        window = full_ref.at[:, :, :, pl.ds(start, half)]
        leave = pltpu.make_async_copy(window, exciting_ref, refs[3])
        leave.start()
    for row in range(particles):
        with_real, with_imag = stacked_parts(full_ref[row, 0], full_ref[row, 1])
        right = jnp.concatenate((with_real, with_imag, with_real, with_imag), axis=1)
        total = dot_nt(parts_ref[row], right)
        out = (total[:, : 2 * directions] + total[:, 2 * directions :]).T
        scattered_ref[row, 0] = out[:directions]
        scattered_ref[row, 1] = out[directions:]
    if last:
        leave.wait()


def apply_tmat(halves, last, side, mine, theirs, parts):
    particles, _, directions, _ = mine.shape
    half = parts.shape[1]
    half_shape = jax.ShapeDtypeStruct((particles, 2, directions, half), F32)
    scratch = [pltpu.VMEM((particles, 2, directions, 2 * half), F32)]
    if last:
        scratch.append(pltpu.SemaphoreType.DMA)
    return pl.pallas_call(
        functools.partial(tmat_kernel, halves),
        out_shape=[half_shape] * (2 if last else 1),
        in_specs=[SMEM, VMEM, VMEM, VMEM],
        out_specs=[HBM, VMEM] if last else [VMEM],
        scratch_shapes=scratch,
        compiler_params=params(3 * size_of(mine, theirs), size_of(parts)),
        name="tmat_apply",
    )(side, mine, theirs, parts)


def chosen_slots(index_ref, groups, slots):
    stride, counts = GROUPS * slots, 3 * GROUPS * slots
    starts, total = [], 0
    for group in groups:
        starts.append(total)
        total = total + index_ref[counts + group]

    def at_turn(turn):
        position = groups[0] * slots + turn
        for group, start in zip(groups[1:], starts[1:]):
            position = jnp.where(turn >= start, group * slots + turn - start, position)
        return [index_ref[number * stride + position] for number in range(3)]

    return total, at_turn


def backward_kernel(first, groups, base, index_ref, own_ref, other_ref, blocks_ref, *refs):
    if first:
        out_ref, parts_ref, left_ref, buf_ref, sems, made_ref, made_sems = refs[-7:]
    else:
        out_ref, left_ref, buf_ref, sems = refs
    directions, half = own_ref.shape[2], own_ref.shape[3]
    width = 2 * half
    slots = blocks_ref.shape[0]
    wanted, at_turn = chosen_slots(index_ref, groups, slots)
    own_side = index_ref[3 * GROUPS * slots + GROUPS]

    def fetch(turn, place):
        return pltpu.make_async_copy(
            blocks_ref.at[at_turn(turn)[0]], buf_ref.at[place], sems.at[place]
        )

    def keep(turn, place):
        return pltpu.make_async_copy(
            made_ref.at[place], parts_ref.at[at_turn(turn)[0]], made_sems.at[place]
        )

    for early in range(BUFFERS):

        @pl.when(early < wanted)
        def _():
            fetch(early, early).start()

    for field_ref, side in ((own_ref, own_side), (other_ref, 1 - own_side)):
        for row in range(other_ref.shape[0]):
            with_real, with_imag = stacked_parts(field_ref[row, 0], field_ref[row, 1])
            for part, value in enumerate((with_real, with_imag)):
                start = pl.multiple_of(part * width + side * half, half)
                left_ref[row, :, pl.ds(start, half)] = value
    out_ref[...] = jnp.zeros_like(out_ref)

    def body(turn, carry):
        here = lax.rem(turn, BUFFERS)
        fetch(turn, here).wait()
        _, place, holder = at_turn(turn)
        place = place - base
        if first:
            spot = lax.rem(turn, 2)

            @pl.when(turn >= 2)
            def _():
                keep(turn - 2, spot).wait()

            high, low = split_value(buf_ref[here].reshape(2 * width, half))
            made_ref[spot, 0] = high.reshape(2, width, half)
            made_ref[spot, 1] = low.reshape(2, width, half)
            keep(turn, spot).start()
        else:
            high = buf_ref[here, 0].reshape(2 * width, half)
            low = buf_ref[here, 1].reshape(2 * width, half)
        total = dot_nn(left_ref[holder], high)
        rest = dot_nn(left_ref[holder, : 2 * directions], low)
        out = total[: 2 * directions] + total[2 * directions :] + rest
        out_ref[place, 0] = out[:directions]
        out_ref[place, 1] = out[directions:]

        @pl.when(turn + BUFFERS < wanted)
        def _():
            fetch(turn + BUFFERS, here).start()

        return carry

    lax.fori_loop(0, wanted, body, 0)
    if first:

        @pl.when(wanted >= 2)
        def _():
            keep(wanted - 2, lax.rem(wanted, 2)).wait()

        @pl.when(wanted >= 1)
        def _():
            keep(wanted - 1, lax.rem(wanted - 1, 2)).wait()


def backward(first, groups, base, count, index, own_half, other_half, blocks, parts):
    particles, _, directions, half = other_half.shape
    width = 2 * half
    slots = blocks.shape[0]
    out_shape = [jax.ShapeDtypeStruct((count, 2, directions, half), F32)]
    out_specs = [VMEM]
    source = blocks if first else parts
    scratch = [
        pltpu.VMEM((particles, 4 * directions, 2 * width), BF16),
        pltpu.VMEM((BUFFERS,) + source.shape[1:], source.dtype),
        pltpu.SemaphoreType.DMA((BUFFERS,)),
    ]
    operands = [index, own_half, other_half, source]
    in_specs = [SMEM, VMEM, VMEM, HBM]
    aliases = {}
    if first:
        out_shape.append(jax.ShapeDtypeStruct((slots, 2, 2, width, half), BF16))
        out_specs.append(HBM)
        scratch.append(pltpu.VMEM((2, 2, 2, width, half), BF16))
        scratch.append(pltpu.SemaphoreType.DMA((2,)))
        if parts is not None:
            aliases = {len(operands): 1}
            operands.append(parts)
            in_specs.append(HBM)
    return pl.pallas_call(
        functools.partial(backward_kernel, first, groups, base),
        out_shape=out_shape,
        in_specs=in_specs,
        out_specs=out_specs,
        scratch_shapes=scratch,
        input_output_aliases=aliases,
        compiler_params=pltpu.CompilerParams(vmem_limit_bytes=STREAM_LIMIT),
        cost_estimate=pl.CostEstimate(
            flops=directions * width * half,
            bytes_accessed=size_of(own_half),
            transcendentals=0,
        ),
        name="backward_group" + str(groups[0]),
    )(*operands)


def forward_kernel(groups, copies, count, begun, last, index_ref, *refs):
    field_refs = refs[:count]
    parts_ref = refs[count]
    if last:
        out_ref, every_ref, buf_ref, sems, acc_ref = refs[-5:]
    else:
        acc_ref, every_ref, buf_ref, sems = refs[-4:]
    directions = every_ref.shape[2]
    wanted, at_turn = chosen_slots(index_ref, groups, parts_ref.shape[0])

    def fetch(turn, place):
        return pltpu.make_async_copy(
            parts_ref.at[at_turn(turn)[0]], buf_ref.at[place], sems.at[place]
        )

    for early in range(BUFFERS):

        @pl.when(early < wanted)
        def _():
            fetch(early, early).start()

    acc_ref[...] = refs[count + 1][...] if begun else jnp.zeros_like(acc_ref)
    for number, row, place in copies:
        every_ref[place] = field_refs[number][row]

    def body(turn, carry):
        here = lax.rem(turn, BUFFERS)
        _, place, holder = at_turn(turn)
        with_real, with_imag = stacked_parts(every_ref[place, 0], every_ref[place, 1])
        fetch(turn, here).wait()
        total = dot_nt(buf_ref[here, 0, 0], with_real) + dot_nt(buf_ref[here, 0, 1], with_imag)
        total += dot_nt(buf_ref[here, 1, 0], with_real) + dot_nt(buf_ref[here, 1, 1], with_imag)
        acc_ref[holder] += total

        @pl.when(turn + BUFFERS < wanted)
        def _():
            fetch(turn + BUFFERS, here).start()

        return carry

    lax.fori_loop(0, wanted, body, 0)
    for row in range(acc_ref.shape[0] if last else 0):
        total = acc_ref[row]
        out = (total[:, : 2 * directions] + total[:, 2 * directions :]).T
        out_ref[row, 0] = out[:directions]
        out_ref[row, 1] = out[directions:]


def forward(groups, index, fields, copies, parts, particles, total_rows, before, last, after):
    slots, _, _, width, half = parts.shape
    directions = fields[0].shape[2]
    acc = (particles, width, 4 * directions)
    given = [] if before is None else [before]
    scratch = [
        pltpu.VMEM((total_rows, 2, directions, half), F32),
        pltpu.VMEM((BUFFERS,) + parts.shape[1:], BF16),
        pltpu.SemaphoreType.DMA((BUFFERS,)),
    ]
    if last:
        scratch.append(pltpu.VMEM(acc, F32))
    out_shape = jax.ShapeDtypeStruct((particles, 2, directions, width) if last else acc, F32)
    return pl.pallas_call(
        functools.partial(forward_kernel, groups, copies, len(fields), bool(given), last),
        out_shape=out_shape,
        in_specs=[SMEM] + [VMEM] * len(fields) + [HBM] + [VMEM] * len(given) + [ANY] * len(after),
        out_specs=VMEM,
        scratch_shapes=scratch,
        compiler_params=pltpu.CompilerParams(vmem_limit_bytes=STREAM_LIMIT),
        cost_estimate=pl.CostEstimate(
            flops=directions * width * half,
            bytes_accessed=size_of(out_shape),
            transcendentals=0,
        ),
        name="forward_group" + str(groups[0]),
    )(index, *fields, parts, *given, *after)


def pack_kernel(plans, count, *refs):
    in_refs, out_refs = refs[:count], refs[-len(plans) :]
    for out_ref, plan in zip(out_refs, plans):
        for row, terms in enumerate(plan):
            value = in_refs[terms[0][0]][terms[0][1]]
            for number, source in terms[1:]:
                value = value + in_refs[number][source]
            out_ref[row] = value


def pack(name, inputs, plans, after=()):
    shapes = [jax.ShapeDtypeStruct((len(plan),) + inputs[0].shape[1:], F32) for plan in plans]
    return pl.pallas_call(
        functools.partial(pack_kernel, plans, len(inputs)),
        out_shape=shapes,
        in_specs=[VMEM] * len(inputs) + [ANY] * len(after),
        out_specs=[VMEM] * len(plans),
        compiler_params=params(size_of(*inputs), size_of(*shapes)),
        name=name,
    )(*inputs, *after)


def total_kernel(counts, side_ref, incident_ref, *refs):
    nears, halves, out_ref = refs[: counts[0]], refs[counts[0] : -1], refs[-1]
    particles, half = incident_ref.shape[0], incident_ref.shape[3]
    start = pl.multiple_of(side_ref[0] * half, half)
    near = nears[0][...]
    for ref in nears[1:]:
        near = near + ref[...]
    out_ref[...] = near
    for particle in range(particles):
        value = incident_ref[particle]
        for ref, step in zip(halves, counts[1]):
            value = value + ref[particle * step]
        window = (particle, slice(None), slice(None), pl.ds(start, half))
        out_ref[window] = out_ref[window] + value


def whole_total(side, incident, nears, halves):
    arrays = [value for value, _ in halves]
    steps = tuple(step for _, step in halves)
    return pl.pallas_call(
        functools.partial(total_kernel, (len(nears), steps)),
        out_shape=jax.ShapeDtypeStruct(nears[0].shape, F32),
        in_specs=[SMEM] + [VMEM] * (1 + len(nears) + len(arrays)),
        out_specs=VMEM,
        compiler_params=params(size_of(*nears, nears[0], incident, *arrays)),
        name="total",
    )(side, incident, *nears, *arrays)


def from_other(value):
    return lax.ppermute(value, "pair", [(0, 1), (1, 0)])


def across(value, bit):
    count = lax.axis_size("owner")
    return lax.ppermute(value, "owner", [(source, source ^ bit) for source in range(count)])


def scatter_step(incident, scattered, blocks, parts, index, side, layers):
    particles = incident.shape[0]
    every = range(particles)
    by_x = range((particles + 1) // 2)
    by_y = range((particles + 1) // 2, particles)
    rest = range(1, layers)
    powers = [1 << step for step in range(layers.bit_length() - 1)]
    at = functools.partial(place_of, particles=particles, layers=layers)
    total_rows = COLUMNS * particles * layers
    first_n, first_d = at(1, 0, 0), at(3, 0, 0)
    first = parts is None

    def row_of(particle, layer):
        return particle * layers + layer

    other = from_other(scattered)
    x1 = across(scattered, 1)
    y1 = across(scattered, 2)
    reached = [across(scattered, COLUMNS)]
    where = {1: (0, 0), 2: (1, 0), 3: (2, 0)}
    fetched = (scattered, other, blocks)
    products_d, *made = backward(
        first, (2, 4), first_d, total_rows - first_d, index, *fetched, parts
    )
    if first:
        parts = made[0]

    inputs = [products_d, x1, y1, scattered]
    x_plan = [[(0, row_of(particle, layer))] for particle in by_x for layer in range(layers)]
    y_plan = [[(0, row_of(particle, layer))] for particle in by_y for layer in range(layers)]
    x_head, y_head = len(x_plan), len(y_plan)
    x_plan += [[(2, particle)] for particle in by_y]
    y_plan += [[(1, particle)] for particle in by_x]
    x2, y2, copied = pack(
        "pack_second",
        inputs,
        [x_plan, y_plan, [[(3, particle)] for particle in every]],
        reached,
    )
    x2, y2 = across(x2, 1), across(y2, 2)
    reached.append(across(copied, 2 * COLUMNS))
    products_n, *made = backward(first, (1, 3), first_n, first_d - first_n, index, *fetched, parts)
    if first:
        parts = made[0]

    def z_row(particle, layer):
        number, start = where[layer]
        return number, start + particle

    inputs = [products_n, x2, y2, scattered, reached[0]]
    x_plan, y_plan = [], []
    for particle in every:
        for layer in range(layers):
            x_terms = [(0, at(1, particle, layer) - first_n)]
            y_terms = [(0, at(2, particle, layer) - first_n)]
            if particle in by_x:
                y_terms.append((1, row_of(particle, layer)))
            else:
                x_terms.append((2, row_of(particle - len(by_x), layer)))
            x_plan.append(x_terms)
            y_plan.append(y_terms)
    z_plans = [[[(number, particle)] for particle in every] for number in (3, 4)]
    x3, y3, copied, known = pack("pack_third", inputs, [x_plan, y_plan] + z_plans, reached[1:])
    x3, y3 = across(x3, 1), across(y3, 2)
    reached.append(across(known, 2 * COLUMNS))
    for bit in powers[2:]:
        plan = [[(0, particle)] for particle in every]
        for layer in range(1, bit):
            plan += [[(1 + where[layer][0], where[layer][1] + particle)] for particle in every]
        (known,) = pack("pack_layers", [scattered] + reached, [plan])
        for layer in range(bit):
            where[bit + layer] = (len(reached), layer * particles)
        reached.append(across(known, bit * COLUMNS))
    products_o, *made = backward(first, (0,), 0, first_n, index, copied, other, blocks, parts)
    if first:
        parts = made[0]
    copies = []
    for particle in every:
        copies.append((0, particle, at(1, particle, 0)))
        copies.append((1, particle, at(2, particle, 0)))
        if particle in by_x:
            copies.append((3, y_head + particle, at(3, particle, 0)))
        else:
            copies.append((2, x_head + particle - len(by_x), at(3, particle, 0)))
    sizes = (particles, total_rows)
    near = forward(
        (1, 2), index, [x1, y1, x2, y2], tuple(copies), parts, *sizes, None, False, [products_o]
    )

    def summed(layer, particle, arrived):
        terms = [(number, row_of(particle, layer)) for number in range(3)]
        for step in range(arrived):
            terms.append((3 + step, (layer >> (step + 1)) * particles + particle))
        return terms

    def half_sums(bit, arrived):
        chosen = range(bit, layers, 2 * bit)
        return [summed(layer, particle, arrived) for layer in chosen for particle in every]

    inputs = [products_o, x3, y3] + reached
    tails = []
    for particle in every:
        for layer in rest:
            step, row = z_row(particle, layer)
            tails.append([(3 + step, row)])
    x4, y4, sums, mark = pack(
        "pack_fourth",
        inputs,
        [tails, tails, half_sums(1, 0), [[(1, 0)]]],
        [near],
    )
    x4, y4 = across(x4, 1), across(y4, 2)
    arrived = [across(sums, COLUMNS)]
    copies = []
    for particle in every:
        for layer in rest:
            step, row = z_row(particle, layer)
            copies.append((step, row, at(0, particle, layer)))
    near = forward((0,), index, reached, tuple(copies), parts, *sizes, near, False, [mark])

    def tail(particle, layer):
        return particle * len(rest) + layer - 1

    x5, y5, mark = pack(
        "pack_fifth",
        [x4, y4],
        [
            [[(1, tail(particle, layer))] for particle in by_y for layer in rest],
            [[(0, tail(particle, layer))] for particle in by_x for layer in rest],
            [[(0, 0)]],
        ],
        [near],
    )
    x5, y5 = across(x5, 1), across(y5, 2)
    for bit in powers[1:]:
        inputs = [products_o, x3, y3] + arrived
        (sums,) = pack("pack_sums", inputs, [half_sums(bit, len(arrived))], [mark])
        arrived.append(across(sums, bit * COLUMNS))
    copies = []
    for particle in every:
        for layer in rest:
            copies.append((0, tail(particle, layer), at(1, particle, layer)))
            copies.append((1, tail(particle, layer), at(2, particle, layer)))
    near = forward((3,), index, [x4, y4], tuple(copies), parts, *sizes, near, False, [mark, sums])
    copies = []
    for number, group in ((0, by_y), (1, by_x)):
        for order, particle in enumerate(group):
            for layer in rest:
                copies.append((number, tail(order, layer), at(3, particle, layer)))
    near = forward((4,), index, [x5, y5], tuple(copies), parts, *sizes, near, True, [])
    halves = [(products_o, layers), (x3, layers), (y3, layers)] + [(value, 1) for value in arrived]
    return whole_total(side, incident, [near], halves), parts


def local(incident, tmat, blocks, block_rows, partners, live, owner_of):
    layers = lax.axis_size("owner") // COLUMNS
    my_owner = lax.axis_index("owner").astype(jnp.int32)[None]
    side = lax.axis_index("pair").astype(jnp.int32)[None]
    theirs = from_other(incident)
    index = slot_index(
        my_owner, side, partners, owner_of, block_rows, live, layers, incident.shape[0]
    )
    tmat_parts, incident = prepare(tmat, incident, index)
    (scattered,) = apply_tmat(True, False, side, incident, theirs, tmat_parts)
    parts = None
    for turn in range(ITERS):
        mine, parts = scatter_step(incident, scattered, blocks, parts, index, side, layers)
        theirs = from_other(mine)
        last = turn == ITERS - 1
        *exciting, scattered = apply_tmat(False, last, side, mine, theirs, tmat_parts)
    return (scattered, exciting[0])


def solution(mesh):
    in_specs = (
        P("owner", None, None, "pair"),
        P("owner", None, "pair", None),
        P("owner", None, None, "pair"),
        P("owner"),
        P(),
        P("owner"),
        P(),
    )
    out_specs = (P("owner", None, None, "pair"), P("owner", None, None, "pair"))
    return jax.shard_map(local, mesh=mesh, in_specs=in_specs, out_specs=out_specs, check_vma=False)
```

```python
import functools

import jax
import jax.numpy as jnp
from jax import lax
from jax.experimental import pallas as pl
from jax.experimental.pallas import tpu as pltpu
from jax.sharding import PartitionSpec as P

ITERS = 2
COLUMNS = 4
BUFFERS = 4
F32 = jnp.float32
BF16 = jnp.bfloat16
MIB = 1 << 20
STREAM_LIMIT = 48 * MIB
ALONE_LIMIT = 63 * MIB
GROUPS = 5
VMEM = pl.BlockSpec(memory_space=pltpu.VMEM)
SMEM = pl.BlockSpec(memory_space=pltpu.SMEM)
ANY = pl.BlockSpec(memory_space=pl.ANY)
HBM = pl.BlockSpec(memory_space=pltpu.MemorySpace.HBM)


def split_value(value):
    high = value.astype(BF16)
    low = (value - high.astype(F32)).astype(BF16)
    return high, low


def stacked_parts(real, imag):
    real_high, real_low = split_value(real)
    imag_high, imag_low = split_value(imag)
    with_real = jnp.concatenate((real_high, imag_high, real_low, imag_low), axis=0)
    with_imag = jnp.concatenate((-imag_high, real_high, -imag_low, real_low), axis=0)
    return with_real, with_imag


def dot_nt(left, right):
    return lax.dot_general(left, right, (((1,), (1,)), ((), ())), preferred_element_type=F32)


def dot_nn(left, right):
    return jnp.dot(left, right, preferred_element_type=F32)


def params(*byte_counts):
    return pltpu.CompilerParams(vmem_limit_bytes=sum(byte_counts) + 6 * MIB)


def size_of(*arrays):
    return sum(value.size * value.dtype.itemsize for value in arrays)


def place_of(column, particle, layer, particles, layers):
    return (column * particles + particle) * layers + layer


def index_kernel(
    layers, particles, owner_ref, side_ref, partners_ref, rows_of_ref, holders_ref, live_ref, *refs
):
    index_ref = refs[-1]
    slots = holders_ref.shape[0]
    stride, counts = GROUPS * slots, 3 * GROUPS * slots
    me = owner_ref[0]
    my_column, my_layer = lax.rem(me, COLUMNS), lax.div(me, COLUMNS)
    for group in range(GROUPS):
        index_ref[counts + group] = 0
    index_ref[counts + GROUPS] = side_ref[0]
    index_ref[counts + GROUPS + 1] = my_layer

    def step(slot, carry):
        row = rows_of_ref[partners_ref[me * slots + slot]]
        owner, particle = lax.div(row, particles), lax.rem(row, particles)
        column = lax.bitwise_xor(lax.rem(owner, COLUMNS), my_column)
        layer = lax.bitwise_xor(lax.div(owner, COLUMNS), my_layer)
        near = jnp.where(column == COLUMNS - 1, 2, 1)
        far = jnp.where(column == COLUMNS - 1, 4, 3)
        group = jnp.where(column == 0, 0, jnp.where(layer == 0, near, far))
        found = index_ref[counts + group]
        index_ref[counts + group] = found + 1
        position = group * slots + found
        index_ref[position] = slot
        index_ref[stride + position] = place_of(column, particle, layer, particles, layers)
        index_ref[2 * stride + position] = holders_ref[slot]
        return carry

    lax.fori_loop(0, live_ref[0], step, 0)


def slot_index(my_owner, side, partners, owner_of, block_rows, live, layers, particles):
    slots = block_rows.shape[0]
    return pl.pallas_call(
        functools.partial(index_kernel, layers, particles),
        out_shape=jax.ShapeDtypeStruct((3 * GROUPS * slots + GROUPS + 2,), jnp.int32),
        in_specs=[SMEM] * 6,
        out_specs=SMEM,
        compiler_params=pltpu.CompilerParams(vmem_limit_bytes=ALONE_LIMIT),
        name="slot_index",
    )(my_owner, side, partners, owner_of, block_rows, live)


def prepare_kernel(tmat_ref, incident_ref, after_ref, parts_ref, copy_ref, buf_ref, sems):
    particles, _, half, width = tmat_ref.shape

    def fetch(row):
        return pltpu.make_async_copy(tmat_ref.at[row], buf_ref.at[row], sems.at[row])

    for row in range(particles):
        fetch(row).start()
    own = pltpu.make_async_copy(incident_ref, copy_ref, sems.at[particles])
    own.start()
    for row in range(particles):
        fetch(row).wait()
        for part in range(2):
            high, low = split_value(buf_ref[row, part])
            parts_ref[row, :, part * width : (part + 1) * width] = high
            parts_ref[row, :, (2 + part) * width : (3 + part) * width] = low
    own.wait()


def prepare(tmat, incident, after):
    particles, _, half, width = tmat.shape
    return pl.pallas_call(
        prepare_kernel,
        out_shape=(
            jax.ShapeDtypeStruct((particles, half, 4 * width), BF16),
            jax.ShapeDtypeStruct(incident.shape, F32),
        ),
        in_specs=[HBM, HBM, ANY],
        out_specs=(VMEM, VMEM),
        scratch_shapes=[pltpu.VMEM(tmat.shape, F32), pltpu.SemaphoreType.DMA((particles + 1,))],
        compiler_params=params(2 * size_of(tmat), size_of(incident)),
        name="prepare",
    )(tmat, incident, after)


def tmat_kernel(halves, side_ref, mine_ref, theirs_ref, parts_ref, *refs):
    last = len(refs) == 4
    exciting_ref = refs[0] if last else None
    scattered_ref, full_ref = refs[1:3] if last else refs
    particles, _, directions, width = full_ref.shape
    half = width // 2
    start = pl.multiple_of(side_ref[0] * half, half)
    if halves:
        full_ref[:, :, :, pl.ds(start, half)] = mine_ref[...]
        full_ref[:, :, :, pl.ds(pl.multiple_of(half - start, half), half)] = theirs_ref[...]
    else:
        full_ref[...] = mine_ref[...] + theirs_ref[...]
    if last:
        window = full_ref.at[:, :, :, pl.ds(start, half)]
        leave = pltpu.make_async_copy(window, exciting_ref, refs[3])
        leave.start()
    for row in range(particles):
        with_real, with_imag = stacked_parts(full_ref[row, 0], full_ref[row, 1])
        right = jnp.concatenate((with_real, with_imag, with_real, with_imag), axis=1)
        total = dot_nt(parts_ref[row], right)
        out = (total[:, : 2 * directions] + total[:, 2 * directions :]).T
        scattered_ref[row, 0] = out[:directions]
        scattered_ref[row, 1] = out[directions:]
    if last:
        leave.wait()


def apply_tmat(halves, last, side, mine, theirs, parts):
    particles, _, directions, _ = mine.shape
    half = parts.shape[1]
    half_shape = jax.ShapeDtypeStruct((particles, 2, directions, half), F32)
    scratch = [pltpu.VMEM((particles, 2, directions, 2 * half), F32)]
    if last:
        scratch.append(pltpu.SemaphoreType.DMA)
    return pl.pallas_call(
        functools.partial(tmat_kernel, halves),
        out_shape=[half_shape] * (2 if last else 1),
        in_specs=[SMEM, VMEM, VMEM, VMEM],
        out_specs=[HBM, VMEM] if last else [VMEM],
        scratch_shapes=scratch,
        compiler_params=params(3 * size_of(mine, theirs), size_of(parts)),
        name="tmat_apply",
    )(side, mine, theirs, parts)


def row_from(row, my_layer):
    if isinstance(row, tuple):
        return lax.bitwise_xor(my_layer, row[0]) * row[2] + row[1]
    return row


def chosen_slots(index_ref, groups, slots):
    stride, counts = GROUPS * slots, 3 * GROUPS * slots
    starts, total = [], 0
    for group in groups:
        starts.append(total)
        total = total + index_ref[counts + group]

    def at_turn(turn):
        position = groups[0] * slots + turn
        for group, start in zip(groups[1:], starts[1:]):
            position = jnp.where(turn >= start, group * slots + turn - start, position)
        return [index_ref[number * stride + position] for number in range(3)]

    return total, at_turn


def backward_kernel(first, groups, base, index_ref, own_ref, other_ref, blocks_ref, *refs):
    if first:
        out_ref, parts_ref, left_ref, buf_ref, sems, made_ref, made_sems = refs[-7:]
    else:
        out_ref, left_ref, buf_ref, sems = refs
    directions, half = own_ref.shape[2], own_ref.shape[3]
    width = 2 * half
    slots = blocks_ref.shape[0]
    wanted, at_turn = chosen_slots(index_ref, groups, slots)
    own_side = index_ref[3 * GROUPS * slots + GROUPS]

    def fetch(turn, place):
        return pltpu.make_async_copy(
            blocks_ref.at[at_turn(turn)[0]], buf_ref.at[place], sems.at[place]
        )

    def keep(turn, place):
        return pltpu.make_async_copy(
            made_ref.at[place], parts_ref.at[at_turn(turn)[0]], made_sems.at[place]
        )

    for early in range(BUFFERS):

        @pl.when(early < wanted)
        def _():
            fetch(early, early).start()

    for field_ref, side in ((own_ref, own_side), (other_ref, 1 - own_side)):
        for row in range(other_ref.shape[0]):
            with_real, with_imag = stacked_parts(field_ref[row, 0], field_ref[row, 1])
            for part, value in enumerate((with_real, with_imag)):
                start = pl.multiple_of(part * width + side * half, half)
                left_ref[row, :, pl.ds(start, half)] = value
    out_ref[...] = jnp.zeros_like(out_ref)

    def body(turn, carry):
        here = lax.rem(turn, BUFFERS)
        fetch(turn, here).wait()
        _, place, holder = at_turn(turn)
        place = place - base
        if first:
            spot = lax.rem(turn, 2)

            @pl.when(turn >= 2)
            def _():
                keep(turn - 2, spot).wait()

            high, low = split_value(buf_ref[here].reshape(2 * width, half))
            made_ref[spot, 0] = high.reshape(2, width, half)
            made_ref[spot, 1] = low.reshape(2, width, half)
            keep(turn, spot).start()
        else:
            high = buf_ref[here, 0].reshape(2 * width, half)
            low = buf_ref[here, 1].reshape(2 * width, half)
        total = dot_nn(left_ref[holder], high)
        rest = dot_nn(left_ref[holder, : 2 * directions], low)
        out = total[: 2 * directions] + total[2 * directions :] + rest
        out_ref[place, 0] = out[:directions]
        out_ref[place, 1] = out[directions:]

        @pl.when(turn + BUFFERS < wanted)
        def _():
            fetch(turn + BUFFERS, here).start()

        return carry

    lax.fori_loop(0, wanted, body, 0)
    if first:

        @pl.when(wanted >= 2)
        def _():
            keep(wanted - 2, lax.rem(wanted, 2)).wait()

        @pl.when(wanted >= 1)
        def _():
            keep(wanted - 1, lax.rem(wanted - 1, 2)).wait()


def backward(first, groups, base, count, index, own_half, other_half, blocks, parts):
    particles, _, directions, half = other_half.shape
    width = 2 * half
    slots = blocks.shape[0]
    out_shape = [jax.ShapeDtypeStruct((count, 2, directions, half), F32)]
    out_specs = [VMEM]
    source = blocks if first else parts
    scratch = [
        pltpu.VMEM((particles, 4 * directions, 2 * width), BF16),
        pltpu.VMEM((BUFFERS,) + source.shape[1:], source.dtype),
        pltpu.SemaphoreType.DMA((BUFFERS,)),
    ]
    operands = [index, own_half, other_half, source]
    in_specs = [SMEM, VMEM, VMEM, HBM]
    aliases = {}
    if first:
        out_shape.append(jax.ShapeDtypeStruct((slots, 2, 2, width, half), BF16))
        out_specs.append(HBM)
        scratch.append(pltpu.VMEM((2, 2, 2, width, half), BF16))
        scratch.append(pltpu.SemaphoreType.DMA((2,)))
        if parts is not None:
            aliases = {len(operands): 1}
            operands.append(parts)
            in_specs.append(HBM)
    return pl.pallas_call(
        functools.partial(backward_kernel, first, groups, base),
        out_shape=out_shape,
        in_specs=in_specs,
        out_specs=out_specs,
        scratch_shapes=scratch,
        input_output_aliases=aliases,
        compiler_params=pltpu.CompilerParams(vmem_limit_bytes=STREAM_LIMIT),
        cost_estimate=pl.CostEstimate(
            flops=directions * width * half,
            bytes_accessed=size_of(own_half),
            transcendentals=0,
        ),
        name="backward_group" + str(groups[0]),
    )(*operands)


def forward_kernel(groups, copies, count, begun, last, index_ref, *refs):
    field_refs = refs[:count]
    parts_ref = refs[count]
    if last:
        out_ref, every_ref, buf_ref, sems, acc_ref = refs[-5:]
    else:
        acc_ref, every_ref, buf_ref, sems = refs[-4:]
    directions = every_ref.shape[2]
    wanted, at_turn = chosen_slots(index_ref, groups, parts_ref.shape[0])

    def fetch(turn, place):
        return pltpu.make_async_copy(
            parts_ref.at[at_turn(turn)[0]], buf_ref.at[place], sems.at[place]
        )

    for early in range(BUFFERS):

        @pl.when(early < wanted)
        def _():
            fetch(early, early).start()

    acc_ref[...] = refs[count + 1][...] if begun else jnp.zeros_like(acc_ref)
    my_layer = index_ref[3 * GROUPS * parts_ref.shape[0] + GROUPS + 1]
    for number, row, place in copies:
        every_ref[place] = field_refs[number][row_from(row, my_layer)]

    def body(turn, carry):
        here = lax.rem(turn, BUFFERS)
        _, place, holder = at_turn(turn)
        with_real, with_imag = stacked_parts(every_ref[place, 0], every_ref[place, 1])
        fetch(turn, here).wait()
        total = dot_nt(buf_ref[here, 0, 0], with_real) + dot_nt(buf_ref[here, 0, 1], with_imag)
        total += dot_nt(buf_ref[here, 1, 0], with_real) + dot_nt(buf_ref[here, 1, 1], with_imag)
        acc_ref[holder] += total

        @pl.when(turn + BUFFERS < wanted)
        def _():
            fetch(turn + BUFFERS, here).start()

        return carry

    lax.fori_loop(0, wanted, body, 0)
    for row in range(acc_ref.shape[0] if last else 0):
        total = acc_ref[row]
        out = (total[:, : 2 * directions] + total[:, 2 * directions :]).T
        out_ref[row, 0] = out[:directions]
        out_ref[row, 1] = out[directions:]


def forward(groups, index, fields, copies, parts, particles, total_rows, before, last, after):
    slots, _, _, width, half = parts.shape
    directions = fields[0].shape[2]
    acc = (particles, width, 4 * directions)
    given = [] if before is None else [before]
    scratch = [
        pltpu.VMEM((total_rows, 2, directions, half), F32),
        pltpu.VMEM((BUFFERS,) + parts.shape[1:], BF16),
        pltpu.SemaphoreType.DMA((BUFFERS,)),
    ]
    if last:
        scratch.append(pltpu.VMEM(acc, F32))
    out_shape = jax.ShapeDtypeStruct((particles, 2, directions, width) if last else acc, F32)
    return pl.pallas_call(
        functools.partial(forward_kernel, groups, copies, len(fields), bool(given), last),
        out_shape=out_shape,
        in_specs=[SMEM] + [VMEM] * len(fields) + [HBM] + [VMEM] * len(given) + [ANY] * len(after),
        out_specs=VMEM,
        scratch_shapes=scratch,
        compiler_params=pltpu.CompilerParams(vmem_limit_bytes=STREAM_LIMIT),
        cost_estimate=pl.CostEstimate(
            flops=directions * width * half,
            bytes_accessed=size_of(out_shape),
            transcendentals=0,
        ),
        name="forward_group" + str(groups[0]),
    )(index, *fields, parts, *given, *after)


def pack_kernel(plans, count, layer_ref, *refs):
    in_refs, out_refs = refs[:count], refs[-len(plans) :]
    my_layer = layer_ref[0]
    for out_ref, plan in zip(out_refs, plans):
        for row, terms in enumerate(plan):
            value = in_refs[terms[0][0]][row_from(terms[0][1], my_layer)]
            for number, source in terms[1:]:
                value = value + in_refs[number][row_from(source, my_layer)]
            out_ref[row] = value


def pack(name, inputs, plans, after=(), *, my_layer):
    shapes = [jax.ShapeDtypeStruct((len(plan),) + inputs[0].shape[1:], F32) for plan in plans]
    return pl.pallas_call(
        functools.partial(pack_kernel, plans, len(inputs)),
        out_shape=shapes,
        in_specs=[SMEM] + [VMEM] * len(inputs) + [ANY] * len(after),
        out_specs=[VMEM] * len(plans),
        compiler_params=params(size_of(*inputs), size_of(*shapes)),
        name=name,
    )(my_layer, *inputs, *after)


def total_kernel(counts, side_ref, incident_ref, *refs):
    nears, halves, out_ref = refs[: counts[0]], refs[counts[0] : -1], refs[-1]
    particles, half = incident_ref.shape[0], incident_ref.shape[3]
    start = pl.multiple_of(side_ref[0] * half, half)
    near = nears[0][...]
    for ref in nears[1:]:
        near = near + ref[...]
    out_ref[...] = near
    for particle in range(particles):
        value = incident_ref[particle]
        for ref, step in zip(halves, counts[1]):
            value = value + ref[particle * step]
        window = (particle, slice(None), slice(None), pl.ds(start, half))
        out_ref[window] = out_ref[window] + value


def whole_total(side, incident, nears, halves):
    arrays = [value for value, _ in halves]
    steps = tuple(step for _, step in halves)
    return pl.pallas_call(
        functools.partial(total_kernel, (len(nears), steps)),
        out_shape=jax.ShapeDtypeStruct(nears[0].shape, F32),
        in_specs=[SMEM] + [VMEM] * (1 + len(nears) + len(arrays)),
        out_specs=VMEM,
        compiler_params=params(size_of(*nears, nears[0], incident, *arrays)),
        name="total",
    )(side, incident, *nears, *arrays)


def from_other(value):
    return lax.ppermute(value, "pair", [(0, 1), (1, 0)])


def across(value, bit):
    count = lax.axis_size("owner")
    return lax.ppermute(value, "owner", [(source, source ^ bit) for source in range(count)])


def scatter_step(incident, scattered, blocks, parts, index, side, my_layer, layers):
    particles = incident.shape[0]
    every = range(particles)
    by_x = range((particles + 1) // 2)
    by_y = range((particles + 1) // 2, particles)
    rest = range(1, layers)
    powers = [1 << step for step in range(layers.bit_length() - 1)]
    at = functools.partial(place_of, particles=particles, layers=layers)
    total_rows = COLUMNS * particles * layers
    first_n, first_d = at(1, 0, 0), at(3, 0, 0)
    first = parts is None
    joined = functools.partial(pack, my_layer=my_layer)

    def row_of(particle, layer):
        return particle * layers + layer

    other = from_other(scattered)
    x1 = across(scattered, 1)
    y1 = across(scattered, 2)
    columns = [[column + COLUMNS * layer for layer in range(layers)] for column in range(COLUMNS)]
    reached = lax.all_gather(scattered, "owner", axis_index_groups=columns, axis=0, tiled=True)
    fetched = (scattered, other, blocks)
    products_d, *made = backward(
        first, (2, 4), first_d, total_rows - first_d, index, *fetched, parts
    )
    if first:
        parts = made[0]

    inputs = [products_d, x1, y1]
    x_plan = [[(0, row_of(particle, layer))] for particle in by_x for layer in range(layers)]
    y_plan = [[(0, row_of(particle, layer))] for particle in by_y for layer in range(layers)]
    x_head, y_head = len(x_plan), len(y_plan)
    x_plan += [[(2, particle)] for particle in by_y]
    y_plan += [[(1, particle)] for particle in by_x]
    x2, y2 = joined("pack_second", inputs, [x_plan, y_plan])
    x2, y2 = across(x2, 1), across(y2, 2)
    products_n, *made = backward(first, (1, 3), first_n, first_d - first_n, index, *fetched, parts)
    if first:
        parts = made[0]

    inputs = [products_n, x2, y2, scattered]
    x_plan, y_plan = [], []
    for particle in every:
        for layer in range(layers):
            x_terms = [(0, at(1, particle, layer) - first_n)]
            y_terms = [(0, at(2, particle, layer) - first_n)]
            if particle in by_x:
                y_terms.append((1, row_of(particle, layer)))
            else:
                x_terms.append((2, row_of(particle - len(by_x), layer)))
            x_plan.append(x_terms)
            y_plan.append(y_terms)
    x3, y3, copied = joined(
        "pack_third", inputs, [x_plan, y_plan, [[(3, particle)] for particle in every]]
    )
    x3, y3 = across(x3, 1), across(y3, 2)
    products_o, *made = backward(first, (0,), 0, first_n, index, copied, other, blocks, parts)
    if first:
        parts = made[0]
    copies = []
    for particle in every:
        copies.append((0, particle, at(1, particle, 0)))
        copies.append((1, particle, at(2, particle, 0)))
        if particle in by_x:
            copies.append((3, y_head + particle, at(3, particle, 0)))
        else:
            copies.append((2, x_head + particle - len(by_x), at(3, particle, 0)))
    sizes = (particles, total_rows)
    near = forward(
        (1, 2), index, [x1, y1, x2, y2], tuple(copies), parts, *sizes, None, False, [products_o]
    )

    def summed(layer, particle, arrived):
        terms = [(number, row_of(particle, layer)) for number in range(3)]
        for step in range(arrived):
            terms.append((3 + step, (layer >> (step + 1)) * particles + particle))
        return terms

    def half_sums(bit, arrived):
        chosen = range(bit, layers, 2 * bit)
        return [summed(layer, particle, arrived) for layer in chosen for particle in every]

    inputs = [products_o, x3, y3, reached]
    tails = [[(3, (layer, particle, particles))] for particle in every for layer in rest]
    x4, y4, sums, mark = joined(
        "pack_fourth",
        inputs,
        [tails, tails, half_sums(1, 0), [[(1, 0)]]],
        [near],
    )
    x4, y4 = across(x4, 1), across(y4, 2)
    arrived = [across(sums, COLUMNS)]
    copies = []
    for particle in every:
        for layer in rest:
            copies.append((0, (layer, particle, particles), at(0, particle, layer)))
    near = forward((0,), index, [reached], tuple(copies), parts, *sizes, near, False, [mark])

    def tail(particle, layer):
        return particle * len(rest) + layer - 1

    x5, y5, mark = joined(
        "pack_fifth",
        [x4, y4],
        [
            [[(1, tail(particle, layer))] for particle in by_y for layer in rest],
            [[(0, tail(particle, layer))] for particle in by_x for layer in rest],
            [[(0, 0)]],
        ],
        [near],
    )
    x5, y5 = across(x5, 1), across(y5, 2)
    for bit in powers[1:]:
        inputs = [products_o, x3, y3] + arrived
        (sums,) = joined("pack_sums", inputs, [half_sums(bit, len(arrived))], [mark])
        arrived.append(across(sums, bit * COLUMNS))
    copies = []
    for particle in every:
        for layer in rest:
            copies.append((0, tail(particle, layer), at(1, particle, layer)))
            copies.append((1, tail(particle, layer), at(2, particle, layer)))
    near = forward((3,), index, [x4, y4], tuple(copies), parts, *sizes, near, False, [mark, sums])
    copies = []
    for number, group in ((0, by_y), (1, by_x)):
        for order, particle in enumerate(group):
            for layer in rest:
                copies.append((number, tail(order, layer), at(3, particle, layer)))
    near = forward((4,), index, [x5, y5], tuple(copies), parts, *sizes, near, True, [])
    halves = [(products_o, layers), (x3, layers), (y3, layers)] + [(value, 1) for value in arrived]
    return whole_total(side, incident, [near], halves), parts


def local(incident, tmat, blocks, block_rows, partners, live, owner_of):
    layers = lax.axis_size("owner") // COLUMNS
    my_owner = lax.axis_index("owner").astype(jnp.int32)[None]
    side = lax.axis_index("pair").astype(jnp.int32)[None]
    my_layer = my_owner // COLUMNS
    theirs = from_other(incident)
    index = slot_index(
        my_owner, side, partners, owner_of, block_rows, live, layers, incident.shape[0]
    )
    tmat_parts, incident = prepare(tmat, incident, index)
    (scattered,) = apply_tmat(True, False, side, incident, theirs, tmat_parts)
    parts = None
    for turn in range(ITERS):
        mine, parts = scatter_step(incident, scattered, blocks, parts, index, side, my_layer, layers)
        theirs = from_other(mine)
        last = turn == ITERS - 1
        *exciting, scattered = apply_tmat(False, last, side, mine, theirs, tmat_parts)
    return (scattered, exciting[0])


def solution(mesh):
    in_specs = (
        P("owner", None, None, "pair"),
        P("owner", None, "pair", None),
        P("owner", None, None, "pair"),
        P("owner"),
        P(),
        P("owner"),
        P(),
    )
    out_specs = (P("owner", None, None, "pair"), P("owner", None, None, "pair"))
    return jax.shard_map(local, mesh=mesh, in_specs=in_specs, out_specs=out_specs, check_vma=False)
```

```python
import functools

import jax
import jax.numpy as jnp
from jax import lax
from jax.experimental import pallas as pl
from jax.experimental.pallas import tpu as pltpu
from jax.sharding import PartitionSpec as P

ITERS = 2
COLUMNS = 4
BUFFERS = 4
F32 = jnp.float32
BF16 = jnp.bfloat16
MIB = 1 << 20
STREAM_LIMIT = 48 * MIB
ALONE_LIMIT = 63 * MIB
GROUPS = 5
VMEM = pl.BlockSpec(memory_space=pltpu.VMEM)
SMEM = pl.BlockSpec(memory_space=pltpu.SMEM)
ANY = pl.BlockSpec(memory_space=pl.ANY)
HBM = pl.BlockSpec(memory_space=pltpu.MemorySpace.HBM)


def split_value(value):
    high = value.astype(BF16)
    low = (value - high.astype(F32)).astype(BF16)
    return high, low


def stacked_parts(real, imag):
    real_high, real_low = split_value(real)
    imag_high, imag_low = split_value(imag)
    with_real = jnp.concatenate((real_high, imag_high, real_low, imag_low), axis=0)
    with_imag = jnp.concatenate((-imag_high, real_high, -imag_low, real_low), axis=0)
    return with_real, with_imag


def dot_nt(left, right):
    return lax.dot_general(left, right, (((1,), (1,)), ((), ())), preferred_element_type=F32)


def dot_nn(left, right):
    return jnp.dot(left, right, preferred_element_type=F32)


def params(*byte_counts):
    return pltpu.CompilerParams(vmem_limit_bytes=sum(byte_counts) + 6 * MIB)


def size_of(*arrays):
    return sum(value.size * value.dtype.itemsize for value in arrays)


def place_of(column, particle, layer, particles, layers):
    return (column * particles + particle) * layers + layer


def index_kernel(
    layers, particles, owner_ref, side_ref, partners_ref, rows_of_ref, holders_ref, live_ref, *refs
):
    index_ref = refs[-1]
    slots = holders_ref.shape[0]
    stride, counts = GROUPS * slots, 3 * GROUPS * slots
    me = owner_ref[0]
    my_column, my_layer = lax.rem(me, COLUMNS), lax.div(me, COLUMNS)
    for group in range(GROUPS):
        index_ref[counts + group] = 0
    index_ref[counts + GROUPS] = side_ref[0]

    def step(slot, carry):
        row = rows_of_ref[partners_ref[me * slots + slot]]
        owner, particle = lax.div(row, particles), lax.rem(row, particles)
        column = lax.bitwise_xor(lax.rem(owner, COLUMNS), my_column)
        layer = lax.bitwise_xor(lax.div(owner, COLUMNS), my_layer)
        near = jnp.where(column == COLUMNS - 1, 2, 1)
        far = jnp.where(column == COLUMNS - 1, 4, 3)
        group = jnp.where(column == 0, 0, jnp.where(layer == 0, near, far))
        found = index_ref[counts + group]
        index_ref[counts + group] = found + 1
        position = group * slots + found
        index_ref[position] = slot
        index_ref[stride + position] = place_of(column, particle, layer, particles, layers)
        index_ref[2 * stride + position] = holders_ref[slot]
        return carry

    lax.fori_loop(0, live_ref[0], step, 0)


def slot_index(my_owner, side, partners, owner_of, block_rows, live, layers, particles):
    slots = block_rows.shape[0]
    return pl.pallas_call(
        functools.partial(index_kernel, layers, particles),
        out_shape=jax.ShapeDtypeStruct((3 * GROUPS * slots + GROUPS + 1,), jnp.int32),
        in_specs=[SMEM] * 6,
        out_specs=SMEM,
        compiler_params=pltpu.CompilerParams(vmem_limit_bytes=ALONE_LIMIT),
        name="slot_index",
    )(my_owner, side, partners, owner_of, block_rows, live)


def prepare_kernel(tmat_ref, incident_ref, after_ref, parts_ref, copy_ref, buf_ref, sems):
    particles, _, half, width = tmat_ref.shape

    def fetch(row):
        return pltpu.make_async_copy(tmat_ref.at[row], buf_ref.at[row], sems.at[row])

    for row in range(particles):
        fetch(row).start()
    own = pltpu.make_async_copy(incident_ref, copy_ref, sems.at[particles])
    own.start()
    for row in range(particles):
        fetch(row).wait()
        for part in range(2):
            high, low = split_value(buf_ref[row, part])
            parts_ref[row, :, part * width : (part + 1) * width] = high
            parts_ref[row, :, (2 + part) * width : (3 + part) * width] = low
    own.wait()


def prepare(tmat, incident, after):
    particles, _, half, width = tmat.shape
    return pl.pallas_call(
        prepare_kernel,
        out_shape=(
            jax.ShapeDtypeStruct((particles, half, 4 * width), BF16),
            jax.ShapeDtypeStruct(incident.shape, F32),
        ),
        in_specs=[HBM, HBM, ANY],
        out_specs=(VMEM, VMEM),
        scratch_shapes=[pltpu.VMEM(tmat.shape, F32), pltpu.SemaphoreType.DMA((particles + 1,))],
        compiler_params=params(2 * size_of(tmat), size_of(incident)),
        name="prepare",
    )(tmat, incident, after)


def tmat_kernel(halves, side_ref, mine_ref, theirs_ref, parts_ref, *refs):
    last = len(refs) == 4
    exciting_ref = refs[0] if last else None
    scattered_ref, full_ref = refs[1:3] if last else refs
    particles, _, directions, width = full_ref.shape
    half = width // 2
    start = pl.multiple_of(side_ref[0] * half, half)
    if halves:
        full_ref[:, :, :, pl.ds(start, half)] = mine_ref[...]
        full_ref[:, :, :, pl.ds(pl.multiple_of(half - start, half), half)] = theirs_ref[...]
    else:
        full_ref[...] = mine_ref[...] + theirs_ref[...]
    if last:
        window = full_ref.at[:, :, :, pl.ds(start, half)]
        leave = pltpu.make_async_copy(window, exciting_ref, refs[3])
        leave.start()
    for row in range(particles):
        with_real, with_imag = stacked_parts(full_ref[row, 0], full_ref[row, 1])
        right = jnp.concatenate((with_real, with_imag, with_real, with_imag), axis=1)
        total = dot_nt(parts_ref[row], right)
        out = (total[:, : 2 * directions] + total[:, 2 * directions :]).T
        scattered_ref[row, 0] = out[:directions]
        scattered_ref[row, 1] = out[directions:]
    if last:
        leave.wait()


def apply_tmat(halves, last, side, mine, theirs, parts):
    particles, _, directions, _ = mine.shape
    half = parts.shape[1]
    half_shape = jax.ShapeDtypeStruct((particles, 2, directions, half), F32)
    scratch = [pltpu.VMEM((particles, 2, directions, 2 * half), F32)]
    if last:
        scratch.append(pltpu.SemaphoreType.DMA)
    return pl.pallas_call(
        functools.partial(tmat_kernel, halves),
        out_shape=[half_shape] * (2 if last else 1),
        in_specs=[SMEM, VMEM, VMEM, VMEM],
        out_specs=[HBM, VMEM] if last else [VMEM],
        scratch_shapes=scratch,
        compiler_params=params(3 * size_of(mine, theirs), size_of(parts)),
        name="tmat_apply",
    )(side, mine, theirs, parts)


def chosen_slots(index_ref, groups, slots):
    stride, counts = GROUPS * slots, 3 * GROUPS * slots
    starts, total = [], 0
    for group in groups:
        starts.append(total)
        total = total + index_ref[counts + group]

    def at_turn(turn):
        position = groups[0] * slots + turn
        for group, start in zip(groups[1:], starts[1:]):
            position = jnp.where(turn >= start, group * slots + turn - start, position)
        return [index_ref[number * stride + position] for number in range(3)]

    return total, at_turn


def backward_kernel(first, groups, base, index_ref, own_ref, other_ref, blocks_ref, *refs):
    if first:
        out_ref, parts_ref, left_ref, buf_ref, sems, made_ref, made_sems = refs[-7:]
    else:
        out_ref, left_ref, buf_ref, sems = refs
    directions, half = own_ref.shape[2], own_ref.shape[3]
    width = 2 * half
    slots = blocks_ref.shape[0]
    wanted, at_turn = chosen_slots(index_ref, groups, slots)
    own_side = index_ref[3 * GROUPS * slots + GROUPS]

    def fetch(turn, place):
        return pltpu.make_async_copy(
            blocks_ref.at[at_turn(turn)[0]], buf_ref.at[place], sems.at[place]
        )

    def keep(turn, place):
        return pltpu.make_async_copy(
            made_ref.at[place], parts_ref.at[at_turn(turn)[0]], made_sems.at[place]
        )

    for early in range(BUFFERS):

        @pl.when(early < wanted)
        def _():
            fetch(early, early).start()

    for field_ref, side in ((own_ref, own_side), (other_ref, 1 - own_side)):
        for row in range(other_ref.shape[0]):
            with_real, with_imag = stacked_parts(field_ref[row, 0], field_ref[row, 1])
            for part, value in enumerate((with_real, with_imag)):
                start = pl.multiple_of(part * width + side * half, half)
                left_ref[row, :, pl.ds(start, half)] = value
    out_ref[...] = jnp.zeros_like(out_ref)

    def body(turn, carry):
        here = lax.rem(turn, BUFFERS)
        fetch(turn, here).wait()
        _, place, holder = at_turn(turn)
        place = place - base
        if first:
            spot = lax.rem(turn, 2)

            @pl.when(turn >= 2)
            def _():
                keep(turn - 2, spot).wait()

            high, low = split_value(buf_ref[here].reshape(2 * width, half))
            made_ref[spot, 0] = high.reshape(2, width, half)
            made_ref[spot, 1] = low.reshape(2, width, half)
            keep(turn, spot).start()
        else:
            high = buf_ref[here, 0].reshape(2 * width, half)
            low = buf_ref[here, 1].reshape(2 * width, half)
        total = dot_nn(left_ref[holder], high)
        rest = dot_nn(left_ref[holder, : 2 * directions], low)
        out = total[: 2 * directions] + total[2 * directions :] + rest
        out_ref[place, 0] = out[:directions]
        out_ref[place, 1] = out[directions:]

        @pl.when(turn + BUFFERS < wanted)
        def _():
            fetch(turn + BUFFERS, here).start()

        return carry

    lax.fori_loop(0, wanted, body, 0)
    if first:

        @pl.when(wanted >= 2)
        def _():
            keep(wanted - 2, lax.rem(wanted, 2)).wait()

        @pl.when(wanted >= 1)
        def _():
            keep(wanted - 1, lax.rem(wanted - 1, 2)).wait()


def backward(first, groups, base, count, index, own_half, other_half, blocks, parts):
    particles, _, directions, half = other_half.shape
    width = 2 * half
    slots = blocks.shape[0]
    out_shape = [jax.ShapeDtypeStruct((count, 2, directions, half), F32)]
    out_specs = [VMEM]
    source = blocks if first else parts
    scratch = [
        pltpu.VMEM((particles, 4 * directions, 2 * width), BF16),
        pltpu.VMEM((BUFFERS,) + source.shape[1:], source.dtype),
        pltpu.SemaphoreType.DMA((BUFFERS,)),
    ]
    operands = [index, own_half, other_half, source]
    in_specs = [SMEM, VMEM, VMEM, HBM]
    aliases = {}
    if first:
        out_shape.append(jax.ShapeDtypeStruct((slots, 2, 2, width, half), BF16))
        out_specs.append(HBM)
        scratch.append(pltpu.VMEM((2, 2, 2, width, half), BF16))
        scratch.append(pltpu.SemaphoreType.DMA((2,)))
        if parts is not None:
            aliases = {len(operands): 1}
            operands.append(parts)
            in_specs.append(HBM)
    return pl.pallas_call(
        functools.partial(backward_kernel, first, groups, base),
        out_shape=out_shape,
        in_specs=in_specs,
        out_specs=out_specs,
        scratch_shapes=scratch,
        input_output_aliases=aliases,
        compiler_params=pltpu.CompilerParams(vmem_limit_bytes=STREAM_LIMIT),
        cost_estimate=pl.CostEstimate(
            flops=directions * width * half,
            bytes_accessed=size_of(own_half),
            transcendentals=0,
        ),
        name="backward_group" + str(groups[0]),
    )(*operands)


def forward_kernel(groups, copies, count, begun, last, index_ref, *refs):
    field_refs = refs[:count]
    parts_ref = refs[count]
    if last:
        out_ref, every_ref, buf_ref, sems, acc_ref = refs[-5:]
    else:
        acc_ref, every_ref, buf_ref, sems = refs[-4:]
    directions = every_ref.shape[2]
    wanted, at_turn = chosen_slots(index_ref, groups, parts_ref.shape[0])

    def fetch(turn, place):
        return pltpu.make_async_copy(
            parts_ref.at[at_turn(turn)[0]], buf_ref.at[place], sems.at[place]
        )

    for early in range(BUFFERS):

        @pl.when(early < wanted)
        def _():
            fetch(early, early).start()

    acc_ref[...] = refs[count + 1][...] if begun else jnp.zeros_like(acc_ref)
    for number, row, place in copies:
        every_ref[place] = field_refs[number][row]

    def body(turn, carry):
        here = lax.rem(turn, BUFFERS)
        _, place, holder = at_turn(turn)
        with_real, with_imag = stacked_parts(every_ref[place, 0], every_ref[place, 1])
        fetch(turn, here).wait()
        total = dot_nt(buf_ref[here, 0, 0], with_real) + dot_nt(buf_ref[here, 0, 1], with_imag)
        total += dot_nt(buf_ref[here, 1, 0], with_real) + dot_nt(buf_ref[here, 1, 1], with_imag)
        acc_ref[holder] += total

        @pl.when(turn + BUFFERS < wanted)
        def _():
            fetch(turn + BUFFERS, here).start()

        return carry

    lax.fori_loop(0, wanted, body, 0)
    for row in range(acc_ref.shape[0] if last else 0):
        total = acc_ref[row]
        out = (total[:, : 2 * directions] + total[:, 2 * directions :]).T
        out_ref[row, 0] = out[:directions]
        out_ref[row, 1] = out[directions:]


def forward(groups, index, fields, copies, parts, particles, total_rows, before, last, after):
    slots, _, _, width, half = parts.shape
    directions = fields[0].shape[2]
    acc = (particles, width, 4 * directions)
    given = [] if before is None else [before]
    scratch = [
        pltpu.VMEM((total_rows, 2, directions, half), F32),
        pltpu.VMEM((BUFFERS,) + parts.shape[1:], BF16),
        pltpu.SemaphoreType.DMA((BUFFERS,)),
    ]
    if last:
        scratch.append(pltpu.VMEM(acc, F32))
    out_shape = jax.ShapeDtypeStruct((particles, 2, directions, width) if last else acc, F32)
    return pl.pallas_call(
        functools.partial(forward_kernel, groups, copies, len(fields), bool(given), last),
        out_shape=out_shape,
        in_specs=[SMEM] + [VMEM] * len(fields) + [HBM] + [VMEM] * len(given) + [ANY] * len(after),
        out_specs=VMEM,
        scratch_shapes=scratch,
        compiler_params=pltpu.CompilerParams(vmem_limit_bytes=STREAM_LIMIT),
        cost_estimate=pl.CostEstimate(
            flops=directions * width * half,
            bytes_accessed=size_of(out_shape),
            transcendentals=0,
        ),
        name="forward_group" + str(groups[0]),
    )(index, *fields, parts, *given, *after)


def pack_kernel(plans, count, *refs):
    in_refs, out_refs = refs[:count], refs[-len(plans) :]
    for out_ref, plan in zip(out_refs, plans):
        for row, terms in enumerate(plan):
            value = in_refs[terms[0][0]][terms[0][1]]
            for number, source in terms[1:]:
                value = value + in_refs[number][source]
            out_ref[row] = value


def pack(name, inputs, plans, after=()):
    shapes = [jax.ShapeDtypeStruct((len(plan),) + inputs[0].shape[1:], F32) for plan in plans]
    return pl.pallas_call(
        functools.partial(pack_kernel, plans, len(inputs)),
        out_shape=shapes,
        in_specs=[VMEM] * len(inputs) + [ANY] * len(after),
        out_specs=[VMEM] * len(plans),
        compiler_params=params(size_of(*inputs), size_of(*shapes)),
        name=name,
    )(*inputs, *after)


def total_kernel(counts, side_ref, incident_ref, *refs):
    nears, halves, out_ref = refs[: counts[0]], refs[counts[0] : -1], refs[-1]
    particles, half = incident_ref.shape[0], incident_ref.shape[3]
    start = pl.multiple_of(side_ref[0] * half, half)
    near = nears[0][...]
    for ref in nears[1:]:
        near = near + ref[...]
    out_ref[...] = near
    for particle in range(particles):
        value = incident_ref[particle]
        for ref, step in zip(halves, counts[1]):
            value = value + ref[particle * step]
        window = (particle, slice(None), slice(None), pl.ds(start, half))
        out_ref[window] = out_ref[window] + value


def whole_total(side, incident, nears, halves):
    arrays = [value for value, _ in halves]
    steps = tuple(step for _, step in halves)
    return pl.pallas_call(
        functools.partial(total_kernel, (len(nears), steps)),
        out_shape=jax.ShapeDtypeStruct(nears[0].shape, F32),
        in_specs=[SMEM] + [VMEM] * (1 + len(nears) + len(arrays)),
        out_specs=VMEM,
        compiler_params=params(size_of(*nears, nears[0], incident, *arrays)),
        name="total",
    )(side, incident, *nears, *arrays)


def from_other(value):
    return lax.ppermute(value, "pair", [(0, 1), (1, 0)])


def across(value, bit):
    count = lax.axis_size("owner")
    return lax.ppermute(value, "owner", [(source, source ^ bit) for source in range(count)])


def scatter_step(incident, scattered, blocks, parts, index, side, layers):
    particles = incident.shape[0]
    every = range(particles)
    by_x = range((particles + 1) // 2)
    by_y = range((particles + 1) // 2, particles)
    rest = range(1, layers)
    powers = [1 << step for step in range(layers.bit_length() - 1)]
    at = functools.partial(place_of, particles=particles, layers=layers)
    total_rows = COLUMNS * particles * layers
    first_n, first_d = at(1, 0, 0), at(3, 0, 0)
    first = parts is None

    def row_of(particle, layer):
        return particle * layers + layer

    other = from_other(scattered)
    x1 = across(scattered, 1)
    y1 = across(scattered, 2)
    reached = [across(scattered, COLUMNS)]
    where = {1: (0, 0), 2: (1, 0), 3: (2, 0)}
    fetched = (scattered, other, blocks)
    products_d, *made = backward(
        first, (2, 4), first_d, total_rows - first_d, index, *fetched, parts
    )
    if first:
        parts = made[0]

    inputs = [products_d, x1, y1, scattered]
    x_plan = [[(0, row_of(particle, layer))] for particle in by_x for layer in range(layers)]
    y_plan = [[(0, row_of(particle, layer))] for particle in by_y for layer in range(layers)]
    x_head, y_head = len(x_plan), len(y_plan)
    x_plan += [[(2, particle)] for particle in by_y]
    y_plan += [[(1, particle)] for particle in by_x]
    x2, y2, copied = pack(
        "pack_second",
        inputs,
        [x_plan, y_plan, [[(3, particle)] for particle in every]],
        reached,
    )
    x2, y2 = across(x2, 1), across(y2, 2)
    reached.append(across(copied, 2 * COLUMNS))
    products_n, *made = backward(first, (1, 3), first_n, first_d - first_n, index, *fetched, parts)
    if first:
        parts = made[0]

    def z_row(particle, layer):
        number, start = where[layer]
        return number, start + particle

    inputs = [products_n, x2, y2, scattered, reached[0]]
    x_plan, y_plan = [], []
    for particle in every:
        for layer in range(layers):
            x_terms = [(0, at(1, particle, layer) - first_n)]
            y_terms = [(0, at(2, particle, layer) - first_n)]
            if particle in by_x:
                y_terms.append((1, row_of(particle, layer)))
            else:
                x_terms.append((2, row_of(particle - len(by_x), layer)))
            x_plan.append(x_terms)
            y_plan.append(y_terms)
    z_plans = [[[(number, particle)] for particle in every] for number in (3, 4)]
    x3, y3, copied, known = pack("pack_third", inputs, [x_plan, y_plan] + z_plans, reached[1:])
    x3, y3 = across(x3, 1), across(y3, 2)
    reached.append(across(known, 2 * COLUMNS))
    for bit in powers[2:]:
        plan = [[(0, particle)] for particle in every]
        for layer in range(1, bit):
            plan += [[(1 + where[layer][0], where[layer][1] + particle)] for particle in every]
        (known,) = pack("pack_layers", [scattered] + reached, [plan])
        for layer in range(bit):
            where[bit + layer] = (len(reached), layer * particles)
        reached.append(across(known, bit * COLUMNS))
    products_o, *made = backward(first, (0,), 0, first_n, index, copied, other, blocks, parts)
    if first:
        parts = made[0]
    copies = []
    for particle in every:
        copies.append((0, particle, at(1, particle, 0)))
        copies.append((1, particle, at(2, particle, 0)))
        if particle in by_x:
            copies.append((3, y_head + particle, at(3, particle, 0)))
        else:
            copies.append((2, x_head + particle - len(by_x), at(3, particle, 0)))
    sizes = (particles, total_rows)
    near = forward(
        (1, 2), index, [x1, y1, x2, y2], tuple(copies), parts, *sizes, None, False, [products_o]
    )

    def summed(layer, particle, arrived):
        terms = [(number, row_of(particle, layer)) for number in range(3)]
        return terms + [(3 + step, layer * particles + particle) for step in range(arrived)]

    def half_sums(bit, arrived):
        return [
            summed(layer, particle, arrived) for layer in range(bit, 2 * bit) for particle in every
        ]

    inputs = [products_o, x3, y3] + reached
    tails = []
    for particle in every:
        for layer in rest:
            step, row = z_row(particle, layer)
            tails.append([(3 + step, row)])
    x4, y4, sums, mark = pack(
        "pack_fourth",
        inputs,
        [tails, tails, half_sums(powers[-1], 0), [[(1, 0)]]],
        [near],
    )
    x4, y4 = across(x4, 1), across(y4, 2)
    arrived = [across(sums, powers[-1] * COLUMNS)]
    copies = []
    for particle in every:
        for layer in rest:
            step, row = z_row(particle, layer)
            copies.append((step, row, at(0, particle, layer)))
    near = forward((0,), index, reached, tuple(copies), parts, *sizes, near, False, [mark])

    def tail(particle, layer):
        return particle * len(rest) + layer - 1

    x5, y5, mark = pack(
        "pack_fifth",
        [x4, y4],
        [
            [[(1, tail(particle, layer))] for particle in by_y for layer in rest],
            [[(0, tail(particle, layer))] for particle in by_x for layer in rest],
            [[(0, 0)]],
        ],
        [near],
    )
    x5, y5 = across(x5, 1), across(y5, 2)
    copies = []
    for particle in every:
        for layer in rest:
            copies.append((0, tail(particle, layer), at(1, particle, layer)))
            copies.append((1, tail(particle, layer), at(2, particle, layer)))
    near = forward((3,), index, [x4, y4], tuple(copies), parts, *sizes, near, False, [mark])
    for bit in powers[-2::-1]:
        inputs = [products_o, x3, y3] + arrived
        (sums,) = pack("pack_sums", inputs, [half_sums(bit, len(arrived))], [near])
        arrived.append(across(sums, bit * COLUMNS))
    copies = []
    for number, group in ((0, by_y), (1, by_x)):
        for order, particle in enumerate(group):
            for layer in rest:
                copies.append((number, tail(order, layer), at(3, particle, layer)))
    near = forward((4,), index, [x5, y5], tuple(copies), parts, *sizes, near, True, [sums])
    halves = [(products_o, layers), (x3, layers), (y3, layers)] + [(value, 1) for value in arrived]
    return whole_total(side, incident, [near], halves), parts


def local(incident, tmat, blocks, block_rows, partners, live, owner_of):
    layers = lax.axis_size("owner") // COLUMNS
    my_owner = lax.axis_index("owner").astype(jnp.int32)[None]
    side = lax.axis_index("pair").astype(jnp.int32)[None]
    theirs = from_other(incident)
    index = slot_index(
        my_owner, side, partners, owner_of, block_rows, live, layers, incident.shape[0]
    )
    tmat_parts, incident = prepare(tmat, incident, index)
    (scattered,) = apply_tmat(True, False, side, incident, theirs, tmat_parts)
    parts = None
    for turn in range(ITERS):
        mine, parts = scatter_step(incident, scattered, blocks, parts, index, side, layers)
        theirs = from_other(mine)
        last = turn == ITERS - 1
        *exciting, scattered = apply_tmat(False, last, side, mine, theirs, tmat_parts)
    return (scattered, exciting[0])


def solution(mesh):
    in_specs = (
        P("owner", None, None, "pair"),
        P("owner", None, "pair", None),
        P("owner", None, None, "pair"),
        P("owner"),
        P(),
        P("owner"),
        P(),
    )
    out_specs = (P("owner", None, None, "pair"), P("owner", None, None, "pair"))
    return jax.shard_map(local, mesh=mesh, in_specs=in_specs, out_specs=out_specs, check_vma=False)
```
